512 devices in a mesh: ctx: 64 (over y, z_hi, x, core), tp: 8 (over z_lo).
Axes of the slice: x: 4, y: 4, z: 16 (z_hi: 2, z_lo: 8; z = z_hi * 8 + z_lo), core: 2. Of those that a mesh axis runs over, the one named last changes fastest.
Arguments:
- features: bfloat16 [3, 8192, 4096], P(None, 'ctx', 'tp'), may hold values from -60 to 60
- short_taps: float32 [3, 7, 4096], P(None, None, 'tp'), may hold values from -2.5 to 2.5
- long_filter: bfloat16 [8192, 4096], P('ctx', 'tp'), may hold values from -0.8 to 0.8
- gain: float32 [4096], P('tp'), may hold values from 0.5 to 1.5
- out_grad: bfloat16 [8192, 4096], P('ctx', 'tp'), may hold values from -6 to 6
Outputs:
- normed: bfloat16 [8192, 4096], P('ctx', 'tp')
- feature_grad: bfloat16 [3, 8192, 4096], P(None, 'ctx', 'tp')
- filter_grad: bfloat16 [8192, 4096], P('ctx', 'tp')
- taps_grad: float32 [3, 7, 4096], P(None, None, 'tp')
- gain_grad: float32 [4096], P('tp')
The draws below stay inside these ranges and needn't reach their ends.
All inputs are finite; a program needn't handle non-finite values.
Results may differ from the reference program's by a relative error of at most 0.0076.
Values may be sent and summed in bfloat16 or wider, within the bound.
A program may use at most 64 MiB of HBM per device.

```python
import math
import jax
import jax.numpy as jnp
from jax import lax

CH = 4096
TAPS = 7
SEQUENCE_LENGTH = 8192


def draw_features(key, part):
    key = jax.random.fold_in(key, 11)
    key_base, key_chan, key_rows = jax.random.split(key, 3)
    chan_ramp = 10.0 ** (jnp.arange(CH, dtype=jnp.float32) / CH - 0.5)
    rough = jax.random.uniform(key_chan, (3, 1, CH), jnp.float32, 0.7, 1.4)
    noise_base = jnp.clip(jax.random.normal(key_base, (3, SEQUENCE_LENGTH, CH), jnp.float32), -4.0, 4.0)
    spread = 0.5
    row_scale = 10.0 ** jax.random.uniform(key_rows, (3, SEQUENCE_LENGTH, 1), jnp.float32, -spread, spread)
    ones_row = jnp.ones((CH,), jnp.float32)
    stream_lift = jnp.stack([ones_row, ones_row, chan_ramp])[:, None, :]
    return (noise_base * rough * row_scale * stream_lift).astype(jnp.bfloat16)


def draw_long_filter(key, part):
    key = jax.random.fold_in(key, 23)
    flip_key, gradual_key, quick_key, jagged_key, spike_key = jax.random.split(key, 5)
    long_share = 0.5
    rough = jnp.clip(jax.random.normal(jagged_key, (SEQUENCE_LENGTH, CH), jnp.float32), -3.0, 3.0)
    keeps_long = jax.random.uniform(flip_key, (CH,), jnp.float32) < long_share
    slow_rate = jnp.exp(jax.random.uniform(gradual_key, (CH,), jnp.float32, math.log(0.5 / SEQUENCE_LENGTH), math.log(2.0 / SEQUENCE_LENGTH)))
    fast_rate = jnp.exp(jax.random.uniform(quick_key, (CH,), jnp.float32, math.log(1.0 / 50.0), math.log(1.0 / 30.0)))
    damping_speed = jnp.where(keeps_long, slow_rate, fast_rate)
    place_indices = jnp.arange(SEQUENCE_LENGTH, dtype=jnp.float32)[:, None]
    spike_location = jax.random.randint(spike_key, (4,), 0, SEQUENCE_LENGTH)
    spike_falloff = jnp.prod(jnp.where(jnp.arange(SEQUENCE_LENGTH, dtype=jnp.int32)[:, None] >= spike_location[None, :], 0.6, 1.0), axis=1)
    amplitude_shape = jnp.sqrt(2.0 * damping_speed)[None, :] * jnp.exp(-damping_speed[None, :] * place_indices) * spike_falloff[:, None]
    return (rough * amplitude_shape).astype(jnp.bfloat16)


def block_scale(own_key, dims, pieces, least, largest):
    loudness = 1.0
    for position, parts in pieces:
        draws = jax.random.uniform(jax.random.fold_in(jax.random.fold_in(own_key, 6), position), (parts,), jnp.float32, least / len(pieces), largest / len(pieces))
        loudness = loudness * jnp.repeat(jnp.exp(draws), dims[position] // parts).reshape((-1,) + (1,) * (len(dims) - 1 - position))
    return loudness


def bell_draw(key, shape, scale, most, pieces=(), kind=jnp.bfloat16):
    drawn = scale * jax.random.normal(key, shape, jnp.float32)
    if pieces:
        drawn = drawn * block_scale(key, shape, pieces, -0.22, 0.18)
    return jnp.clip(drawn, -most, most).astype(kind)


def setup_inputs(seed: int = 0) -> dict:
    keys = jax.random.split(jax.random.key(seed), 6)
    return {
        "features": draw_features(jax.random.fold_in(keys[5], 71), 0),
        "short_taps": bell_draw(keys[1], (3, TAPS, CH), 0.5, 2.5, ((2, 8),), jnp.float32),
        "long_filter": draw_long_filter(jax.random.fold_in(keys[5], 71), 0),
        "gain": jnp.clip(1.0 + 0.1 * jax.random.normal(keys[3], (CH,), jnp.float32), 0.5, 1.5),
        "out_grad": bell_draw(keys[4], (SEQUENCE_LENGTH, CH), 1.0, 6.0, ((0, 64), (1, 8))),
    }


def channel_blocks(kernel_fn, left, right):
    block = math.gcd(CH, 256)
    count = CH // block

    def split_up(array):
        return array.reshape(SEQUENCE_LENGTH, count, block).transpose(1, 0, 2)
    result = lax.map(lambda pair: kernel_fn(pair[0], pair[1]), (split_up(left), split_up(right)))
    return result.transpose(1, 0, 2).reshape(SEQUENCE_LENGTH, CH)

def causal_product(signal, kernel):
    size = 2 * SEQUENCE_LENGTH
    spectrum = jnp.fft.rfft(signal, n=size, axis=0) * jnp.fft.rfft(kernel, n=size, axis=0)
    return jnp.fft.irfft(spectrum, n=size, axis=0)[:SEQUENCE_LENGTH]

def lagged_product(signal, kernel):
    size = 2 * SEQUENCE_LENGTH
    spectrum = jnp.fft.rfft(signal, n=size, axis=0) * jnp.conj(jnp.fft.rfft(kernel, n=size, axis=0))
    return jnp.fft.irfft(spectrum, n=size, axis=0)[:SEQUENCE_LENGTH]

def reference(features, short_taps, long_filter, gain, out_grad):
    rim_rows = TAPS - 1
    feats = features.astype(jnp.float32)
    padded = jnp.pad(feats, ((0, 0), (rim_rows, 0), (0, 0)))
    running = jnp.zeros_like(feats)
    for lag_id in range(TAPS):
        running = running + short_taps[:, lag_id, None, :] * padded[:, rim_rows - lag_id:rim_rows - lag_id + SEQUENCE_LENGTH, :]
    shorted = running.astype(jnp.bfloat16)
    q_short = shorted[0].astype(jnp.float32)
    k_short = shorted[1].astype(jnp.float32)
    v_short = shorted[2].astype(jnp.float32)
    product = (k_short * v_short).astype(jnp.bfloat16)
    filt = long_filter.astype(jnp.float32)
    convolved = channel_blocks(causal_product, product.astype(jnp.float32), filt).astype(jnp.bfloat16)
    conv_full = convolved.astype(jnp.float32)
    gated = q_short * conv_full
    scale = lax.rsqrt(lax.optimization_barrier(jnp.mean(gated * gated, axis=1)) + 1e-06)
    normed = (gated * scale[:, None] * gain[None, :]).astype(jnp.bfloat16)
    upstream = out_grad.astype(jnp.float32)
    weighted = gain[None, :] * upstream
    tilt = lax.optimization_barrier(jnp.sum(weighted * gated, axis=1))
    grad_gated = scale[:, None] * weighted - gated * (scale ** 3 * tilt / CH)[:, None]
    gain_grad = lax.optimization_barrier(jnp.sum(upstream * gated * scale[:, None], axis=0))
    grad_conv = (grad_gated * q_short).astype(jnp.bfloat16)
    grad_conv_full = grad_conv.astype(jnp.float32)
    grad_product = channel_blocks(lagged_product, grad_conv_full, filt).astype(jnp.bfloat16)
    filter_grad = channel_blocks(lagged_product, grad_conv_full, product.astype(jnp.float32)).astype(jnp.bfloat16)
    grad_prod_full = grad_product.astype(jnp.float32)
    grad_short = jnp.stack([grad_gated * conv_full, grad_prod_full * v_short, grad_prod_full * k_short]).astype(jnp.bfloat16)
    grad_short_full = grad_short.astype(jnp.float32)
    tail = jnp.pad(grad_short_full, ((0, 0), (0, rim_rows), (0, 0)))
    collected = jnp.zeros_like(feats)
    for lag_id in range(TAPS):
        collected = collected + short_taps[:, lag_id, None, :] * tail[:, lag_id:lag_id + SEQUENCE_LENGTH, :]
    feature_grad = collected.astype(jnp.bfloat16)
    taps_grad = jnp.stack([lax.optimization_barrier(jnp.sum(grad_short_full * padded[:, rim_rows - lag_id:rim_rows - lag_id + SEQUENCE_LENGTH, :], axis=1)) for lag_id in range(TAPS)], axis=1)
    return (normed, feature_grad, filter_grad, taps_grad, gain_grad)
```

```python
import functools

import jax
import jax.numpy as jnp
from jax import lax
from jax.experimental import pallas as pl
from jax.experimental.pallas import tpu as pltpu
from jax.sharding import PartitionSpec as P

F32 = jnp.float32
BF16 = jnp.bfloat16
MESH = pl.DeviceIdType.MESH
norm_eps = 1e-06

TAPS = 7
LANES = 128
GROUP = 8
VMEM = pl.BlockSpec(memory_space=pltpu.VMEM)
ANYWHERE = pl.BlockSpec(memory_space=pl.ANY)


def passed_along(block, axis, distance):
    devices = range(lax.axis_size(axis))
    route = [(i - distance, i) for i in devices if i - distance in devices]
    return lax.ppermute(block, axis, route)


def lane_chunks(width):
    return [slice(start, start + LANES) for start in range(0, width, LANES)]


def each_partner(me, visit):
    row, half, col = me // 16, (me // 8) % 2, me % 8

    def crossing(step, carry):
        partner = ((row + step // 8) % 4) * 16 + (1 - half) * 8 + (col + step % 8) % 8
        visit(partner)
        return carry

    def within(step, carry):
        partner = ((row + step // 8) % 4) * 16 + half * 8 + (col + step % 8) % 8
        visit(partner)
        return carry

    lax.fori_loop(0, 32, crossing, 0)
    lax.fori_loop(1, 32, within, 0)


def greet_all(me):
    barrier = pltpu.get_barrier_semaphore()

    def greet(partner):
        pl.semaphore_signal(barrier, inc=1, device_id={"ctx": partner}, device_id_type=MESH)

    each_partner(me, greet)
    pl.semaphore_wait(barrier, 63)


def start_exchange(me, sources, targets, send_sem, recv_sem, backward=False):
    for source, target, sent, came in zip(sources, targets, send_sem, recv_sem):

        def visit(partner, source=source, target=target, sent=sent, came=came):
            pick = 63 - partner if backward else partner
            pltpu.make_async_remote_copy(
                src_ref=source.at[pick],
                dst_ref=target.at[me],
                send_sem=sent,
                recv_sem=came,
                device_id={"ctx": partner},
                device_id_type=MESH,
            ).start()

        each_partner(me, visit)


def await_bytes(ref, sem):
    pltpu.make_async_copy(ref.at[pl.ds(0, 63)], ref.at[pl.ds(0, 63)], sem).wait()


def exchange_kernel(count, backward, *refs):
    sources, targets = refs[:count], refs[count : 2 * count]
    send_sem, recv_sem, local_sem = refs[2 * count :]
    me = lax.axis_index("ctx")
    greet_all(me)
    start_exchange(
        me,
        sources,
        targets,
        [send_sem.at[i] for i in range(count)],
        [recv_sem.at[i] for i in range(count)],
        backward,
    )
    mine = 63 - me if backward else me
    local = [
        pltpu.make_async_copy(s.at[mine], t.at[me], local_sem.at[i])
        for i, (s, t) in enumerate(zip(sources, targets))
    ]
    for copy in local:
        copy.start()
    for copy in local:
        copy.wait()
    for i in range(count):
        await_bytes(sources[i], send_sem.at[i])
        await_bytes(targets[i], recv_sem.at[i])


def exchange(arrays, collective_id, backward=False):
    count = len(arrays)
    return pl.pallas_call(
        functools.partial(exchange_kernel, count, backward),
        out_shape=[jax.ShapeDtypeStruct(a.shape, a.dtype) for a in arrays],
        in_specs=[ANYWHERE] * count,
        out_specs=[ANYWHERE] * count,
        scratch_shapes=[pltpu.SemaphoreType.DMA((count,))] * 3,
        compiler_params=pltpu.CompilerParams(collective_id=collective_id, has_side_effects=True),
    )(*arrays)


def row_sums_kernel(mine_ref, all_ref, send_sem, recv_sem, local_sem):
    me = lax.axis_index("tp")
    barrier = pltpu.get_barrier_semaphore()
    for step in range(1, 8):
        partner = (me + step) % 8
        pl.semaphore_signal(barrier, inc=1, device_id={"tp": partner}, device_id_type=MESH)
    pl.semaphore_wait(barrier, 7)
    for step in range(1, 8):
        partner = (me + step) % 8
        pltpu.make_async_remote_copy(
            src_ref=mine_ref,
            dst_ref=all_ref.at[me],
            send_sem=send_sem,
            recv_sem=recv_sem,
            device_id={"tp": partner},
            device_id_type=MESH,
        ).start()
    own = pltpu.make_async_copy(mine_ref, all_ref.at[me], local_sem)
    own.start()
    own.wait()
    seven = all_ref.at[pl.ds(0, 7)]
    pltpu.make_async_copy(seven, seven, send_sem).wait()
    pltpu.make_async_copy(seven, seven, recv_sem).wait()


def row_sums(mine, collective_id):
    return pl.pallas_call(
        row_sums_kernel,
        out_shape=jax.ShapeDtypeStruct((8,) + mine.shape, F32),
        in_specs=[VMEM],
        out_specs=VMEM,
        scratch_shapes=[pltpu.SemaphoreType.DMA] * 3,
        compiler_params=pltpu.CompilerParams(collective_id=collective_id, has_side_effects=True),
    )(mine)


def ctx_sum_kernel(mine_ref, total_ref, slots, piece, sems):
    me = lax.axis_index("ctx")
    greet_all(me)
    start_exchange(me, [mine_ref], [slots], [sems.at[0]], [sems.at[1]])
    own = pltpu.make_async_copy(mine_ref.at[me], slots.at[me], sems.at[4])
    own.start()
    own.wait()
    await_bytes(mine_ref, sems.at[0])
    await_bytes(slots, sems.at[1])
    piece[...] = jnp.sum(slots[...], axis=0)

    def visit(partner):
        pltpu.make_async_remote_copy(
            src_ref=piece,
            dst_ref=total_ref.at[me],
            send_sem=sems.at[2],
            recv_sem=sems.at[3],
            device_id={"ctx": partner},
            device_id_type=MESH,
        ).start()

    each_partner(me, visit)
    own = pltpu.make_async_copy(piece, total_ref.at[me], sems.at[4])
    own.start()
    own.wait()
    await_bytes(total_ref, sems.at[2])
    await_bytes(total_ref, sems.at[3])


def ctx_sum(mine, collective_id):
    return pl.pallas_call(
        ctx_sum_kernel,
        out_shape=jax.ShapeDtypeStruct(mine.shape, F32),
        in_specs=[VMEM],
        out_specs=VMEM,
        scratch_shapes=[
            pltpu.VMEM(mine.shape, F32),
            pltpu.VMEM(mine.shape[1:], F32),
            pltpu.SemaphoreType.DMA((5,)),
        ],
        compiler_params=pltpu.CompilerParams(collective_id=collective_id, has_side_effects=True),
    )(mine)


def toeplitz_rows(current, other, first, backward):
    rows = lax.broadcasted_iota(jnp.int32, (16, LANES), 0) + first
    lanes = lax.broadcasted_iota(jnp.int32, (16, LANES), 1)
    current = jnp.broadcast_to(current, (16, LANES))
    other = jnp.broadcast_to(other, (16, LANES))
    if backward:
        mixed = jnp.where(lanes >= LANES - 1 - rows, current, other)
        return pltpu.roll(mixed, first + 1, 1, stride=1, stride_axis=0)
    mixed = jnp.where(lanes < LANES - rows, current, other)
    return pltpu.roll(mixed, first, 1, stride=1, stride_axis=0)


def long_kernel(backward, count, window_ref, *refs):
    inputs, outputs = refs[:count], refs[count : 2 * count]
    windows = refs[2 * count]
    padded, flat = refs[2 * count + 1 : 3 * count + 1], refs[3 * count + 1 :]
    blocks = window_ref.shape[0]
    rows = blocks * GROUP
    edge = jnp.zeros((GROUP, LANES), F32)
    windows[pl.ds(0, GROUP), :] = edge
    windows[pl.ds(rows + GROUP, GROUP), :] = edge
    windows[pl.ds(GROUP, rows), :] = window_ref[...].astype(F32).reshape(rows, LANES)
    for source, pad, work in zip(inputs, padded, flat):
        work[...] = source[...].astype(F32).reshape(rows, LANES)
        if backward:
            spots = lax.broadcasted_iota(jnp.int32, (LANES, LANES), 0) + lax.broadcasted_iota(
                jnp.int32, (LANES, LANES), 1
            )
            mirror = jnp.where(spots == LANES - 1, 1.0, 0.0).astype(BF16)
            work[...] = jnp.dot(work[...].astype(BF16), mirror, preferred_element_type=F32)
        for chan in range(GROUP):
            pad[chan, pl.ds(0, blocks), :] = jnp.zeros((blocks, LANES), F32)
            pad[chan, pl.ds(blocks, blocks), :] = work[pl.ds(chan, blocks, stride=GROUP), :]

    def channel(chan, carry):
        def two_lags(pair, total):
            left, right = [], []
            for lag in (2 * pair, 2 * pair + 1):
                base = pl.multiple_of((lag + 1) * GROUP, GROUP) + chan
                current = windows[pl.ds(base, 1), :]
                other = windows[pl.ds(base + (GROUP if backward else -GROUP), 1), :]
                for first in range(0, LANES, 16):
                    right.append(toeplitz_rows(current, other, first, backward).astype(BF16))
                start = lag + 1 if backward else blocks - lag
                left.append(
                    jnp.concatenate([pad[chan, pl.ds(start, blocks), :] for pad in padded], axis=0)
                )
            return total + jnp.dot(
                jnp.concatenate(left, axis=1).astype(BF16),
                jnp.concatenate(right, axis=0),
                preferred_element_type=F32,
            )

        total = lax.fori_loop(
            0, blocks // 2, two_lags, jnp.zeros((count * blocks, LANES), F32), unroll=blocks // 2
        )
        for i, work in enumerate(flat):
            work[pl.ds(chan, blocks, stride=GROUP), :] = total[i * blocks : (i + 1) * blocks]
        return carry

    lax.fori_loop(0, GROUP, channel, 0)
    for output, work in zip(outputs, flat):
        output[...] = work[...].reshape(blocks, GROUP, LANES).astype(BF16)


def long_convolution(window, inputs, backward):
    count = len(inputs)
    blocks = window.shape[0]
    return pl.pallas_call(
        functools.partial(long_kernel, backward, count),
        out_shape=[jax.ShapeDtypeStruct(window.shape, BF16)] * count,
        in_specs=[VMEM] * (count + 1),
        out_specs=[VMEM] * count,
        scratch_shapes=[pltpu.VMEM(((blocks + 2) * GROUP, LANES), F32)]
        + [pltpu.VMEM((GROUP, 2 * blocks, LANES), F32)] * count
        + [pltpu.VMEM((blocks * GROUP, LANES), F32)] * count,
        compiler_params=pltpu.CompilerParams(vmem_limit_bytes=40 << 20),
    )(window, *inputs)


def to_channel_rows(block, index, target):
    target[pl.ds(16 * index, 16)] = block.T.reshape(16, GROUP, LANES).astype(BF16)


def from_channel_rows(source, index):
    return source[pl.ds(16 * index, 16)].astype(F32).reshape(LANES, LANES).T


def pad_before(pad, stream, earlier_ref, features_ref):
    pad[pl.ds(0, 8), :] = earlier_ref[stream].astype(F32)[8:, :]
    pad[pl.ds(8, LANES), :] = features_ref[stream].astype(F32)


def short_kernel(features_ref, earlier_ref, taps_ref, filter_ref, shorted_ref, filt_ref, prod_ref, pad):
    width = features_ref.shape[2]
    for stream in range(3):
        pad_before(pad, stream, earlier_ref, features_ref)
        for lanes in lane_chunks(width):
            for top in (0, 64):
                running = jnp.zeros((64, LANES), F32)
                for lag in range(TAPS):
                    running = running + taps_ref[stream, lag : lag + 1, lanes] * pad[
                        pl.ds(8 - lag + top, 64), lanes
                    ]
                shorted_ref[stream, pl.ds(top, 64), lanes] = running.astype(BF16)
    for index, lanes in enumerate(lane_chunks(width)):
        product = shorted_ref[1, :, lanes].astype(F32) * shorted_ref[2, :, lanes].astype(F32)
        to_channel_rows(product, index, prod_ref)
        to_channel_rows(filter_ref[:, lanes].astype(F32), index, filt_ref)


def gate_kernel(back_ref, shorted_ref, gain_ref, grad_ref, conv_ref, sums_ref):
    width = conv_ref.shape[1]
    squares = jnp.zeros((LANES, LANES), F32)
    tilts = jnp.zeros((LANES, LANES), F32)
    for index, lanes in enumerate(lane_chunks(width)):
        conv = from_channel_rows(back_ref, index)
        conv_ref[:, lanes] = conv.astype(BF16)
        gated = shorted_ref[0, :, lanes].astype(F32) * conv
        squares = squares + gated * gated
        tilts = tilts + gain_ref[:, lanes] * grad_ref[:, lanes].astype(F32) * gated
    sums_ref[...] = jnp.zeros(sums_ref.shape, F32)
    sums_ref[pl.ds(0, 1), :] = jnp.sum(squares.T, axis=0, keepdims=True)
    sums_ref[pl.ds(1, 1), :] = jnp.sum(tilts.T, axis=0, keepdims=True)


def norm_kernel(
    all_ref, conv_ref, shorted_ref, gain_ref, grad_ref, normed_ref, pieces_ref, first_ref, gain_grad_ref
):
    width = conv_ref.shape[1]
    channels = width * all_ref.shape[0]
    sums = jnp.sum(all_ref[...], axis=0)
    scale = lax.rsqrt(sums[0:1] / channels + norm_eps)
    bend = scale**3 * sums[1:2] / channels
    scale = jnp.broadcast_to(scale, (LANES, LANES)).T
    bend = jnp.broadcast_to(bend, (LANES, LANES)).T
    for index, lanes in enumerate(lane_chunks(width)):
        conv = conv_ref[:, lanes].astype(F32)
        q_short = shorted_ref[0, :, lanes].astype(F32)
        gain = gain_ref[:, lanes]
        upstream = grad_ref[:, lanes].astype(F32)
        gated = q_short * conv
        normed_ref[:, lanes] = (gated * scale * gain).astype(BF16)
        grad_gated = scale * (gain * upstream) - gated * bend
        gain_grad_ref[:, lanes] = jnp.sum(upstream * gated * scale, axis=0, keepdims=True)
        first_ref[:, lanes] = (grad_gated * conv).astype(BF16)
        to_channel_rows(grad_gated * q_short, index, pieces_ref)


def stream_kernel(
    grad_prod_ref,
    grad_filt_ref,
    shorted_ref,
    first_ref,
    features_ref,
    earlier_ref,
    gain_grad_ref,
    filter_grad_ref,
    streams_ref,
    sums_ref,
    pad,
):
    width = first_ref.shape[1]
    chunks = lane_chunks(width)
    sums_ref[...] = jnp.zeros(sums_ref.shape, F32)

    def put(row, index, value):
        spot = row * len(chunks) + index
        sums_ref[spot // 2, pl.ds(spot % 2, 1), :] = value

    for index, lanes in enumerate(chunks):
        filter_grad_ref[:, lanes] = from_channel_rows(grad_filt_ref, index).astype(BF16)
        grad_product = from_channel_rows(grad_prod_ref, index)
        streams_ref[0, :, lanes] = first_ref[:, lanes]
        streams_ref[1, :, lanes] = (grad_product * shorted_ref[2, :, lanes].astype(F32)).astype(BF16)
        streams_ref[2, :, lanes] = (grad_product * shorted_ref[1, :, lanes].astype(F32)).astype(BF16)
        put(3 * TAPS, index, gain_grad_ref[:, lanes])
    for stream in range(3):
        pad_before(pad, stream, earlier_ref, features_ref)
        for index, lanes in enumerate(chunks):
            grads = streams_ref[stream, :, lanes].astype(F32)
            for lag in range(TAPS):
                value = jnp.sum(grads * pad[pl.ds(8 - lag, LANES), lanes], axis=0, keepdims=True)
                put(stream * TAPS + lag, index, value)


def gather_kernel(streams_ref, later_ref, taps_ref, out_ref, pad):
    width = streams_ref.shape[2]
    for stream in range(3):
        pad[pl.ds(0, LANES), :] = streams_ref[stream].astype(F32)
        pad[pl.ds(LANES, 8), :] = later_ref[stream].astype(F32)[:8, :]
        for lanes in lane_chunks(width):
            for top in (0, 64):
                total = jnp.zeros((64, LANES), F32)
                for lag in range(TAPS):
                    total = total + taps_ref[stream, lag : lag + 1, lanes] * pad[
                        pl.ds(lag + top, 64), lanes
                    ]
                out_ref[stream, pl.ds(top, 64), lanes] = total.astype(BF16)


def local(kernel, outs, scratch=()):
    return pl.pallas_call(
        kernel,
        out_shape=[jax.ShapeDtypeStruct(shape, kind) for shape, kind in outs],
        out_specs=[VMEM] * len(outs),
        scratch_shapes=list(scratch),
        compiler_params=pltpu.CompilerParams(vmem_limit_bytes=40 << 20),
    )


def per_device(features, short_taps, long_filter, gain, out_grad):
    seq_rows, width = long_filter.shape
    ctx_size = lax.axis_size("ctx")
    pieces = (ctx_size, width // ctx_size, seq_rows)
    plane = (seq_rows, width)
    streams = (3, seq_rows, width)
    pad = pltpu.VMEM((seq_rows + 8, width), F32)
    gain = gain[None, :]
    earlier = passed_along(features[:, seq_rows - 16 :, :], "ctx", 1)
    shorted, filt, prod = local(short_kernel, [(streams, BF16), (pieces, BF16), (pieces, BF16)], [pad])(
        features, earlier, short_taps, long_filter
    )
    filt, prod = exchange([filt, prod], 0)
    (conv,) = long_convolution(filt, [prod], False)
    (conv,) = exchange([conv], 1)
    conv, sums = local(gate_kernel, [(plane, BF16), ((8, seq_rows), F32)])(conv, shorted, gain, out_grad)
    sums = row_sums(sums, 2)
    normed, grad_conv, first, gain_grad = local(
        norm_kernel, [(plane, BF16), (pieces, BF16), (plane, BF16), ((1, width), F32)]
    )(sums, conv, shorted, gain, out_grad)
    (grad_conv,) = exchange([grad_conv], 3)
    grad_prod, grad_filt = long_convolution(grad_conv, [filt, prod], True)
    grad_prod, grad_filt = exchange([grad_prod, grad_filt], 4, True)
    filter_grad, grad_short, sums = local(
        stream_kernel, [(plane, BF16), (streams, BF16), ((ctx_size, 2, LANES), F32)], [pad]
    )(grad_prod, grad_filt, shorted, first, features, earlier, gain_grad)
    later = passed_along(grad_short[:, :16, :], "ctx", -1)
    (feature_grad,) = local(gather_kernel, [(streams, BF16)], [pad])(grad_short, later, short_taps)
    sums = ctx_sum(sums, 5).reshape(-1)[: (3 * TAPS + 1) * width].reshape(3 * TAPS + 1, width)
    taps_grad = sums[: 3 * TAPS].reshape(3, TAPS, width)
    return (normed, feature_grad, filter_grad, taps_grad, sums[3 * TAPS])


def solution(mesh):
    return jax.shard_map(
        per_device,
        mesh=mesh,
        in_specs=(
            P(None, "ctx", "tp"),
            P(None, None, "tp"),
            P("ctx", "tp"),
            P("tp"),
            P("ctx", "tp"),
        ),
        out_specs=(
            P("ctx", "tp"),
            P(None, "ctx", "tp"),
            P("ctx", "tp"),
            P(None, None, "tp"),
            P("tp"),
        ),
        check_vma=False,
    )
```

```python
import functools

import jax
import jax.numpy as jnp
from jax import lax
from jax.experimental import pallas as pl
from jax.experimental.pallas import tpu as pltpu
from jax.sharding import PartitionSpec as P

F32 = jnp.float32
BF16 = jnp.bfloat16
MESH = pl.DeviceIdType.MESH
norm_eps = 1e-06

TAPS = 7
LANES = 128
GROUP = 8
VMEM = pl.BlockSpec(memory_space=pltpu.VMEM)


def lane_chunks(width):
    return [slice(start, start + LANES) for start in range(0, width, LANES)]


def each_partner(me, visit, crossing=True, within=True):
    row, half, col = me // 16, (me // 8) % 2, me % 8

    def other_half(step, carry):
        visit(((row + step // 8) % 4) * 16 + (1 - half) * 8 + (col + step % 8) % 8)
        return carry

    def same_half(step, carry):
        visit(((row + step // 8) % 4) * 16 + half * 8 + (col + step % 8) % 8)
        return carry

    if crossing:
        lax.fori_loop(0, 32, other_half, 0)
    if within:
        lax.fori_loop(1, 32, same_half, 0)


def remote(source, target, sems, device):
    return pltpu.make_async_remote_copy(
        src_ref=source,
        dst_ref=target,
        send_sem=sems.at[0],
        recv_sem=sems.at[1],
        device_id=device,
        device_id_type=MESH,
    )


def start_exchange(me, source, target, sems):
    def visit(partner):
        remote(source.at[partner], target.at[me], sems, {"ctx": partner}).start()

    each_partner(me, visit)
    target[pl.ds(me, 1)] = source[pl.ds(me, 1)]


def start_gather(me, piece, target, sems):
    def visit(partner):
        remote(piece, target.at[me], sems, {"ctx": partner}).start()

    each_partner(me, visit)
    target[pl.ds(me, 1)] = piece[...][None]


def await_slots(ref, count, sem):
    slots = ref.at[pl.ds(0, count)]
    pltpu.make_async_copy(slots, slots, sem).wait()


def toeplitz_rows(current, other, first, backward):
    rows = lax.broadcasted_iota(jnp.int32, (16, LANES), 0) + first
    lanes = lax.broadcasted_iota(jnp.int32, (16, LANES), 1)
    current = jnp.broadcast_to(current, (16, LANES))
    other = jnp.broadcast_to(other, (16, LANES))
    if backward:
        mixed = jnp.where(lanes >= LANES - 1 - rows, current, other)
        return pltpu.roll(mixed, first + 1, 1, stride=1, stride_axis=0)
    mixed = jnp.where(lanes < LANES - rows, current, other)
    return pltpu.roll(mixed, first, 1, stride=1, stride_axis=0)


def fill_padded(pad, work, mirrored):
    blocks = pad.shape[1] // 2
    if mirrored:
        spots = lax.broadcasted_iota(jnp.int32, (LANES, LANES), 0) + lax.broadcasted_iota(
            jnp.int32, (LANES, LANES), 1
        )
        mirror = jnp.where(spots == LANES - 1, 1.0, 0.0).astype(BF16)
    for chan in range(GROUP):
        rows = work[pl.ds(chan, blocks, stride=GROUP), :]
        if mirrored:
            rows = jnp.dot(rows.astype(BF16), mirror, preferred_element_type=F32)
        pad[chan, pl.ds(0, blocks), :] = jnp.zeros((blocks, LANES), F32)
        pad[chan, pl.ds(blocks, blocks), :] = rows


def fill_windows(windows, pieces):
    blocks = pieces.shape[0]
    rows = blocks * GROUP
    edge = jnp.zeros((GROUP, LANES), F32)
    windows[pl.ds(0, GROUP), :] = edge
    windows[pl.ds(rows + GROUP, GROUP), :] = edge
    windows[pl.ds(GROUP, rows), :] = pieces[...].astype(F32).reshape(rows, LANES)


def long_products(backward, windows, padded, flat):
    count = len(padded)
    blocks = padded[0].shape[1] // 2

    def channel(chan, carry):
        def two_lags(pair, total):
            left, right = [], []
            for lag in (2 * pair, 2 * pair + 1):
                base = pl.multiple_of((lag + 1) * GROUP, GROUP) + chan
                current = windows[pl.ds(base, 1), :]
                other = windows[pl.ds(base + (GROUP if backward else -GROUP), 1), :]
                for first in range(0, LANES, 16):
                    right.append(toeplitz_rows(current, other, first, backward).astype(BF16))
                start = lag + 1 if backward else blocks - lag
                left.append(
                    jnp.concatenate([pad[chan, pl.ds(start, blocks), :] for pad in padded], axis=0)
                )
            return total + jnp.dot(
                jnp.concatenate(left, axis=1).astype(BF16),
                jnp.concatenate(right, axis=0),
                preferred_element_type=F32,
            )

        total = lax.fori_loop(
            0, blocks // 2, two_lags, jnp.zeros((count * blocks, LANES), F32), unroll=blocks // 2
        )
        for i, work in enumerate(flat):
            work[pl.ds(chan, blocks, stride=GROUP), :] = total[i * blocks : (i + 1) * blocks]
        return carry

    lax.fori_loop(0, GROUP, channel, 0)


def to_pieces(block):
    return block.T.reshape(16, GROUP, LANES).astype(BF16)


def from_pieces(pieces):
    return pieces.astype(F32).reshape(LANES, LANES).T


def owner_taps(taps, stream):
    return [
        jnp.broadcast_to(taps[:, stream * TAPS + lag : stream * TAPS + lag + 1], (GROUP, LANES))
        for lag in range(TAPS)
    ]


def owner_short(raw, which, taps, target):
    lanes = lax.broadcasted_iota(jnp.int32, (GROUP, LANES), 1)

    def block(index, before):
        now = raw[index, which].astype(F32)
        total = taps[0] * now
        after = []
        for lag in range(1, TAPS):
            turned = pltpu.roll(now, lag, 1)
            total = total + taps[lag] * jnp.where(lanes >= lag, turned, before[lag - 1])
            after.append(turned)
        target[pl.ds(pl.multiple_of(index * GROUP, GROUP), GROUP), :] = total.astype(BF16).astype(F32)
        return tuple(after)

    zero = jnp.zeros((GROUP, LANES), F32)
    lax.fori_loop(0, raw.shape[0], block, (zero,) * (TAPS - 1), unroll=8)


def owner_back(raw, which, taps, grad_flat, partner_flat, target, slot):
    lanes = lax.broadcasted_iota(jnp.int32, (GROUP, LANES), 1)
    blocks = raw.shape[0]

    def block(step, carry):
        after, sums = carry
        index = blocks - 1 - step
        grad = grad_flat[pl.ds(pl.multiple_of(step * GROUP, GROUP), GROUP), :].astype(BF16).astype(F32)
        rows = pl.ds(pl.multiple_of(index * GROUP, GROUP), GROUP)
        grad = (grad * partner_flat[rows, :]).astype(BF16).astype(F32)
        value = raw[index, which].astype(F32)
        total = taps[0] * grad
        new_sums = [sums[0] + value * grad]
        new_after = []
        for lag in range(1, TAPS):
            turned = pltpu.roll(grad, LANES - lag, 1)
            moved = jnp.where(lanes < LANES - lag, turned, after[lag - 1])
            total = total + taps[lag] * moved
            new_sums.append(sums[lag] + value * moved)
            new_after.append(turned)
        target[index, slot] = total.astype(BF16)
        return tuple(new_after), tuple(new_sums)

    zero = jnp.zeros((GROUP, LANES), F32)
    _, sums = lax.fori_loop(
        0, blocks, block, ((zero,) * (TAPS - 1), (zero,) * TAPS), unroll=8
    )
    return sums


def block_kernel(
    features_ref,
    taps_ref,
    filter_ref,
    gain_ref,
    grad_ref,
    normed_ref,
    feature_grad_ref,
    filter_grad_ref,
    first_sums_ref,
    owner_sums_ref,
    filt_send,
    filt_recv,
    pair_send,
    pair_recv,
    conv_send,
    conv_recv,
    back_send,
    back_recv,
    out_send,
    out_recv,
    before_recv,
    after_send,
    after_recv,
    row_send,
    row_recv,
    part_send,
    part_recv,
    part_sum,
    first_all,
    owner_sum,
    owner_all,
    taps_turned,
    pad,
    q_short,
    conv,
    windows,
    k_short,
    v_short,
    flat_a,
    flat_b,
    pad_fwd,
    pad_filt,
    pad_prod,
    sems,
):
    me = lax.axis_index("ctx")
    rank = lax.axis_index("tp")
    half = (me // 8) % 2
    width = filter_ref.shape[1]
    chunks = list(enumerate(lane_chunks(width)))
    blocks = filt_recv.shape[0]
    rows = blocks * GROUP
    channels = width * 8
    following = {"ctx": (me + 1) % 64}
    preceding = {"ctx": (me + 63) % 64}

    barrier = pltpu.get_barrier_semaphore()

    def greet(partner):
        pl.semaphore_signal(barrier, inc=1, device_id={"ctx": partner}, device_id_type=MESH)

    each_partner(me, greet)
    for step in range(1, 8):
        pl.semaphore_signal(
            barrier, inc=1, device_id={"tp": (rank + step) % 8}, device_id_type=MESH
        )

    for index, lanes in chunks:
        spot = pl.ds(16 * index, 16)
        filt_send[spot] = to_pieces(filter_ref[:, lanes].astype(F32))
        pair_send[spot, 0] = to_pieces(features_ref[1, :, lanes].astype(F32))
        pair_send[spot, 1] = to_pieces(features_ref[2, :, lanes].astype(F32))
    pl.semaphore_wait(barrier, 70)
    start_exchange(me, filt_send, filt_recv, sems.at[0])
    start_exchange(me, pair_send, pair_recv, sems.at[1])
    last = features_ref.at[0, pl.ds(LANES - 16, 16)]
    remote(last, before_recv, sems.at[2], following).start()

    filler = jnp.zeros((LANES - 3 * TAPS, LANES), F32)
    for index, lanes in chunks:
        stack = jnp.concatenate([taps_ref[i, :, lanes] for i in range(3)] + [filler], axis=0)
        taps_turned[pl.ds(LANES * index, LANES), :] = stack.T
    own_taps = taps_turned[pl.ds(pl.multiple_of(me * GROUP, GROUP), GROUP), :]
    remote(last, before_recv, sems.at[2], following).wait_recv()
    pad[pl.ds(0, 8), :] = jnp.where(me > 0, before_recv[...].astype(F32)[8:, :], 0.0)
    pad[pl.ds(8, LANES), :] = features_ref[0].astype(F32)
    for _, lanes in chunks:
        for top in (0, 64):
            running = jnp.zeros((64, LANES), F32)
            for lag in range(TAPS):
                running = running + taps_ref[0, lag : lag + 1, lanes] * pad[
                    pl.ds(8 - lag + top, 64), lanes
                ]
            q_short[pl.ds(top, 64), lanes] = running.astype(BF16).astype(F32)

    await_slots(filt_recv, 63, sems.at[0, 1])
    fill_windows(windows, filt_recv)
    flat_a[...] = filt_recv[...].astype(F32).reshape(rows, LANES)
    fill_padded(pad_filt, flat_a, True)
    await_slots(pair_recv, 63, sems.at[1, 1])
    k_taps, v_taps = owner_taps(own_taps, 1), owner_taps(own_taps, 2)
    owner_short(pair_recv, 0, k_taps, k_short)
    owner_short(pair_recv, 1, v_taps, v_short)
    flat_b[...] = (k_short[...] * v_short[...]).astype(BF16).astype(F32)
    fill_padded(pad_fwd, flat_b, False)
    long_products(False, windows, [pad_fwd], [flat_a])
    conv_send[...] = flat_a[...].reshape(blocks, GROUP, LANES).astype(BF16)
    start_exchange(me, conv_send, conv_recv, sems.at[3])
    fill_padded(pad_prod, flat_b, True)
    await_slots(conv_recv, 63, sems.at[3, 1])

    squares = jnp.zeros((LANES, LANES), F32)
    tilts = jnp.zeros((LANES, LANES), F32)
    for index, lanes in chunks:
        value = from_pieces(conv_recv[pl.ds(16 * index, 16)])
        conv[:, lanes] = value
        gated = q_short[:, lanes] * value
        squares = squares + gated * gated
        tilts = tilts + gain_ref[:, lanes] * grad_ref[:, lanes].astype(F32) * gated
    row_send[...] = jnp.zeros(row_send.shape, F32)
    row_send[pl.ds(0, 1), :] = jnp.sum(squares.T, axis=0, keepdims=True)
    row_send[pl.ds(1, 1), :] = jnp.sum(tilts.T, axis=0, keepdims=True)
    for step in range(1, 8):
        remote(row_send, row_recv.at[rank], sems.at[4], {"tp": (rank + step) % 8}).start()
    row_recv[pl.ds(rank, 1)] = row_send[...][None]
    await_slots(row_recv, 7, sems.at[4, 1])
    sums = jnp.sum(row_recv[...], axis=0)
    scale = lax.rsqrt(sums[0:1] / channels + norm_eps)
    bend = scale**3 * sums[1:2] / channels
    scale = jnp.broadcast_to(scale, (LANES, LANES)).T
    bend = jnp.broadcast_to(bend, (LANES, LANES)).T

    def gate(lanes):
        value, q_value = conv[:, lanes], q_short[:, lanes]
        gain = gain_ref[:, lanes]
        upstream = grad_ref[:, lanes].astype(F32)
        gated = q_value * value
        grad_gated = scale * (gain * upstream) - gated * bend
        return value, q_value, gain, upstream, gated, grad_gated

    for index, lanes in chunks:
        _, q_value, _, _, _, grad_gated = gate(lanes)
        back_send[pl.ds(16 * index, 16)] = to_pieces(grad_gated * q_value)
    start_exchange(me, back_send, back_recv, sems.at[5])

    for index, lanes in chunks:
        value, _, gain, upstream, gated, grad_gated = gate(lanes)
        normed_ref[:, lanes] = (gated * scale * gain).astype(BF16)
        part_send[7 * 4 + index] = jnp.sum(upstream * gated * scale, axis=0, keepdims=True)
        first = (grad_gated * value).astype(BF16)
        after_send[:, lanes] = first[:16]
        first = first.astype(F32)
        conv[:, lanes] = first
        for lag in range(TAPS):
            part_send[lag * 4 + index] = jnp.sum(
                first * pad[pl.ds(8 - lag, LANES), lanes], axis=0, keepdims=True
            )
    remote(after_send, after_recv, sems.at[6], preceding).start()
    mine = (me // 16) * 8 + me % 8

    def send_part(partner):
        place = (partner // 16) * 8 + partner % 8
        remote(part_send.at[place], part_recv.at[mine], sems.at[7], {"ctx": partner}).start()

    each_partner(me, send_part, crossing=False)
    part_recv[pl.ds(mine, 1)] = part_send[pl.ds(mine, 1)]
    await_slots(part_recv, 31, sems.at[7, 1])
    part_sum[...] = jnp.sum(part_recv[...], axis=0)
    start_gather(me, part_sum, first_all, sems.at[8])

    await_slots(back_recv, 63, sems.at[5, 1])
    fill_windows(windows, back_recv)
    long_products(True, windows, [pad_filt, pad_prod], [flat_a, flat_b])

    def place_filter(index, carry):
        step = pl.multiple_of((blocks - 1 - index) * GROUP, GROUP)
        out_send[index, 0] = flat_b[pl.ds(step, GROUP), :].astype(BF16)
        return carry

    lax.fori_loop(0, blocks, place_filter, 0, unroll=8)
    k_sums = owner_back(pair_recv, 0, k_taps, flat_a, v_short, out_send, 1)
    v_sums = owner_back(pair_recv, 1, v_taps, flat_a, k_short, out_send, 2)
    start_exchange(me, out_send, out_recv, sems.at[9])
    lane_ids = lax.broadcasted_iota(jnp.int32, (GROUP, LANES), 1)
    chan_ids = lax.broadcasted_iota(jnp.int32, (GROUP, LANES), 0)
    packed = jnp.zeros((GROUP, LANES), F32)
    for place, value in enumerate(k_sums + v_sums):
        total = jnp.sum(value, axis=1, keepdims=True)
        packed = packed + jnp.where(lane_ids == place * GROUP + chan_ids, total, 0.0)
    owner_sum[...] = jnp.sum(packed, axis=0, keepdims=True)
    start_gather(me, owner_sum, owner_all, sems.at[10])

    remote(after_send, after_recv, sems.at[6], preceding).wait_recv()
    pad[pl.ds(0, LANES), :] = conv[...]
    pad[pl.ds(LANES, 8), :] = jnp.where(me < 63, after_recv[...].astype(F32)[:8, :], 0.0)
    for _, lanes in chunks:
        for top in (0, 64):
            total = jnp.zeros((64, LANES), F32)
            for lag in range(TAPS):
                total = total + taps_ref[0, lag : lag + 1, lanes] * pad[pl.ds(lag + top, 64), lanes]
            feature_grad_ref[0, pl.ds(top, 64), lanes] = total.astype(BF16)

    await_slots(first_all, 63, sems.at[8, 1])
    first_sums_ref[...] = first_all[...]
    await_slots(out_recv, 63, sems.at[9, 1])
    for index, lanes in chunks:
        spot = pl.ds(16 * index, 16)
        filter_grad_ref[:, lanes] = from_pieces(out_recv[spot, 0]).astype(BF16)
        feature_grad_ref[1, :, lanes] = from_pieces(out_recv[spot, 1]).astype(BF16)
        feature_grad_ref[2, :, lanes] = from_pieces(out_recv[spot, 2]).astype(BF16)
    await_slots(owner_all, 63, sems.at[10, 1])
    owner_sums_ref[...] = owner_all[...]

    for ref, count, number in (
        (filt_recv, 63, 0),
        (pair_recv, 63, 1),
        (conv_recv, 63, 3),
        (row_recv, 7, 4),
        (back_recv, 63, 5),
        (part_recv, 31, 7),
        (first_all, 63, 8),
        (out_recv, 63, 9),
        (owner_all, 63, 10),
    ):
        await_slots(ref, count, sems.at[number, 0])
    remote(last, before_recv, sems.at[2], following).wait_send()
    remote(after_send, after_recv, sems.at[6], preceding).wait_send()


def per_device(features, short_taps, long_filter, gain, out_grad):
    seq_rows, width = long_filter.shape
    blocks = lax.axis_size("ctx")
    pieces = (blocks, GROUP, LANES)
    flat = (blocks * GROUP, LANES)
    padded = (GROUP, 2 * blocks, LANES)
    row = (1, LANES)
    exchanged = [pltpu.VMEM(pieces, BF16)] * 2
    pairs = [pltpu.VMEM((blocks, 2, GROUP, LANES), BF16)] * 2
    triples = [pltpu.VMEM((blocks, 3, GROUP, LANES), BF16)] * 2
    normed, feature_grad, filter_grad, first, owner = pl.pallas_call(
        block_kernel,
        out_shape=[
            jax.ShapeDtypeStruct((seq_rows, width), BF16),
            jax.ShapeDtypeStruct((3, seq_rows, width), BF16),
            jax.ShapeDtypeStruct((seq_rows, width), BF16),
            jax.ShapeDtypeStruct((blocks,) + row, F32),
            jax.ShapeDtypeStruct((blocks,) + row, F32),
        ],
        in_specs=[VMEM] * 5,
        out_specs=[VMEM] * 5,
        scratch_shapes=exchanged
        + pairs
        + exchanged
        + exchanged
        + triples
        + [pltpu.VMEM((16, width), BF16)] * 3
        + [
            pltpu.VMEM((8, LANES), F32),
            pltpu.VMEM((8, 8, LANES), F32),
            pltpu.VMEM((32,) + row, F32),
            pltpu.VMEM((32,) + row, F32),
            pltpu.VMEM(row, F32),
            pltpu.VMEM((blocks,) + row, F32),
            pltpu.VMEM(row, F32),
            pltpu.VMEM((blocks,) + row, F32),
            pltpu.VMEM((width, LANES), F32),
            pltpu.VMEM((seq_rows + 8, width), F32),
            pltpu.VMEM((seq_rows, width), F32),
            pltpu.VMEM((seq_rows, width), F32),
            pltpu.VMEM(((blocks + 2) * GROUP, LANES), F32),
        ]
        + [pltpu.VMEM(flat, F32)] * 4
        + [pltpu.VMEM(padded, F32)] * 3
        + [pltpu.SemaphoreType.DMA((11, 2))],
        compiler_params=pltpu.CompilerParams(
            collective_id=0, has_side_effects=True, vmem_limit_bytes=48 << 20
        ),
    )(features, short_taps, long_filter, gain[None, :], out_grad)
    first = first.reshape(4, 2, 8, LANES).sum(axis=1).reshape(TAPS + 1, width)
    owner = owner.reshape(blocks, LANES)[:, : 2 * TAPS * GROUP].reshape(blocks, 2, TAPS, GROUP)
    owner = owner.transpose(1, 2, 0, 3).reshape(2, TAPS, width)
    taps_grad = jnp.concatenate([first[None, :TAPS], owner], axis=0)
    return (normed, feature_grad, filter_grad, taps_grad, first[TAPS])


def solution(mesh):
    return jax.shard_map(
        per_device,
        mesh=mesh,
        in_specs=(
            P(None, "ctx", "tp"),
            P(None, None, "tp"),
            P("ctx", "tp"),
            P("tp"),
            P("ctx", "tp"),
        ),
        out_specs=(
            P("ctx", "tp"),
            P(None, "ctx", "tp"),
            P("ctx", "tp"),
            P(None, None, "tp"),
            P("tp"),
        ),
        check_vma=False,
    )
```

```python
import functools

import jax
import jax.numpy as jnp
from jax import lax
from jax.experimental import pallas as pl
from jax.experimental.pallas import tpu as pltpu
from jax.sharding import PartitionSpec as P

F32 = jnp.float32
BF16 = jnp.bfloat16
MESH = pl.DeviceIdType.MESH
norm_eps = 1e-06

TAPS = 7
LANES = 128
GROUP = 8
HBM = pl.BlockSpec(memory_space=pltpu.HBM)


def lane_chunks(width):
    return [slice(start, start + LANES) for start in range(0, width, LANES)]


def each_partner(me, visit, same_half=False):
    row, half, col = me // 16, (me // 8) % 2, me % 8

    def one(step, carry):
        if same_half:
            visit(((row + 2 + step // 8) % 4) * 16 + half * 8 + (col + step % 8) % 8)
        else:
            side = (half + (step // 8) % 2) % 2
            visit(((row + 2 + step // 16) % 4) * 16 + side * 8 + (col + step % 8) % 8)
        return carry

    lax.fori_loop(0, 32 if same_half else 64, one, 0)


def remote(source, target, sems, device):
    return pltpu.make_async_remote_copy(
        src_ref=source,
        dst_ref=target,
        send_sem=sems.at[0],
        recv_sem=sems.at[1],
        device_id=device,
        device_id_type=MESH,
    )


def start_exchange(me, across, source, target, sems):
    def visit(partner):
        remote(source.at[partner], target.at[me], sems, {"ctx": partner, "tp": across}).start()

    each_partner(me, visit)


def start_gather(me, across, piece, target, sems):
    def visit(partner):
        remote(piece, target.at[me], sems, {"ctx": partner, "tp": across}).start()

    each_partner(me, visit)


def await_slots(ref, sem):
    pltpu.make_async_copy(ref, ref, sem).wait()


def toeplitz_rows(current, other, first, backward):
    rows = lax.broadcasted_iota(jnp.int32, (16, LANES), 0) + first
    lanes = lax.broadcasted_iota(jnp.int32, (16, LANES), 1)
    current = jnp.broadcast_to(current, (16, LANES))
    other = jnp.broadcast_to(other, (16, LANES))
    if backward:
        mixed = jnp.where(lanes >= LANES - 1 - rows, current, other)
        return pltpu.roll(mixed, first + 1, 1, stride=1, stride_axis=0)
    mixed = jnp.where(lanes < LANES - rows, current, other)
    return pltpu.roll(mixed, first, 1, stride=1, stride_axis=0)


def fill_padded(pad, work, mirrored):
    blocks = pad.shape[1] // 2
    if mirrored:
        spots = lax.broadcasted_iota(jnp.int32, (LANES, LANES), 0) + lax.broadcasted_iota(
            jnp.int32, (LANES, LANES), 1
        )
        mirror = jnp.where(spots == LANES - 1, 1.0, 0.0).astype(BF16)
    for chan in range(GROUP):
        rows = work[pl.ds(chan, blocks, stride=GROUP), :]
        if mirrored:
            rows = jnp.dot(rows.astype(BF16), mirror, preferred_element_type=F32)
        pad[chan, pl.ds(0, blocks), :] = jnp.zeros((blocks, LANES), F32)
        pad[chan, pl.ds(blocks, blocks), :] = rows


def fill_windows(windows, pieces):
    blocks = pieces.shape[0]
    rows = blocks * GROUP
    edge = jnp.zeros((GROUP, LANES), F32)
    windows[pl.ds(0, GROUP), :] = edge
    windows[pl.ds(rows + GROUP, GROUP), :] = edge
    windows[pl.ds(GROUP, rows), :] = pieces[...].astype(F32).reshape(rows, LANES)


def toeplitz_block(windows, chan, lag, backward):
    base = pl.multiple_of((lag + 1) * GROUP, GROUP) + chan
    current = windows[pl.ds(base, 1), :]
    other = windows[pl.ds(base + (GROUP if backward else -GROUP), 1), :]
    return [
        toeplitz_rows(current, other, first, backward).astype(BF16) for first in range(0, LANES, 16)
    ]


def build_toeplitz(windows, toeplitz):
    blocks = toeplitz.shape[1] // LANES

    def channel(chan, carry):
        def lags(lag, inner):
            rows = toeplitz_block(windows, chan, lag, False)
            for i, part in enumerate(rows):
                toeplitz[chan, pl.ds(pl.multiple_of(lag * LANES, LANES) + 16 * i, 16), :] = part
            return inner

        return lax.fori_loop(0, blocks, lags, carry, unroll=16)

    lax.fori_loop(0, GROUP, channel, 0)


def causal_products(toeplitz, padded, flat):
    blocks = padded.shape[1] // 2

    def channel(chan, carry):
        def two_lags(pair, total):
            left = [padded[chan, pl.ds(blocks - 2 * pair - i, blocks), :] for i in range(2)]
            right = toeplitz[chan, pl.ds(pl.multiple_of(pair * 2 * LANES, 2 * LANES), 2 * LANES), :]
            return total + jnp.dot(
                jnp.concatenate(left, axis=1).astype(BF16), right, preferred_element_type=F32
            )

        total = lax.fori_loop(
            0, blocks // 2, two_lags, jnp.zeros((blocks, LANES), F32), unroll=blocks // 2
        )
        flat[pl.ds(chan, blocks, stride=GROUP), :] = total
        return carry

    lax.fori_loop(0, GROUP, channel, 0)


def lagged_products(windows, padded, flat):
    count = len(padded)
    blocks = padded[0].shape[1] // 2

    def channel(chan, carry):
        def two_lags(pair, total):
            left, right = [], []
            for lag in (2 * pair, 2 * pair + 1):
                right += toeplitz_block(windows, chan, lag, True)
                left.append(
                    jnp.concatenate([pad[chan, pl.ds(lag + 1, blocks), :] for pad in padded], axis=0)
                )
            return total + jnp.dot(
                jnp.concatenate(left, axis=1).astype(BF16),
                jnp.concatenate(right, axis=0),
                preferred_element_type=F32,
            )

        total = lax.fori_loop(
            0, blocks // 2, two_lags, jnp.zeros((count * blocks, LANES), F32), unroll=blocks // 2
        )
        for i, work in enumerate(flat):
            work[pl.ds(chan, blocks, stride=GROUP), :] = total[i * blocks : (i + 1) * blocks]
        return carry

    lax.fori_loop(0, GROUP, channel, 0)


def to_pieces(block):
    return block.T.reshape(16, GROUP, LANES).astype(BF16)


def from_pieces(pieces):
    return pieces.astype(F32).reshape(LANES, LANES).T


def owner_taps(taps, stream):
    return [
        jnp.broadcast_to(taps[:, stream * TAPS + lag : stream * TAPS + lag + 1], (GROUP, LANES))
        for lag in range(TAPS)
    ]


def owner_short(raw, which, taps, target):
    lanes = lax.broadcasted_iota(jnp.int32, (GROUP, LANES), 1)

    def block(index, before):
        now = raw[index, which].astype(F32)
        total = taps[0] * now
        after = []
        for lag in range(1, TAPS):
            turned = pltpu.roll(now, lag, 1)
            total = total + taps[lag] * jnp.where(lanes >= lag, turned, before[lag - 1])
            after.append(turned)
        target[pl.ds(pl.multiple_of(index * GROUP, GROUP), GROUP), :] = total.astype(BF16).astype(F32)
        return tuple(after)

    zero = jnp.zeros((GROUP, LANES), F32)
    lax.fori_loop(0, raw.shape[0], block, (zero,) * (TAPS - 1), unroll=8)


def owner_back(raw, which, taps, grad_flat, partner_flat, target, slot):
    lanes = lax.broadcasted_iota(jnp.int32, (GROUP, LANES), 1)
    blocks = raw.shape[0]

    def block(step, carry):
        after, sums = carry
        index = blocks - 1 - step
        grad = grad_flat[pl.ds(pl.multiple_of(step * GROUP, GROUP), GROUP), :].astype(BF16).astype(F32)
        rows = pl.ds(pl.multiple_of(index * GROUP, GROUP), GROUP)
        grad = (grad * partner_flat[rows, :]).astype(BF16).astype(F32)
        value = raw[index, which].astype(F32)
        total = taps[0] * grad
        new_sums = [sums[0] + value * grad]
        new_after = []
        for lag in range(1, TAPS):
            turned = pltpu.roll(grad, LANES - lag, 1)
            moved = jnp.where(lanes < LANES - lag, turned, after[lag - 1])
            total = total + taps[lag] * moved
            new_sums.append(sums[lag] + value * moved)
            new_after.append(turned)
        target[index, slot] = total.astype(BF16)
        return tuple(new_after), tuple(new_sums)

    zero = jnp.zeros((GROUP, LANES), F32)
    _, sums = lax.fori_loop(
        0, blocks, block, ((zero,) * (TAPS - 1), (zero,) * TAPS), unroll=8
    )
    return sums


def block_kernel(
    features_hbm,
    taps_hbm,
    filter_hbm,
    gain_hbm,
    grad_hbm,
    normed_hbm,
    feature_grad_hbm,
    filter_grad_hbm,
    taps_grad_hbm,
    gain_grad_hbm,
    normed_ref,
    feature_grad_ref,
    filter_grad_ref,
    taps_grad_ref,
    gain_grad_ref,
    features_ref,
    taps_ref,
    filter_ref,
    gain_ref,
    grad_ref,
    filt_send,
    filt_recv,
    pair_send,
    pair_recv,
    conv_send,
    conv_recv,
    back_send,
    back_recv,
    out_send,
    out_recv,
    before_recv,
    after_send,
    after_recv,
    row_send,
    row_recv,
    part_send,
    part_recv,
    part_sum,
    first_all,
    owner_sum,
    owner_all,
    taps_turned,
    taps_recv,
    pad,
    q_short,
    conv,
    windows,
    k_short,
    v_short,
    flat_a,
    flat_b,
    pad_fwd,
    pad_filt,
    pad_prod,
    toeplitz,
    sems,
    load_sems,
    store_sems,
):
    me = lax.axis_index("ctx")
    rank = lax.axis_index("tp")
    across = (rank + 4) % 8
    width = filter_ref.shape[1]
    chunks = list(enumerate(lane_chunks(width)))
    blocks = filt_recv.shape[0]
    rows = blocks * GROUP
    channels = width * 8
    following = {"ctx": (me + 1) % 64}
    preceding = {"ctx": (me + 63) % 64}

    barrier = pltpu.get_barrier_semaphore()

    def greet(partner):
        pl.semaphore_signal(
            barrier, inc=1, device_id={"ctx": partner, "tp": across}, device_id_type=MESH
        )

    for device in (following, preceding):
        pl.semaphore_signal(barrier, inc=1, device_id=device, device_id_type=MESH)
    for step in range(1, 8):
        pl.semaphore_signal(
            barrier, inc=1, device_id={"tp": (rank + step) % 8}, device_id_type=MESH
        )
    each_partner(me, greet)
    loads = [
        pltpu.make_async_copy(source, target, load_sems.at[i])
        for i, (source, target) in enumerate(
            (
                (filter_hbm, filter_ref),
                (features_hbm, features_ref),
                (taps_hbm, taps_ref),
                (gain_hbm, gain_ref),
                (grad_hbm, grad_ref),
            )
        )
    ]
    for load in loads:
        load.start()
    for load in loads:
        load.wait()

    for index, lanes in chunks:
        spot = pl.ds(16 * index, 16)
        filt_send[spot] = to_pieces(filter_ref[:, lanes].astype(F32))
        pair_send[spot, 0] = to_pieces(features_ref[1, :, lanes].astype(F32))
        pair_send[spot, 1] = to_pieces(features_ref[2, :, lanes].astype(F32))
    filler = jnp.zeros((LANES - 3 * TAPS, LANES), F32)
    for index, lanes in chunks:
        stack = jnp.concatenate([taps_ref[i, :, lanes] for i in range(3)] + [filler], axis=0)
        taps_turned[pl.ds(LANES * index, LANES), :] = stack.T
    pl.semaphore_wait(barrier, 73)
    start_exchange(me, across, filt_send, filt_recv, sems.at[0])
    start_exchange(me, across, pair_send, pair_recv, sems.at[1])
    own_taps = taps_turned.at[pl.ds(pl.multiple_of(me * GROUP, GROUP), GROUP)]
    taps_copy = remote(own_taps, taps_recv, sems.at[11], {"tp": across})
    taps_copy.start()
    last = features_ref.at[0, pl.ds(LANES - 16, 16)]
    remote(last, before_recv, sems.at[2], following).start()

    remote(last, before_recv, sems.at[2], following).wait_recv()
    pad[pl.ds(0, 8), :] = jnp.where(me > 0, before_recv[...].astype(F32)[8:, :], 0.0)
    pad[pl.ds(8, LANES), :] = features_ref[0].astype(F32)
    for _, lanes in chunks:
        for top in (0, 64):
            running = jnp.zeros((64, LANES), F32)
            for lag in range(TAPS):
                running = running + taps_ref[0, lag : lag + 1, lanes] * pad[
                    pl.ds(8 - lag + top, 64), lanes
                ]
            q_short[pl.ds(top, 64), lanes] = running.astype(BF16).astype(F32)

    await_slots(filt_recv, sems.at[0, 1])
    fill_windows(windows, filt_recv)
    build_toeplitz(windows, toeplitz)
    flat_a[...] = filt_recv[...].astype(F32).reshape(rows, LANES)
    fill_padded(pad_filt, flat_a, True)
    taps_copy.wait_recv()
    await_slots(pair_recv, sems.at[1, 1])
    turned = taps_recv[...]
    k_taps, v_taps = owner_taps(turned, 1), owner_taps(turned, 2)
    owner_short(pair_recv, 0, k_taps, k_short)
    owner_short(pair_recv, 1, v_taps, v_short)
    flat_b[...] = (k_short[...] * v_short[...]).astype(BF16).astype(F32)
    fill_padded(pad_fwd, flat_b, False)
    causal_products(toeplitz, pad_fwd, flat_a)
    conv_send[...] = flat_a[...].reshape(blocks, GROUP, LANES).astype(BF16)
    start_exchange(me, across, conv_send, conv_recv, sems.at[3])
    fill_padded(pad_prod, flat_b, True)
    await_slots(conv_recv, sems.at[3, 1])

    squares = jnp.zeros((LANES, LANES), F32)
    tilts = jnp.zeros((LANES, LANES), F32)
    for index, lanes in chunks:
        value = from_pieces(conv_recv[pl.ds(16 * index, 16)])
        conv[:, lanes] = value
        gated = q_short[:, lanes] * value
        squares = squares + gated * gated
        tilts = tilts + gain_ref[:, lanes] * grad_ref[:, lanes].astype(F32) * gated
    row_send[...] = jnp.zeros(row_send.shape, F32)
    row_send[pl.ds(0, 1), :] = jnp.sum(squares.T, axis=0, keepdims=True)
    row_send[pl.ds(1, 1), :] = jnp.sum(tilts.T, axis=0, keepdims=True)
    for step in range(1, 8):
        remote(row_send, row_recv.at[rank], sems.at[4], {"tp": (rank + step) % 8}).start()
    row_recv[pl.ds(rank, 1)] = row_send[...][None]
    await_slots(row_recv.at[pl.ds(0, 7)], sems.at[4, 1])
    sums = jnp.sum(row_recv[...], axis=0)
    scale = lax.rsqrt(sums[0:1] / channels + norm_eps)
    bend = scale**3 * sums[1:2] / channels
    scale = jnp.broadcast_to(scale, (LANES, LANES)).T
    bend = jnp.broadcast_to(bend, (LANES, LANES)).T

    def gate(lanes):
        value, q_value = conv[:, lanes], q_short[:, lanes]
        gain = gain_ref[:, lanes]
        upstream = grad_ref[:, lanes].astype(F32)
        gated = q_value * value
        grad_gated = scale * (gain * upstream) - gated * bend
        return value, q_value, gain, upstream, gated, grad_gated

    for index, lanes in chunks:
        _, q_value, _, _, _, grad_gated = gate(lanes)
        back_send[pl.ds(16 * index, 16)] = to_pieces(grad_gated * q_value)
    start_exchange(me, across, back_send, back_recv, sems.at[5])

    for index, lanes in chunks:
        value, _, gain, upstream, gated, grad_gated = gate(lanes)
        normed_ref[:, lanes] = (gated * scale * gain).astype(BF16)
        part_send[7 * 4 + index] = jnp.sum(upstream * gated * scale, axis=0, keepdims=True)
        first = (grad_gated * value).astype(BF16)
        after_send[:, lanes] = first[:16]
        first = first.astype(F32)
        conv[:, lanes] = first
        for lag in range(TAPS):
            part_send[lag * 4 + index] = jnp.sum(
                first * pad[pl.ds(8 - lag, LANES), lanes], axis=0, keepdims=True
            )
    remote(after_send, after_recv, sems.at[6], preceding).start()
    store_normed = pltpu.make_async_copy(normed_ref, normed_hbm, store_sems.at[0])
    store_normed.start()

    def send_part(partner):
        place = (partner // 16) * 8 + partner % 8
        remote(
            part_send.at[place], part_recv.at[me], sems.at[7], {"ctx": partner, "tp": across}
        ).start()

    each_partner(me, send_part)
    await_slots(part_recv, sems.at[7, 1])
    part_sum[...] = jnp.sum(part_recv[...], axis=0)
    mine = (me // 16) * 8 + me % 8

    def send_total(partner):
        remote(part_sum, first_all.at[mine], sems.at[8], {"ctx": partner, "tp": across}).start()

    each_partner(me, send_total, same_half=True)

    await_slots(back_recv, sems.at[5, 1])
    fill_windows(windows, back_recv)
    lagged_products(windows, [pad_filt, pad_prod], [flat_a, flat_b])

    def place_filter(index, carry):
        step = pl.multiple_of((blocks - 1 - index) * GROUP, GROUP)
        out_send[index, 0] = flat_b[pl.ds(step, GROUP), :].astype(BF16)
        return carry

    lax.fori_loop(0, blocks, place_filter, 0, unroll=8)
    k_sums = owner_back(pair_recv, 0, k_taps, flat_a, v_short, out_send, 1)
    v_sums = owner_back(pair_recv, 1, v_taps, flat_a, k_short, out_send, 2)
    start_exchange(me, across, out_send, out_recv, sems.at[9])
    lane_ids = lax.broadcasted_iota(jnp.int32, (GROUP, LANES), 1)
    chan_ids = lax.broadcasted_iota(jnp.int32, (GROUP, LANES), 0)
    packed = jnp.zeros((GROUP, LANES), F32)
    for place, value in enumerate(k_sums + v_sums):
        total = jnp.sum(value, axis=1, keepdims=True)
        packed = packed + jnp.where(lane_ids == place * GROUP + chan_ids, total, 0.0)
    owner_sum[...] = jnp.sum(packed, axis=0, keepdims=True)
    start_gather(me, across, owner_sum, owner_all, sems.at[10])

    remote(after_send, after_recv, sems.at[6], preceding).wait_recv()
    pad[pl.ds(0, LANES), :] = conv[...]
    pad[pl.ds(LANES, 8), :] = jnp.where(me < 63, after_recv[...].astype(F32)[:8, :], 0.0)
    for _, lanes in chunks:
        for top in (0, 64):
            total = jnp.zeros((64, LANES), F32)
            for lag in range(TAPS):
                total = total + taps_ref[0, lag : lag + 1, lanes] * pad[pl.ds(lag + top, 64), lanes]
            feature_grad_ref[0, pl.ds(top, 64), lanes] = total.astype(BF16)

    await_slots(first_all, sems.at[8, 1])
    for index, lanes in chunks:
        for lag in range(TAPS):
            taps_grad_ref[0, lag : lag + 1, lanes] = first_all[lag * len(chunks) + index]
        gain_grad_ref[:, lanes] = first_all[TAPS * len(chunks) + index]
    await_slots(owner_all, sems.at[10, 1])
    lane_ids = lax.broadcasted_iota(jnp.int32, (16, LANES), 1)
    row_ids = lax.broadcasted_iota(jnp.int32, (16, LANES), 0)
    for index, lanes in chunks:
        owned = owner_all[pl.ds(16 * index, 16)].reshape(16, LANES)
        owned = pltpu.roll(owned, 0, 1, stride=GROUP, stride_axis=0)
        for place in range(2 * TAPS):
            turned = pltpu.roll(owned, (LANES - GROUP * place) % LANES, 1) if place else owned
            value = jnp.where(lane_ids // GROUP == row_ids, turned, 0.0)
            taps_grad_ref[1 + place // TAPS, pl.ds(place % TAPS, 1), lanes] = jnp.sum(
                value, axis=0, keepdims=True
            )
    stores = [
        pltpu.make_async_copy(feature_grad_ref.at[0], feature_grad_hbm.at[0], store_sems.at[1]),
        pltpu.make_async_copy(taps_grad_ref, taps_grad_hbm, store_sems.at[2]),
        pltpu.make_async_copy(gain_grad_ref, gain_grad_hbm, store_sems.at[3]),
    ]
    for store in stores:
        store.start()

    await_slots(out_recv, sems.at[9, 1])
    for place, (target, hbm) in enumerate(
        (
            (filter_grad_ref, filter_grad_hbm),
            (feature_grad_ref.at[1], feature_grad_hbm.at[1]),
            (feature_grad_ref.at[2], feature_grad_hbm.at[2]),
        )
    ):
        for index, lanes in chunks:
            target[:, lanes] = from_pieces(out_recv[pl.ds(16 * index, 16), place]).astype(BF16)
        store = pltpu.make_async_copy(target, hbm, store_sems.at[4 + place])
        store.start()
        stores.append(store)

    for ref, number in (
        (filt_recv, 0),
        (pair_recv, 1),
        (conv_recv, 3),
        (row_recv.at[pl.ds(0, 7)], 4),
        (back_recv, 5),
        (part_recv, 7),
        (first_all, 8),
        (out_recv, 9),
        (owner_all, 10),
    ):
        await_slots(ref, sems.at[number, 0])
    taps_copy.wait_send()
    store_normed.wait()
    for store in stores:
        store.wait()
    remote(last, before_recv, sems.at[2], following).wait_send()
    remote(after_send, after_recv, sems.at[6], preceding).wait_send()


def hand_on_kernel(*refs):
    copies = [pltpu.make_async_copy(refs[i], refs[5 + i], refs[10].at[i]) for i in range(5)]
    for copy in copies:
        copy.start()
    for copy in copies:
        copy.wait()


def per_device(features, short_taps, long_filter, gain, out_grad):
    seq_rows, width = long_filter.shape
    blocks = lax.axis_size("ctx")
    pieces = (blocks, GROUP, LANES)
    flat = (blocks * GROUP, LANES)
    padded = (GROUP, 2 * blocks, LANES)
    row = (1, LANES)
    exchanged = [pltpu.VMEM(pieces, BF16)] * 2
    pairs = [pltpu.VMEM((blocks, 2, GROUP, LANES), BF16)] * 2
    triples = [pltpu.VMEM((blocks, 3, GROUP, LANES), BF16)] * 2
    outs = [
        jax.ShapeDtypeStruct((seq_rows, width), BF16),
        jax.ShapeDtypeStruct((3, seq_rows, width), BF16),
        jax.ShapeDtypeStruct((seq_rows, width), BF16),
        jax.ShapeDtypeStruct((3, TAPS, width), F32),
        jax.ShapeDtypeStruct((1, width), F32),
    ]
    results = pl.pallas_call(
        block_kernel,
        out_shape=outs,
        in_specs=[HBM] * 5,
        out_specs=[HBM] * 5,
        scratch_shapes=[pltpu.VMEM(out.shape, out.dtype) for out in outs]
        + [
            pltpu.VMEM((3, seq_rows, width), BF16),
            pltpu.VMEM(short_taps.shape, F32),
            pltpu.VMEM((seq_rows, width), BF16),
            pltpu.VMEM((1, width), F32),
            pltpu.VMEM((seq_rows, width), BF16),
        ]
        + exchanged
        + pairs
        + exchanged
        + exchanged
        + triples
        + [pltpu.VMEM((16, width), BF16)] * 3
        + [
            pltpu.VMEM((8, LANES), F32),
            pltpu.VMEM((8, 8, LANES), F32),
            pltpu.VMEM((blocks // 2,) + row, F32),
            pltpu.VMEM((blocks,) + row, F32),
            pltpu.VMEM(row, F32),
            pltpu.VMEM((blocks // 2,) + row, F32),
            pltpu.VMEM(row, F32),
            pltpu.VMEM((blocks,) + row, F32),
            pltpu.VMEM((width, LANES), F32),
            pltpu.VMEM((GROUP, LANES), F32),
            pltpu.VMEM((seq_rows + 8, width), F32),
            pltpu.VMEM((seq_rows, width), F32),
            pltpu.VMEM((seq_rows, width), F32),
            pltpu.VMEM(((blocks + 2) * GROUP, LANES), F32),
        ]
        + [pltpu.VMEM(flat, F32)] * 4
        + [pltpu.VMEM(padded, F32)] * 3
        + [pltpu.VMEM((GROUP, blocks * LANES, LANES), BF16)]
        + [pltpu.SemaphoreType.DMA((12, 2)), pltpu.SemaphoreType.DMA((5,)), pltpu.SemaphoreType.DMA((7,))],
        compiler_params=pltpu.CompilerParams(
            collective_id=0, has_side_effects=True, vmem_limit_bytes=60 << 20
        ),
    )(features, short_taps, long_filter, gain[None, :], out_grad)
    normed, feature_grad, filter_grad, taps_grad, gain_grad = pl.pallas_call(
        hand_on_kernel,
        out_shape=outs,
        in_specs=[HBM] * 5,
        out_specs=[HBM] * 5,
        scratch_shapes=[pltpu.SemaphoreType.DMA((5,))],
    )(*results)
    return (normed, feature_grad, filter_grad, taps_grad, gain_grad[0])


def solution(mesh):
    return jax.shard_map(
        per_device,
        mesh=mesh,
        in_specs=(
            P(None, "ctx", "tp"),
            P(None, None, "tp"),
            P("ctx", "tp"),
            P("tp"),
            P("ctx", "tp"),
        ),
        out_specs=(
            P("ctx", "tp"),
            P(None, "ctx", "tp"),
            P("ctx", "tp"),
            P(None, None, "tp"),
            P("tp"),
        ),
        check_vma=False,
    )
```

```python
import functools

import jax
import jax.numpy as jnp
from jax import lax
from jax.experimental import pallas as pl
from jax.experimental.pallas import tpu as pltpu
from jax.sharding import PartitionSpec as P

F32 = jnp.float32
BF16 = jnp.bfloat16
MESH = pl.DeviceIdType.MESH
norm_eps = 1e-06

TAPS = 7
LANES = 128
GROUP = 8
HBM = pl.BlockSpec(memory_space=pltpu.HBM)


def lane_chunks(width):
    return [slice(start, start + LANES) for start in range(0, width, LANES)]


def each_partner(me, visit):
    def one(step, carry):
        visit((me + step) % 64)
        return carry

    lax.fori_loop(0, 64, one, 0)


def each_of_half(me, visit):
    row, half, col = me // 16, (me // 8) % 2, me % 8

    def one(step, carry):
        visit(((row + step // 8) % 4) * 16 + half * 8 + (col + step % 8) % 8)
        return carry

    lax.fori_loop(0, 32, one, 0)


def remote(source, target, sems, device):
    return pltpu.make_async_remote_copy(
        src_ref=source,
        dst_ref=target,
        send_sem=sems.at[0],
        recv_sem=sems.at[1],
        device_id=device,
        device_id_type=MESH,
    )


def start_exchange(me, across, source, target, sems):
    def visit(partner):
        remote(source.at[partner], target.at[me], sems, {"ctx": partner, "tp": across}).start()

    each_partner(me, visit)


def start_gather(me, across, piece, target, sems):
    def visit(partner):
        remote(piece, target.at[me], sems, {"ctx": partner, "tp": across}).start()

    each_partner(me, visit)


def await_slots(ref, sem):
    pltpu.make_async_copy(ref, ref, sem).wait()


def toeplitz_rows(current, other, first, backward):
    rows = lax.broadcasted_iota(jnp.int32, (16, LANES), 0) + first
    lanes = lax.broadcasted_iota(jnp.int32, (16, LANES), 1)
    current = jnp.broadcast_to(current, (16, LANES))
    other = jnp.broadcast_to(other, (16, LANES))
    if backward:
        mixed = jnp.where(lanes >= LANES - 1 - rows, current, other)
        return pltpu.roll(mixed, first + 1, 1, stride=1, stride_axis=0)
    mixed = jnp.where(lanes < LANES - rows, current, other)
    return pltpu.roll(mixed, first, 1, stride=1, stride_axis=0)


def fill_padded(pad, work, mirrored):
    blocks = pad.shape[1] // 2
    if mirrored:
        spots = lax.broadcasted_iota(jnp.int32, (LANES, LANES), 0) + lax.broadcasted_iota(
            jnp.int32, (LANES, LANES), 1
        )
        mirror = jnp.where(spots == LANES - 1, 1.0, 0.0).astype(BF16)
    for chan in range(GROUP):
        rows = work[pl.ds(chan, blocks, stride=GROUP), :]
        if mirrored:
            rows = jnp.dot(rows.astype(BF16), mirror, preferred_element_type=F32)
        pad[chan, pl.ds(0, blocks), :] = jnp.zeros((blocks, LANES), F32)
        pad[chan, pl.ds(blocks, blocks), :] = rows


def fill_windows(windows, pieces):
    blocks = pieces.shape[0]
    rows = blocks * GROUP
    edge = jnp.zeros((GROUP, LANES), F32)
    windows[pl.ds(0, GROUP), :] = edge
    windows[pl.ds(rows + GROUP, GROUP), :] = edge
    windows[pl.ds(GROUP, rows), :] = pieces[...].astype(F32).reshape(rows, LANES)


def toeplitz_block(windows, chan, lag, backward):
    base = pl.multiple_of((lag + 1) * GROUP, GROUP) + chan
    current = windows[pl.ds(base, 1), :]
    other = windows[pl.ds(base + (GROUP if backward else -GROUP), 1), :]
    return [
        toeplitz_rows(current, other, first, backward).astype(BF16) for first in range(0, LANES, 16)
    ]


def build_toeplitz(windows, toeplitz):
    blocks = toeplitz.shape[1] // LANES

    def channel(chan, carry):
        def lags(lag, inner):
            rows = toeplitz_block(windows, chan, lag, False)
            for i, part in enumerate(rows):
                toeplitz[chan, pl.ds(pl.multiple_of(lag * LANES, LANES) + 16 * i, 16), :] = part
            return inner

        return lax.fori_loop(0, blocks, lags, carry, unroll=16)

    lax.fori_loop(0, GROUP, channel, 0)


def causal_products(toeplitz, padded, flat):
    blocks = padded.shape[1] // 2

    def channel(chan, carry):
        def two_lags(pair, total):
            left = [padded[chan, pl.ds(blocks - 2 * pair - i, blocks), :] for i in range(2)]
            right = toeplitz[chan, pl.ds(pl.multiple_of(pair * 2 * LANES, 2 * LANES), 2 * LANES), :]
            return total + jnp.dot(
                jnp.concatenate(left, axis=1).astype(BF16), right, preferred_element_type=F32
            )

        total = lax.fori_loop(
            0, blocks // 2, two_lags, jnp.zeros((blocks, LANES), F32), unroll=blocks // 2
        )
        flat[pl.ds(chan, blocks, stride=GROUP), :] = total
        return carry

    lax.fori_loop(0, GROUP, channel, 0)


def lagged_products(windows, padded, flat):
    count = len(padded)
    blocks = padded[0].shape[1] // 2

    def channel(chan, carry):
        def two_lags(pair, total):
            left, right = [], []
            for lag in (2 * pair, 2 * pair + 1):
                right += toeplitz_block(windows, chan, lag, True)
                left.append(
                    jnp.concatenate([pad[chan, pl.ds(lag + 1, blocks), :] for pad in padded], axis=0)
                )
            return total + jnp.dot(
                jnp.concatenate(left, axis=1).astype(BF16),
                jnp.concatenate(right, axis=0),
                preferred_element_type=F32,
            )

        total = lax.fori_loop(
            0, blocks // 2, two_lags, jnp.zeros((count * blocks, LANES), F32), unroll=blocks // 2
        )
        for i, work in enumerate(flat):
            work[pl.ds(chan, blocks, stride=GROUP), :] = total[i * blocks : (i + 1) * blocks]
        return carry

    lax.fori_loop(0, GROUP, channel, 0)


def to_pieces(block):
    return block.T.reshape(16, GROUP, LANES).astype(BF16)


def from_pieces(pieces):
    return pieces.astype(F32).reshape(LANES, LANES).T


def owner_taps(taps, stream):
    return [
        jnp.broadcast_to(taps[:, stream * TAPS + lag : stream * TAPS + lag + 1], (GROUP, LANES))
        for lag in range(TAPS)
    ]


def owner_short(raw, which, taps, target):
    lanes = lax.broadcasted_iota(jnp.int32, (GROUP, LANES), 1)

    def block(index, before):
        now = raw[index, which].astype(F32)
        total = taps[0] * now
        after = []
        for lag in range(1, TAPS):
            turned = pltpu.roll(now, lag, 1)
            total = total + taps[lag] * jnp.where(lanes >= lag, turned, before[lag - 1])
            after.append(turned)
        target[pl.ds(pl.multiple_of(index * GROUP, GROUP), GROUP), :] = total.astype(BF16).astype(F32)
        return tuple(after)

    zero = jnp.zeros((GROUP, LANES), F32)
    lax.fori_loop(0, raw.shape[0], block, (zero,) * (TAPS - 1), unroll=8)


def owner_back(raw, which, taps, grad_flat, partner_flat, target, slot):
    lanes = lax.broadcasted_iota(jnp.int32, (GROUP, LANES), 1)
    blocks = raw.shape[0]

    def block(step, carry):
        after, sums = carry
        index = blocks - 1 - step
        grad = grad_flat[pl.ds(pl.multiple_of(step * GROUP, GROUP), GROUP), :].astype(BF16).astype(F32)
        rows = pl.ds(pl.multiple_of(index * GROUP, GROUP), GROUP)
        grad = (grad * partner_flat[rows, :]).astype(BF16).astype(F32)
        value = raw[index, which].astype(F32)
        total = taps[0] * grad
        new_sums = [sums[0] + value * grad]
        new_after = []
        for lag in range(1, TAPS):
            turned = pltpu.roll(grad, LANES - lag, 1)
            moved = jnp.where(lanes < LANES - lag, turned, after[lag - 1])
            total = total + taps[lag] * moved
            new_sums.append(sums[lag] + value * moved)
            new_after.append(turned)
        target[index, slot] = total.astype(BF16)
        return tuple(new_after), tuple(new_sums)

    zero = jnp.zeros((GROUP, LANES), F32)
    _, sums = lax.fori_loop(
        0, blocks, block, ((zero,) * (TAPS - 1), (zero,) * TAPS), unroll=8
    )
    return sums


def block_kernel(
    features_hbm,
    taps_hbm,
    filter_hbm,
    gain_hbm,
    grad_hbm,
    normed_hbm,
    feature_grad_hbm,
    filter_grad_hbm,
    taps_grad_hbm,
    gain_grad_hbm,
    normed_ref,
    feature_grad_ref,
    filter_grad_ref,
    taps_grad_ref,
    gain_grad_ref,
    features_ref,
    taps_ref,
    filter_ref,
    gain_ref,
    grad_ref,
    filt_send,
    filt_recv,
    pair_send,
    pair_recv,
    conv_send,
    conv_recv,
    back_send,
    back_recv,
    lag_send,
    lag_recv,
    out_send,
    out_recv,
    before_recv,
    after_send,
    after_recv,
    row_send,
    row_recv,
    part_send,
    part_recv,
    part_sum,
    first_all,
    owner_sum,
    owner_all,
    taps_turned,
    taps_recv,
    pad,
    q_short,
    conv,
    windows,
    k_short,
    v_short,
    flat_a,
    flat_b,
    pad_fwd,
    pad_filt,
    pad_prod,
    toeplitz,
    sems,
    load_sems,
    store_sems,
):
    me = lax.axis_index("ctx")
    rank = lax.axis_index("tp")
    across = (rank + 4) % 8
    width = filter_ref.shape[1]
    chunks = list(enumerate(lane_chunks(width)))
    blocks = filt_recv.shape[0]
    rows = blocks * GROUP
    channels = width * 8
    following = {"ctx": (me + 1) % 64}
    preceding = {"ctx": (me + 63) % 64}

    barrier = pltpu.get_barrier_semaphore()

    def greet(partner):
        pl.semaphore_signal(
            barrier, inc=1, device_id={"ctx": partner, "tp": across}, device_id_type=MESH
        )

    for device in (following, preceding):
        pl.semaphore_signal(barrier, inc=1, device_id=device, device_id_type=MESH)
    for step in range(1, 8):
        pl.semaphore_signal(
            barrier, inc=1, device_id={"tp": (rank + step) % 8}, device_id_type=MESH
        )
    each_partner(me, greet)
    loads = [
        pltpu.make_async_copy(source, target, load_sems.at[i])
        for i, (source, target) in enumerate(
            (
                (filter_hbm, filter_ref),
                (features_hbm, features_ref),
                (taps_hbm, taps_ref),
                (gain_hbm, gain_ref),
                (grad_hbm, grad_ref),
            )
        )
    ]
    for load in loads:
        load.start()
    for load in loads:
        load.wait()

    for index, lanes in chunks:
        spot = pl.ds(16 * index, 16)
        filt_send[spot] = to_pieces(filter_ref[:, lanes].astype(F32))
        pair_send[spot, 0] = to_pieces(features_ref[1, :, lanes].astype(F32))
        pair_send[spot, 1] = to_pieces(features_ref[2, :, lanes].astype(F32))
    filler = jnp.zeros((LANES - 3 * TAPS, LANES), F32)
    for index, lanes in chunks:
        stack = jnp.concatenate([taps_ref[i, :, lanes] for i in range(3)] + [filler], axis=0)
        taps_turned[pl.ds(LANES * index, LANES), :] = stack.T
    pl.semaphore_wait(barrier, 73)
    start_exchange(me, across, filt_send, filt_recv, sems.at[0])
    start_exchange(me, across, pair_send, pair_recv, sems.at[1])
    own_taps = taps_turned.at[pl.ds(pl.multiple_of(me * GROUP, GROUP), GROUP)]
    taps_copy = remote(own_taps, taps_recv, sems.at[11], {"tp": across})
    taps_copy.start()
    last = features_ref.at[0, pl.ds(LANES - 16, 16)]
    remote(last, before_recv, sems.at[2], following).start()

    remote(last, before_recv, sems.at[2], following).wait_recv()
    pad[pl.ds(0, 8), :] = jnp.where(me > 0, before_recv[...].astype(F32)[8:, :], 0.0)
    pad[pl.ds(8, LANES), :] = features_ref[0].astype(F32)
    for _, lanes in chunks:
        for top in (0, 64):
            running = jnp.zeros((64, LANES), F32)
            for lag in range(TAPS):
                running = running + taps_ref[0, lag : lag + 1, lanes] * pad[
                    pl.ds(8 - lag + top, 64), lanes
                ]
            q_short[pl.ds(top, 64), lanes] = running.astype(BF16).astype(F32)

    await_slots(filt_recv, sems.at[0, 1])
    fill_windows(windows, filt_recv)
    build_toeplitz(windows, toeplitz)
    flat_a[...] = filt_recv[...].astype(F32).reshape(rows, LANES)
    fill_padded(pad_filt, flat_a, True)
    taps_copy.wait_recv()
    await_slots(pair_recv, sems.at[1, 1])
    turned = taps_recv[...]
    k_taps, v_taps = owner_taps(turned, 1), owner_taps(turned, 2)
    owner_short(pair_recv, 0, k_taps, k_short)
    owner_short(pair_recv, 1, v_taps, v_short)
    flat_b[...] = (k_short[...] * v_short[...]).astype(BF16).astype(F32)
    fill_padded(pad_fwd, flat_b, False)
    causal_products(toeplitz, pad_fwd, flat_a)
    conv_send[...] = flat_a[...].reshape(blocks, GROUP, LANES).astype(BF16)
    start_exchange(me, across, conv_send, conv_recv, sems.at[3])
    fill_padded(pad_prod, flat_b, True)
    await_slots(conv_recv, sems.at[3, 1])

    squares = jnp.zeros((LANES, LANES), F32)
    tilts = jnp.zeros((LANES, LANES), F32)
    for index, lanes in chunks:
        value = from_pieces(conv_recv[pl.ds(16 * index, 16)])
        conv[:, lanes] = value
        gated = q_short[:, lanes] * value
        squares = squares + gated * gated
        tilts = tilts + gain_ref[:, lanes] * grad_ref[:, lanes].astype(F32) * gated
    row_send[...] = jnp.zeros(row_send.shape, F32)
    row_send[pl.ds(0, 1), :] = jnp.sum(squares.T, axis=0, keepdims=True)
    row_send[pl.ds(1, 1), :] = jnp.sum(tilts.T, axis=0, keepdims=True)
    for step in range(1, 8):
        remote(row_send, row_recv.at[rank], sems.at[4], {"tp": (rank + step) % 8}).start()
    row_recv[pl.ds(rank, 1)] = row_send[...][None]
    await_slots(row_recv.at[pl.ds(0, 7)], sems.at[4, 1])
    sums = jnp.sum(row_recv[...], axis=0)
    scale = lax.rsqrt(sums[0:1] / channels + norm_eps)
    bend = scale**3 * sums[1:2] / channels
    scale = jnp.broadcast_to(scale, (LANES, LANES)).T
    bend = jnp.broadcast_to(bend, (LANES, LANES)).T

    def gate(lanes):
        value, q_value = conv[:, lanes], q_short[:, lanes]
        gain = gain_ref[:, lanes]
        upstream = grad_ref[:, lanes].astype(F32)
        gated = q_value * value
        grad_gated = scale * (gain * upstream) - gated * bend
        return value, q_value, gain, upstream, gated, grad_gated

    for index, lanes in chunks:
        _, q_value, _, _, _, grad_gated = gate(lanes)
        back_send[pl.ds(16 * index, 16)] = to_pieces(grad_gated * q_value)
    start_exchange(me, across, back_send, back_recv, sems.at[5])

    for index, lanes in chunks:
        value, _, gain, upstream, gated, grad_gated = gate(lanes)
        normed_ref[:, lanes] = (gated * scale * gain).astype(BF16)
        part_send[7 * 4 + index] = jnp.sum(upstream * gated * scale, axis=0, keepdims=True)
        first = (grad_gated * value).astype(BF16)
        after_send[:, lanes] = first[:16]
        first = first.astype(F32)
        conv[:, lanes] = first
        for lag in range(TAPS):
            part_send[lag * 4 + index] = jnp.sum(
                first * pad[pl.ds(8 - lag, LANES), lanes], axis=0, keepdims=True
            )
    remote(after_send, after_recv, sems.at[6], preceding).start()
    store_normed = pltpu.make_async_copy(normed_ref, normed_hbm, store_sems.at[0])
    store_normed.start()

    def send_part(partner):
        place = (partner // 16) * 8 + partner % 8
        remote(
            part_send.at[place], part_recv.at[me], sems.at[7], {"ctx": partner, "tp": across}
        ).start()

    each_partner(me, send_part)
    await_slots(part_recv, sems.at[7, 1])
    part_sum[...] = jnp.sum(part_recv[...], axis=0)
    mine = (me // 16) * 8 + me % 8

    def send_total(partner):
        remote(part_sum, first_all.at[mine], sems.at[8], {"ctx": partner, "tp": across}).start()

    each_of_half(me, send_total)

    await_slots(back_recv, sems.at[5, 1])
    fill_windows(windows, back_recv)
    lagged_products(windows, [pad_filt, pad_prod], [flat_a, flat_b])

    def place_filter(index, carry):
        step = pl.multiple_of((blocks - 1 - index) * GROUP, GROUP)
        lag_send[index] = flat_b[pl.ds(step, GROUP), :].astype(BF16)
        return carry

    lax.fori_loop(0, blocks, place_filter, 0, unroll=8)
    start_exchange(me, across, lag_send, lag_recv, sems.at[12])
    k_sums = owner_back(pair_recv, 0, k_taps, flat_a, v_short, out_send, 0)
    v_sums = owner_back(pair_recv, 1, v_taps, flat_a, k_short, out_send, 1)
    start_exchange(me, across, out_send, out_recv, sems.at[9])
    lane_ids = lax.broadcasted_iota(jnp.int32, (GROUP, LANES), 1)
    chan_ids = lax.broadcasted_iota(jnp.int32, (GROUP, LANES), 0)
    packed = jnp.zeros((GROUP, LANES), F32)
    for place, value in enumerate(k_sums + v_sums):
        total = jnp.sum(value, axis=1, keepdims=True)
        packed = packed + jnp.where(lane_ids == place * GROUP + chan_ids, total, 0.0)
    owner_sum[...] = jnp.sum(packed, axis=0, keepdims=True)
    start_gather(me, across, owner_sum, owner_all, sems.at[10])

    remote(after_send, after_recv, sems.at[6], preceding).wait_recv()
    pad[pl.ds(0, LANES), :] = conv[...]
    pad[pl.ds(LANES, 8), :] = jnp.where(me < 63, after_recv[...].astype(F32)[:8, :], 0.0)
    for _, lanes in chunks:
        for top in (0, 64):
            total = jnp.zeros((64, LANES), F32)
            for lag in range(TAPS):
                total = total + taps_ref[0, lag : lag + 1, lanes] * pad[pl.ds(lag + top, 64), lanes]
            feature_grad_ref[0, pl.ds(top, 64), lanes] = total.astype(BF16)

    await_slots(first_all, sems.at[8, 1])
    for index, lanes in chunks:
        for lag in range(TAPS):
            taps_grad_ref[0, lag : lag + 1, lanes] = first_all[lag * len(chunks) + index]
        gain_grad_ref[:, lanes] = first_all[TAPS * len(chunks) + index]
    await_slots(owner_all, sems.at[10, 1])
    lane_ids = lax.broadcasted_iota(jnp.int32, (16, LANES), 1)
    row_ids = lax.broadcasted_iota(jnp.int32, (16, LANES), 0)
    for index, lanes in chunks:
        owned = owner_all[pl.ds(16 * index, 16)].reshape(16, LANES)
        owned = pltpu.roll(owned, 0, 1, stride=GROUP, stride_axis=0)
        for place in range(2 * TAPS):
            turned = pltpu.roll(owned, (LANES - GROUP * place) % LANES, 1) if place else owned
            value = jnp.where(lane_ids // GROUP == row_ids, turned, 0.0)
            taps_grad_ref[1 + place // TAPS, pl.ds(place % TAPS, 1), lanes] = jnp.sum(
                value, axis=0, keepdims=True
            )
    stores = [
        pltpu.make_async_copy(feature_grad_ref.at[0], feature_grad_hbm.at[0], store_sems.at[1]),
        pltpu.make_async_copy(taps_grad_ref, taps_grad_hbm, store_sems.at[2]),
        pltpu.make_async_copy(gain_grad_ref, gain_grad_hbm, store_sems.at[3]),
    ]
    for store in stores:
        store.start()

    def finish(pieces, target, hbm, number):
        for index, lanes in chunks:
            target[:, lanes] = from_pieces(pieces(pl.ds(16 * index, 16))).astype(BF16)
        store = pltpu.make_async_copy(target, hbm, store_sems.at[number])
        store.start()
        stores.append(store)

    await_slots(lag_recv, sems.at[12, 1])
    finish(lambda spot: lag_recv[spot], filter_grad_ref, filter_grad_hbm, 4)
    await_slots(out_recv, sems.at[9, 1])
    for stream in (1, 2):
        finish(
            lambda spot, stream=stream: out_recv[spot, stream - 1],
            feature_grad_ref.at[stream],
            feature_grad_hbm.at[stream],
            4 + stream,
        )

    for ref, number in (
        (filt_recv, 0),
        (pair_recv, 1),
        (conv_recv, 3),
        (row_recv.at[pl.ds(0, 7)], 4),
        (back_recv, 5),
        (part_recv, 7),
        (first_all, 8),
        (out_recv, 9),
        (lag_recv, 12),
        (owner_all, 10),
    ):
        await_slots(ref, sems.at[number, 0])
    taps_copy.wait_send()
    store_normed.wait()
    for store in stores:
        store.wait()
    remote(last, before_recv, sems.at[2], following).wait_send()
    remote(after_send, after_recv, sems.at[6], preceding).wait_send()


def hand_on_kernel(*refs):
    sources, targets, stages = refs[:5], refs[5:10], refs[10:15]
    load_sems, store_sems = refs[15:]
    loads = [pltpu.make_async_copy(sources[i], stages[i], load_sems.at[i]) for i in range(5)]
    stores = [pltpu.make_async_copy(stages[i], targets[i], store_sems.at[i]) for i in range(5)]
    for load in loads:
        load.start()
    for load, store in zip(loads, stores):
        load.wait()
        store.start()
    for store in stores:
        store.wait()


def per_device(features, short_taps, long_filter, gain, out_grad):
    seq_rows, width = long_filter.shape
    blocks = lax.axis_size("ctx")
    pieces = (blocks, GROUP, LANES)
    flat = (blocks * GROUP, LANES)
    padded = (GROUP, 2 * blocks, LANES)
    row = (1, LANES)
    exchanged = [pltpu.VMEM(pieces, BF16)] * 2
    pairs = [pltpu.VMEM((blocks, 2, GROUP, LANES), BF16)] * 2
    outs = [
        jax.ShapeDtypeStruct((seq_rows, width), BF16),
        jax.ShapeDtypeStruct((3, seq_rows, width), BF16),
        jax.ShapeDtypeStruct((seq_rows, width), BF16),
        jax.ShapeDtypeStruct((3, TAPS, width), F32),
        jax.ShapeDtypeStruct((1, width), F32),
    ]
    results = pl.pallas_call(
        block_kernel,
        out_shape=outs,
        in_specs=[HBM] * 5,
        out_specs=[HBM] * 5,
        scratch_shapes=[pltpu.VMEM(out.shape, out.dtype) for out in outs]
        + [
            pltpu.VMEM((3, seq_rows, width), BF16),
            pltpu.VMEM(short_taps.shape, F32),
            pltpu.VMEM((seq_rows, width), BF16),
            pltpu.VMEM((1, width), F32),
            pltpu.VMEM((seq_rows, width), BF16),
        ]
        + exchanged
        + pairs
        + exchanged
        + exchanged
        + exchanged
        + pairs
        + [pltpu.VMEM((16, width), BF16)] * 3
        + [
            pltpu.VMEM((8, LANES), F32),
            pltpu.VMEM((8, 8, LANES), F32),
            pltpu.VMEM((blocks // 2,) + row, F32),
            pltpu.VMEM((blocks,) + row, F32),
            pltpu.VMEM(row, F32),
            pltpu.VMEM((blocks // 2,) + row, F32),
            pltpu.VMEM(row, F32),
            pltpu.VMEM((blocks,) + row, F32),
            pltpu.VMEM((width, LANES), F32),
            pltpu.VMEM((GROUP, LANES), F32),
            pltpu.VMEM((seq_rows + 8, width), F32),
            pltpu.VMEM((seq_rows, width), F32),
            pltpu.VMEM((seq_rows, width), F32),
            pltpu.VMEM(((blocks + 2) * GROUP, LANES), F32),
        ]
        + [pltpu.VMEM(flat, F32)] * 4
        + [pltpu.VMEM(padded, F32)] * 3
        + [pltpu.VMEM((GROUP, blocks * LANES, LANES), BF16)]
        + [pltpu.SemaphoreType.DMA((13, 2)), pltpu.SemaphoreType.DMA((5,)), pltpu.SemaphoreType.DMA((7,))],
        compiler_params=pltpu.CompilerParams(
            collective_id=0, has_side_effects=True, vmem_limit_bytes=60 << 20
        ),
    )(features, short_taps, long_filter, gain[None, :], out_grad)
    normed, feature_grad, filter_grad, taps_grad, gain_grad = pl.pallas_call(
        hand_on_kernel,
        out_shape=outs,
        in_specs=[HBM] * 5,
        out_specs=[HBM] * 5,
        scratch_shapes=[pltpu.VMEM(out.shape, out.dtype) for out in outs]
        + [pltpu.SemaphoreType.DMA((5,))] * 2,
        compiler_params=pltpu.CompilerParams(vmem_limit_bytes=60 << 20),
    )(*results)
    return (normed, feature_grad, filter_grad, taps_grad, gain_grad[0])


def solution(mesh):
    return jax.shard_map(
        per_device,
        mesh=mesh,
        in_specs=(
            P(None, "ctx", "tp"),
            P(None, None, "tp"),
            P("ctx", "tp"),
            P("tp"),
            P("ctx", "tp"),
        ),
        out_specs=(
            P("ctx", "tp"),
            P(None, "ctx", "tp"),
            P("ctx", "tp"),
            P(None, None, "tp"),
            P("tp"),
        ),
        check_vma=False,
    )
```

```python
import functools

import jax
import jax.numpy as jnp
from jax import lax
from jax.experimental import pallas as pl
from jax.experimental.pallas import tpu as pltpu
from jax.sharding import PartitionSpec as P

F32 = jnp.float32
BF16 = jnp.bfloat16
MESH = pl.DeviceIdType.MESH
norm_eps = 1e-06

TAPS = 7
LANES = 128
GROUP = 8
HBM = pl.BlockSpec(memory_space=pltpu.HBM)


def lane_chunks(width):
    return [slice(start, start + LANES) for start in range(0, width, LANES)]


def each_partner(me, visit):
    def one(step, carry):
        visit((me + step) % 64)
        return carry

    lax.fori_loop(0, 64, one, 0)


def each_of_half(me, visit):
    row, half, col = me // 16, (me // 8) % 2, me % 8

    def one(step, carry):
        visit(((row + step // 8) % 4) * 16 + half * 8 + (col + step % 8) % 8)
        return carry

    lax.fori_loop(0, 32, one, 0)


def remote(source, target, sems, device):
    return pltpu.make_async_remote_copy(
        src_ref=source,
        dst_ref=target,
        send_sem=sems.at[0],
        recv_sem=sems.at[1],
        device_id=device,
        device_id_type=MESH,
    )


def start_exchange(me, across, source, target, sems):
    def visit(partner):
        remote(source.at[partner], target.at[me], sems, {"ctx": partner, "tp": across}).start()

    each_partner(me, visit)


def start_gather(me, across, piece, target, sems):
    def visit(partner):
        remote(piece, target.at[me], sems, {"ctx": partner, "tp": across}).start()

    each_partner(me, visit)


def await_slots(ref, sem):
    pltpu.make_async_copy(ref, ref, sem).wait()


def toeplitz_rows(current, other, first, backward):
    rows = lax.broadcasted_iota(jnp.int32, (16, LANES), 0) + first
    lanes = lax.broadcasted_iota(jnp.int32, (16, LANES), 1)
    current = jnp.broadcast_to(current, (16, LANES))
    other = jnp.broadcast_to(other, (16, LANES))
    if backward:
        mixed = jnp.where(lanes >= LANES - 1 - rows, current, other)
        return pltpu.roll(mixed, first + 1, 1, stride=1, stride_axis=0)
    mixed = jnp.where(lanes < LANES - rows, current, other)
    return pltpu.roll(mixed, first, 1, stride=1, stride_axis=0)


def fill_padded(pad, work, mirrored):
    blocks = pad.shape[1] // 2
    if mirrored:
        spots = lax.broadcasted_iota(jnp.int32, (LANES, LANES), 0) + lax.broadcasted_iota(
            jnp.int32, (LANES, LANES), 1
        )
        mirror = jnp.where(spots == LANES - 1, 1.0, 0.0).astype(BF16)
    for chan in range(GROUP):
        rows = work[pl.ds(chan, blocks, stride=GROUP), :]
        if mirrored:
            rows = jnp.dot(rows.astype(BF16), mirror, preferred_element_type=F32)
        pad[chan, pl.ds(0, blocks), :] = jnp.zeros((blocks, LANES), F32)
        pad[chan, pl.ds(blocks, blocks), :] = rows


def fill_windows(windows, pieces):
    blocks = pieces.shape[0]
    rows = blocks * GROUP
    edge = jnp.zeros((GROUP, LANES), F32)
    windows[pl.ds(0, GROUP), :] = edge
    windows[pl.ds(rows + GROUP, GROUP), :] = edge
    windows[pl.ds(GROUP, rows), :] = pieces[...].astype(F32).reshape(rows, LANES)


def toeplitz_block(windows, chan, lag, backward):
    base = pl.multiple_of((lag + 1) * GROUP, GROUP) + chan
    current = windows[pl.ds(base, 1), :]
    other = windows[pl.ds(base + (GROUP if backward else -GROUP), 1), :]
    return [
        toeplitz_rows(current, other, first, backward).astype(BF16) for first in range(0, LANES, 16)
    ]


def build_toeplitz(windows, toeplitz):
    blocks = toeplitz.shape[1] // LANES

    def channel(chan, carry):
        def lags(lag, inner):
            rows = toeplitz_block(windows, chan, lag, False)
            for i, part in enumerate(rows):
                toeplitz[chan, pl.ds(pl.multiple_of(lag * LANES, LANES) + 16 * i, 16), :] = part
            return inner

        return lax.fori_loop(0, blocks, lags, carry, unroll=blocks)

    lax.fori_loop(0, GROUP, channel, 0)


def causal_products(toeplitz, padded, flat):
    blocks = padded.shape[1] // 2

    def channel(chan, carry):
        def two_lags(pair, total):
            left = [padded[chan, pl.ds(blocks - 2 * pair - i, blocks), :] for i in range(2)]
            right = toeplitz[chan, pl.ds(pl.multiple_of(pair * 2 * LANES, 2 * LANES), 2 * LANES), :]
            return total + jnp.dot(
                jnp.concatenate(left, axis=1).astype(BF16), right, preferred_element_type=F32
            )

        total = lax.fori_loop(
            0, blocks // 2, two_lags, jnp.zeros((blocks, LANES), F32), unroll=blocks // 2
        )
        flat[pl.ds(chan, blocks, stride=GROUP), :] = total
        return carry

    lax.fori_loop(0, GROUP, channel, 0, unroll=2)


def lagged_products(windows, padded, flat):
    count = len(padded)
    blocks = padded[0].shape[1] // 2

    def channel(chan, carry):
        def two_lags(pair, total):
            left, right = [], []
            for lag in (2 * pair, 2 * pair + 1):
                right += toeplitz_block(windows, chan, lag, True)
                left.append(
                    jnp.concatenate([pad[chan, pl.ds(lag + 1, blocks), :] for pad in padded], axis=0)
                )
            return total + jnp.dot(
                jnp.concatenate(left, axis=1).astype(BF16),
                jnp.concatenate(right, axis=0),
                preferred_element_type=F32,
            )

        total = lax.fori_loop(
            0, blocks // 2, two_lags, jnp.zeros((count * blocks, LANES), F32), unroll=blocks // 2
        )
        for i, work in enumerate(flat):
            work[pl.ds(chan, blocks, stride=GROUP), :] = total[i * blocks : (i + 1) * blocks]
        return carry

    lax.fori_loop(0, GROUP, channel, 0, unroll=2)


def to_pieces(block):
    return block.T.reshape(16, GROUP, LANES).astype(BF16)


def from_pieces(pieces):
    return pieces.astype(F32).reshape(LANES, LANES).T


def owner_taps(taps, stream):
    return [
        jnp.broadcast_to(taps[:, stream * TAPS + lag : stream * TAPS + lag + 1], (GROUP, LANES))
        for lag in range(TAPS)
    ]


def owner_short(raw, taps, target):
    lanes = lax.broadcasted_iota(jnp.int32, (GROUP, LANES), 1)

    def block(index, before):
        now = raw[index].astype(F32)
        total = taps[0] * now
        after = []
        for lag in range(1, TAPS):
            turned = pltpu.roll(now, lag, 1)
            total = total + taps[lag] * jnp.where(lanes >= lag, turned, before[lag - 1])
            after.append(turned)
        target[pl.ds(pl.multiple_of(index * GROUP, GROUP), GROUP), :] = total.astype(BF16).astype(F32)
        return tuple(after)

    zero = jnp.zeros((GROUP, LANES), F32)
    lax.fori_loop(0, raw.shape[0], block, (zero,) * (TAPS - 1), unroll=8)


def owner_back(raw, taps, grad_flat, partner_flat, target):
    lanes = lax.broadcasted_iota(jnp.int32, (GROUP, LANES), 1)
    blocks = raw.shape[0]

    def block(step, carry):
        after, sums = carry
        index = blocks - 1 - step
        grad = grad_flat[pl.ds(pl.multiple_of(step * GROUP, GROUP), GROUP), :].astype(BF16).astype(F32)
        rows = pl.ds(pl.multiple_of(index * GROUP, GROUP), GROUP)
        grad = (grad * partner_flat[rows, :]).astype(BF16).astype(F32)
        value = raw[index].astype(F32)
        total = taps[0] * grad
        new_sums = [sums[0] + value * grad]
        new_after = []
        for lag in range(1, TAPS):
            turned = pltpu.roll(grad, LANES - lag, 1)
            moved = jnp.where(lanes < LANES - lag, turned, after[lag - 1])
            total = total + taps[lag] * moved
            new_sums.append(sums[lag] + value * moved)
            new_after.append(turned)
        target[index] = total.astype(BF16)
        return tuple(new_after), tuple(new_sums)

    zero = jnp.zeros((GROUP, LANES), F32)
    _, sums = lax.fori_loop(
        0, blocks, block, ((zero,) * (TAPS - 1), (zero,) * TAPS), unroll=8
    )
    return sums


def block_kernel(
    features_hbm,
    taps_hbm,
    filter_hbm,
    gain_hbm,
    grad_hbm,
    normed_hbm,
    feature_grad_hbm,
    filter_grad_hbm,
    taps_grad_hbm,
    gain_grad_hbm,
    normed_ref,
    feature_grad_ref,
    filter_grad_ref,
    taps_grad_ref,
    gain_grad_ref,
    features_ref,
    taps_ref,
    filter_ref,
    gain_ref,
    grad_ref,
    filt_send,
    filt_recv,
    k_send,
    k_recv,
    v_send,
    v_recv,
    conv_send,
    conv_recv,
    back_send,
    back_recv,
    lag_send,
    lag_recv,
    k_back_send,
    k_back_recv,
    v_back_send,
    v_back_recv,
    before_recv,
    after_send,
    after_recv,
    row_send,
    row_recv,
    part_send,
    part_recv,
    part_sum,
    first_all,
    owner_sum,
    owner_all,
    taps_turned,
    taps_recv,
    pad,
    q_short,
    conv,
    windows,
    k_short,
    v_short,
    flat_a,
    flat_b,
    pad_fwd,
    pad_filt,
    pad_prod,
    toeplitz,
    sems,
    load_sems,
    store_sems,
):
    me = lax.axis_index("ctx")
    rank = lax.axis_index("tp")
    across = (rank + 4) % 8
    width = filter_ref.shape[1]
    chunks = list(enumerate(lane_chunks(width)))
    blocks = filt_recv.shape[0]
    rows = blocks * GROUP
    channels = width * 8
    following = {"ctx": (me + 1) % 64}
    preceding = {"ctx": (me + 63) % 64}

    barrier = pltpu.get_barrier_semaphore()

    def greet(partner):
        pl.semaphore_signal(
            barrier, inc=1, device_id={"ctx": partner, "tp": across}, device_id_type=MESH
        )

    for device in (following, preceding):
        pl.semaphore_signal(barrier, inc=1, device_id=device, device_id_type=MESH)
    for step in range(1, 8):
        pl.semaphore_signal(
            barrier, inc=1, device_id={"tp": (rank + step) % 8}, device_id_type=MESH
        )
    each_partner(me, greet)
    loads = [
        pltpu.make_async_copy(source, target, load_sems.at[i])
        for i, (source, target) in enumerate(
            (
                (filter_hbm, filter_ref),
                (features_hbm, features_ref),
                (taps_hbm, taps_ref),
                (gain_hbm, gain_ref),
                (grad_hbm, grad_ref),
            )
        )
    ]
    for load in loads:
        load.start()
    for load in loads:
        load.wait()

    for index, lanes in chunks:
        spot = pl.ds(16 * index, 16)
        filt_send[spot] = to_pieces(filter_ref[:, lanes].astype(F32))
        k_send[spot] = to_pieces(features_ref[1, :, lanes].astype(F32))
        v_send[spot] = to_pieces(features_ref[2, :, lanes].astype(F32))
    filler = jnp.zeros((LANES - 3 * TAPS, LANES), F32)
    for index, lanes in chunks:
        stack = jnp.concatenate([taps_ref[i, :, lanes] for i in range(3)] + [filler], axis=0)
        taps_turned[pl.ds(LANES * index, LANES), :] = stack.T
    pl.semaphore_wait(barrier, 73)
    start_exchange(me, across, filt_send, filt_recv, sems.at[0])
    own_taps = taps_turned.at[pl.ds(pl.multiple_of(me * GROUP, GROUP), GROUP)]
    taps_copy = remote(own_taps, taps_recv, sems.at[11], {"tp": across})
    taps_copy.start()
    last = features_ref.at[0, pl.ds(LANES - 16, 16)]
    remote(last, before_recv, sems.at[2], following).start()
    start_exchange(me, across, k_send, k_recv, sems.at[1])
    start_exchange(me, across, v_send, v_recv, sems.at[13])

    remote(last, before_recv, sems.at[2], following).wait_recv()
    pad[pl.ds(0, 8), :] = jnp.where(me > 0, before_recv[...].astype(F32)[8:, :], 0.0)
    pad[pl.ds(8, LANES), :] = features_ref[0].astype(F32)
    for _, lanes in chunks:
        for top in (0, 64):
            running = jnp.zeros((64, LANES), F32)
            for lag in range(TAPS):
                running = running + taps_ref[0, lag : lag + 1, lanes] * pad[
                    pl.ds(8 - lag + top, 64), lanes
                ]
            q_short[pl.ds(top, 64), lanes] = running.astype(BF16).astype(F32)

    await_slots(filt_recv, sems.at[0, 1])
    fill_windows(windows, filt_recv)
    build_toeplitz(windows, toeplitz)
    flat_a[...] = filt_recv[...].astype(F32).reshape(rows, LANES)
    fill_padded(pad_filt, flat_a, True)
    taps_copy.wait_recv()
    turned = taps_recv[...]
    k_taps, v_taps = owner_taps(turned, 1), owner_taps(turned, 2)
    await_slots(k_recv, sems.at[1, 1])
    owner_short(k_recv, k_taps, k_short)
    await_slots(v_recv, sems.at[13, 1])
    owner_short(v_recv, v_taps, v_short)
    flat_b[...] = (k_short[...] * v_short[...]).astype(BF16).astype(F32)
    fill_padded(pad_fwd, flat_b, False)
    causal_products(toeplitz, pad_fwd, flat_a)
    conv_send[...] = flat_a[...].reshape(blocks, GROUP, LANES).astype(BF16)
    start_exchange(me, across, conv_send, conv_recv, sems.at[3])
    fill_padded(pad_prod, flat_b, True)
    await_slots(conv_recv, sems.at[3, 1])

    squares = jnp.zeros((LANES, LANES), F32)
    tilts = jnp.zeros((LANES, LANES), F32)
    for index, lanes in chunks:
        value = from_pieces(conv_recv[pl.ds(16 * index, 16)])
        conv[:, lanes] = value
        gated = q_short[:, lanes] * value
        squares = squares + gated * gated
        tilts = tilts + gain_ref[:, lanes] * grad_ref[:, lanes].astype(F32) * gated
    row_send[...] = jnp.zeros(row_send.shape, F32)
    row_send[pl.ds(0, 1), :] = jnp.sum(squares.T, axis=0, keepdims=True)
    row_send[pl.ds(1, 1), :] = jnp.sum(tilts.T, axis=0, keepdims=True)
    for step in range(1, 8):
        remote(row_send, row_recv.at[rank], sems.at[4], {"tp": (rank + step) % 8}).start()
    row_recv[pl.ds(rank, 1)] = row_send[...][None]
    await_slots(row_recv.at[pl.ds(0, 7)], sems.at[4, 1])
    sums = jnp.sum(row_recv[...], axis=0)
    scale = lax.rsqrt(sums[0:1] / channels + norm_eps)
    bend = scale**3 * sums[1:2] / channels
    scale = jnp.broadcast_to(scale, (LANES, LANES)).T
    bend = jnp.broadcast_to(bend, (LANES, LANES)).T

    def gate(lanes):
        value, q_value = conv[:, lanes], q_short[:, lanes]
        gain = gain_ref[:, lanes]
        upstream = grad_ref[:, lanes].astype(F32)
        gated = q_value * value
        grad_gated = scale * (gain * upstream) - gated * bend
        return value, q_value, gain, upstream, gated, grad_gated

    for index, lanes in chunks:
        _, q_value, _, _, _, grad_gated = gate(lanes)
        back_send[pl.ds(16 * index, 16)] = to_pieces(grad_gated * q_value)
    start_exchange(me, across, back_send, back_recv, sems.at[5])

    for index, lanes in chunks:
        value, _, gain, upstream, gated, grad_gated = gate(lanes)
        normed_ref[:, lanes] = (gated * scale * gain).astype(BF16)
        part_send[7 * 4 + index] = jnp.sum(upstream * gated * scale, axis=0, keepdims=True)
        first = (grad_gated * value).astype(BF16)
        after_send[:, lanes] = first[:16]
        first = first.astype(F32)
        conv[:, lanes] = first
        for lag in range(TAPS):
            part_send[lag * 4 + index] = jnp.sum(
                first * pad[pl.ds(8 - lag, LANES), lanes], axis=0, keepdims=True
            )
    remote(after_send, after_recv, sems.at[6], preceding).start()
    store_normed = pltpu.make_async_copy(normed_ref, normed_hbm, store_sems.at[0])
    store_normed.start()

    def send_part(partner):
        place = (partner // 16) * 8 + partner % 8
        remote(
            part_send.at[place], part_recv.at[me], sems.at[7], {"ctx": partner, "tp": across}
        ).start()

    each_partner(me, send_part)
    await_slots(part_recv, sems.at[7, 1])
    part_sum[...] = jnp.sum(part_recv[...], axis=0)
    mine = (me // 16) * 8 + me % 8

    def send_total(partner):
        remote(part_sum, first_all.at[mine], sems.at[8], {"ctx": partner, "tp": across}).start()

    each_of_half(me, send_total)

    await_slots(back_recv, sems.at[5, 1])
    fill_windows(windows, back_recv)
    lagged_products(windows, [pad_filt, pad_prod], [flat_a, flat_b])

    def place_filter(index, carry):
        step = pl.multiple_of((blocks - 1 - index) * GROUP, GROUP)
        lag_send[index] = flat_b[pl.ds(step, GROUP), :].astype(BF16)
        return carry

    lax.fori_loop(0, blocks, place_filter, 0, unroll=8)
    start_exchange(me, across, lag_send, lag_recv, sems.at[12])
    k_sums = owner_back(k_recv, k_taps, flat_a, v_short, k_back_send)
    start_exchange(me, across, k_back_send, k_back_recv, sems.at[9])
    v_sums = owner_back(v_recv, v_taps, flat_a, k_short, v_back_send)
    start_exchange(me, across, v_back_send, v_back_recv, sems.at[14])
    lane_ids = lax.broadcasted_iota(jnp.int32, (GROUP, LANES), 1)
    chan_ids = lax.broadcasted_iota(jnp.int32, (GROUP, LANES), 0)
    packed = jnp.zeros((GROUP, LANES), F32)
    for place, value in enumerate(k_sums + v_sums):
        total = jnp.sum(value, axis=1, keepdims=True)
        packed = packed + jnp.where(lane_ids == place * GROUP + chan_ids, total, 0.0)
    owner_sum[...] = jnp.sum(packed, axis=0, keepdims=True)
    start_gather(me, across, owner_sum, owner_all, sems.at[10])

    remote(after_send, after_recv, sems.at[6], preceding).wait_recv()
    pad[pl.ds(0, LANES), :] = conv[...]
    pad[pl.ds(LANES, 8), :] = jnp.where(me < 63, after_recv[...].astype(F32)[:8, :], 0.0)
    for _, lanes in chunks:
        for top in (0, 64):
            total = jnp.zeros((64, LANES), F32)
            for lag in range(TAPS):
                total = total + taps_ref[0, lag : lag + 1, lanes] * pad[pl.ds(lag + top, 64), lanes]
            feature_grad_ref[0, pl.ds(top, 64), lanes] = total.astype(BF16)

    await_slots(first_all, sems.at[8, 1])
    for index, lanes in chunks:
        for lag in range(TAPS):
            taps_grad_ref[0, lag : lag + 1, lanes] = first_all[lag * len(chunks) + index]
        gain_grad_ref[:, lanes] = first_all[TAPS * len(chunks) + index]
    await_slots(owner_all, sems.at[10, 1])
    lane_ids = lax.broadcasted_iota(jnp.int32, (16, LANES), 1)
    row_ids = lax.broadcasted_iota(jnp.int32, (16, LANES), 0)
    for index, lanes in chunks:
        owned = owner_all[pl.ds(16 * index, 16)].reshape(16, LANES)
        owned = pltpu.roll(owned, 0, 1, stride=GROUP, stride_axis=0)
        for place in range(2 * TAPS):
            turned = pltpu.roll(owned, (LANES - GROUP * place) % LANES, 1) if place else owned
            value = jnp.where(lane_ids // GROUP == row_ids, turned, 0.0)
            taps_grad_ref[1 + place // TAPS, pl.ds(place % TAPS, 1), lanes] = jnp.sum(
                value, axis=0, keepdims=True
            )
    stores = [
        pltpu.make_async_copy(feature_grad_ref.at[0], feature_grad_hbm.at[0], store_sems.at[1]),
        pltpu.make_async_copy(taps_grad_ref, taps_grad_hbm, store_sems.at[2]),
        pltpu.make_async_copy(gain_grad_ref, gain_grad_hbm, store_sems.at[3]),
    ]
    for store in stores:
        store.start()

    def finish(pieces, target, hbm, number):
        for index, lanes in chunks:
            target[:, lanes] = from_pieces(pieces(pl.ds(16 * index, 16))).astype(BF16)
        store = pltpu.make_async_copy(target, hbm, store_sems.at[number])
        store.start()
        stores.append(store)

    await_slots(lag_recv, sems.at[12, 1])
    finish(lambda spot: lag_recv[spot], filter_grad_ref, filter_grad_hbm, 4)
    for stream, (pieces, number) in enumerate(((k_back_recv, 9), (v_back_recv, 14)), 1):
        await_slots(pieces, sems.at[number, 1])
        finish(
            lambda spot, pieces=pieces: pieces[spot],
            feature_grad_ref.at[stream],
            feature_grad_hbm.at[stream],
            4 + stream,
        )

    for ref, number in (
        (filt_recv, 0),
        (k_recv, 1),
        (v_recv, 13),
        (conv_recv, 3),
        (row_recv.at[pl.ds(0, 7)], 4),
        (back_recv, 5),
        (part_recv, 7),
        (first_all, 8),
        (k_back_recv, 9),
        (v_back_recv, 14),
        (lag_recv, 12),
        (owner_all, 10),
    ):
        await_slots(ref, sems.at[number, 0])
    taps_copy.wait_send()
    store_normed.wait()
    for store in stores:
        store.wait()
    remote(last, before_recv, sems.at[2], following).wait_send()
    remote(after_send, after_recv, sems.at[6], preceding).wait_send()


def hand_on_kernel(*refs):
    sources, targets, stages = refs[:5], refs[5:10], refs[10:15]
    load_sems, store_sems = refs[15:]
    loads = [pltpu.make_async_copy(sources[i], stages[i], load_sems.at[i]) for i in range(5)]
    stores = [pltpu.make_async_copy(stages[i], targets[i], store_sems.at[i]) for i in range(5)]
    for load in loads:
        load.start()
    for load, store in zip(loads, stores):
        load.wait()
        store.start()
    for store in stores:
        store.wait()


def per_device(features, short_taps, long_filter, gain, out_grad):
    seq_rows, width = long_filter.shape
    blocks = lax.axis_size("ctx")
    pieces = (blocks, GROUP, LANES)
    flat = (blocks * GROUP, LANES)
    padded = (GROUP, 2 * blocks, LANES)
    row = (1, LANES)
    outs = [
        jax.ShapeDtypeStruct((seq_rows, width), BF16),
        jax.ShapeDtypeStruct((3, seq_rows, width), BF16),
        jax.ShapeDtypeStruct((seq_rows, width), BF16),
        jax.ShapeDtypeStruct((3, TAPS, width), F32),
        jax.ShapeDtypeStruct((1, width), F32),
    ]
    results = pl.pallas_call(
        block_kernel,
        out_shape=outs,
        in_specs=[HBM] * 5,
        out_specs=[HBM] * 5,
        scratch_shapes=[pltpu.VMEM(out.shape, out.dtype) for out in outs]
        + [
            pltpu.VMEM((3, seq_rows, width), BF16),
            pltpu.VMEM(short_taps.shape, F32),
            pltpu.VMEM((seq_rows, width), BF16),
            pltpu.VMEM((1, width), F32),
            pltpu.VMEM((seq_rows, width), BF16),
        ]
        + [pltpu.VMEM(pieces, BF16)] * 16
        + [pltpu.VMEM((16, width), BF16)] * 3
        + [
            pltpu.VMEM((8, LANES), F32),
            pltpu.VMEM((8, 8, LANES), F32),
            pltpu.VMEM((blocks // 2,) + row, F32),
            pltpu.VMEM((blocks,) + row, F32),
            pltpu.VMEM(row, F32),
            pltpu.VMEM((blocks // 2,) + row, F32),
            pltpu.VMEM(row, F32),
            pltpu.VMEM((blocks,) + row, F32),
            pltpu.VMEM((width, LANES), F32),
            pltpu.VMEM((GROUP, LANES), F32),
            pltpu.VMEM((seq_rows + 8, width), F32),
            pltpu.VMEM((seq_rows, width), F32),
            pltpu.VMEM((seq_rows, width), F32),
            pltpu.VMEM(((blocks + 2) * GROUP, LANES), F32),
        ]
        + [pltpu.VMEM(flat, F32)] * 4
        + [pltpu.VMEM(padded, F32)] * 3
        + [pltpu.VMEM((GROUP, blocks * LANES, LANES), BF16)]
        + [pltpu.SemaphoreType.DMA((15, 2)), pltpu.SemaphoreType.DMA((5,)), pltpu.SemaphoreType.DMA((7,))],
        compiler_params=pltpu.CompilerParams(
            collective_id=0, has_side_effects=True, vmem_limit_bytes=60 << 20
        ),
    )(features, short_taps, long_filter, gain[None, :], out_grad)
    normed, feature_grad, filter_grad, taps_grad, gain_grad = pl.pallas_call(
        hand_on_kernel,
        out_shape=outs,
        in_specs=[HBM] * 5,
        out_specs=[HBM] * 5,
        scratch_shapes=[pltpu.VMEM(out.shape, out.dtype) for out in outs]
        + [pltpu.SemaphoreType.DMA((5,))] * 2,
        compiler_params=pltpu.CompilerParams(vmem_limit_bytes=60 << 20),
    )(*results)
    return (normed, feature_grad, filter_grad, taps_grad, gain_grad[0])


def solution(mesh):
    return jax.shard_map(
        per_device,
        mesh=mesh,
        in_specs=(
            P(None, "ctx", "tp"),
            P(None, None, "tp"),
            P("ctx", "tp"),
            P("tp"),
            P("ctx", "tp"),
        ),
        out_specs=(
            P("ctx", "tp"),
            P(None, "ctx", "tp"),
            P("ctx", "tp"),
            P(None, None, "tp"),
            P("tp"),
        ),
        check_vma=False,
    )
```

```python
import functools

import jax
import jax.numpy as jnp
from jax import lax
from jax.experimental import pallas as pl
from jax.experimental.pallas import tpu as pltpu
from jax.sharding import PartitionSpec as P

F32 = jnp.float32
BF16 = jnp.bfloat16
MESH = pl.DeviceIdType.MESH
norm_eps = 1e-06

TAPS = 7
LANES = 128
GROUP = 8
HBM = pl.BlockSpec(memory_space=pltpu.HBM)


def lane_chunks(width):
    return [slice(start, start + LANES) for start in range(0, width, LANES)]


def each_partner(me, visit):
    def one(step, carry):
        visit((me + step) % 64)
        return carry

    lax.fori_loop(0, 64, one, 0)


def each_of_half(me, visit):
    row, half, col = me // 16, (me // 8) % 2, me % 8

    def one(step, carry):
        visit(((row + step // 8) % 4) * 16 + half * 8 + (col + step % 8) % 8)
        return carry

    lax.fori_loop(0, 32, one, 0)


def remote(source, target, sems, device):
    return pltpu.make_async_remote_copy(
        src_ref=source,
        dst_ref=target,
        send_sem=sems.at[0],
        recv_sem=sems.at[1],
        device_id=device,
        device_id_type=MESH,
    )


def start_exchange(me, across, source, target, sems):
    def visit(partner):
        remote(source.at[partner], target.at[me], sems, {"ctx": partner, "tp": across}).start()

    each_partner(me, visit)


def start_gather(me, across, piece, target, sems):
    def visit(partner):
        remote(piece, target.at[me], sems, {"ctx": partner, "tp": across}).start()

    each_partner(me, visit)


def await_slots(ref, sem):
    pltpu.make_async_copy(ref, ref, sem).wait()


def toeplitz_rows(current, other, first, backward):
    rows = lax.broadcasted_iota(jnp.int32, (16, LANES), 0) + first
    lanes = lax.broadcasted_iota(jnp.int32, (16, LANES), 1)
    current = jnp.broadcast_to(current, (16, LANES))
    other = jnp.broadcast_to(other, (16, LANES))
    if backward:
        mixed = jnp.where(lanes >= LANES - 1 - rows, current, other)
        return pltpu.roll(mixed, first + 1, 1, stride=1, stride_axis=0)
    mixed = jnp.where(lanes < LANES - rows, current, other)
    return pltpu.roll(mixed, first, 1, stride=1, stride_axis=0)


def fill_padded(pad, work, mirrored):
    blocks = pad.shape[1] // 2
    if mirrored:
        spots = lax.broadcasted_iota(jnp.int32, (LANES, LANES), 0) + lax.broadcasted_iota(
            jnp.int32, (LANES, LANES), 1
        )
        mirror = jnp.where(spots == LANES - 1, 1.0, 0.0).astype(BF16)
    for chan in range(GROUP):
        rows = work[pl.ds(chan, blocks, stride=GROUP), :]
        if mirrored:
            rows = jnp.dot(rows.astype(BF16), mirror, preferred_element_type=F32)
        pad[chan, pl.ds(0, blocks), :] = jnp.zeros((blocks, LANES), F32)
        pad[chan, pl.ds(blocks, blocks), :] = rows


def fill_windows(windows, pieces):
    blocks = pieces.shape[0]
    rows = blocks * GROUP
    edge = jnp.zeros((GROUP, LANES), F32)
    windows[pl.ds(0, GROUP), :] = edge
    windows[pl.ds(rows + GROUP, GROUP), :] = edge
    windows[pl.ds(GROUP, rows), :] = pieces[...].astype(F32).reshape(rows, LANES)


def toeplitz_block(windows, chan, lag, backward):
    base = pl.multiple_of((lag + 1) * GROUP, GROUP) + chan
    current = windows[pl.ds(base, 1), :]
    other = windows[pl.ds(base + (GROUP if backward else -GROUP), 1), :]
    return [
        toeplitz_rows(current, other, first, backward).astype(BF16) for first in range(0, LANES, 16)
    ]


def build_toeplitz(windows, toeplitz):
    blocks = toeplitz.shape[1] // LANES

    def channel(chan, carry):
        def lags(lag, inner):
            rows = toeplitz_block(windows, chan, lag, False)
            for i, part in enumerate(rows):
                toeplitz[chan, pl.ds(pl.multiple_of(lag * LANES, LANES) + 16 * i, 16), :] = part
            return inner

        return lax.fori_loop(0, blocks, lags, carry, unroll=blocks)

    lax.fori_loop(0, GROUP, channel, 0)


def causal_products(toeplitz, padded, flat):
    blocks = padded.shape[1] // 2

    def channel(chan, carry):
        def two_lags(pair, total):
            left = [padded[chan, pl.ds(blocks - 2 * pair - i, blocks), :] for i in range(2)]
            right = toeplitz[chan, pl.ds(pl.multiple_of(pair * 2 * LANES, 2 * LANES), 2 * LANES), :]
            return total + jnp.dot(
                jnp.concatenate(left, axis=1).astype(BF16), right, preferred_element_type=F32
            )

        total = lax.fori_loop(
            0, blocks // 2, two_lags, jnp.zeros((blocks, LANES), F32), unroll=blocks // 2
        )
        flat[pl.ds(chan, blocks, stride=GROUP), :] = total
        return carry

    lax.fori_loop(0, GROUP, channel, 0, unroll=2)


def lagged_products(windows, padded, flat):
    count = len(padded)
    blocks = padded[0].shape[1] // 2

    def channel(chan, carry):
        def two_lags(pair, total):
            left, right = [], []
            for lag in (2 * pair, 2 * pair + 1):
                right += toeplitz_block(windows, chan, lag, True)
                left.append(
                    jnp.concatenate([pad[chan, pl.ds(lag + 1, blocks), :] for pad in padded], axis=0)
                )
            return total + jnp.dot(
                jnp.concatenate(left, axis=1).astype(BF16),
                jnp.concatenate(right, axis=0),
                preferred_element_type=F32,
            )

        total = lax.fori_loop(
            0, blocks // 2, two_lags, jnp.zeros((count * blocks, LANES), F32), unroll=blocks // 2
        )
        for i, work in enumerate(flat):
            work[pl.ds(chan, blocks, stride=GROUP), :] = total[i * blocks : (i + 1) * blocks]
        return carry

    lax.fori_loop(0, GROUP, channel, 0, unroll=2)


def to_pieces(block):
    return block.T.reshape(16, GROUP, LANES).astype(BF16)


def from_pieces(pieces):
    return pieces.astype(F32).reshape(LANES, LANES).T


def owner_taps(taps, stream):
    return [
        jnp.broadcast_to(taps[:, stream * TAPS + lag : stream * TAPS + lag + 1], (GROUP, LANES))
        for lag in range(TAPS)
    ]


def owner_short(raw, taps, target):
    lanes = lax.broadcasted_iota(jnp.int32, (GROUP, LANES), 1)

    def block(index, before):
        now = raw[index].astype(F32)
        total = taps[0] * now
        after = []
        for lag in range(1, TAPS):
            turned = pltpu.roll(now, lag, 1)
            total = total + taps[lag] * jnp.where(lanes >= lag, turned, before[lag - 1])
            after.append(turned)
        target[pl.ds(pl.multiple_of(index * GROUP, GROUP), GROUP), :] = total.astype(BF16).astype(F32)
        return tuple(after)

    zero = jnp.zeros((GROUP, LANES), F32)
    lax.fori_loop(0, raw.shape[0], block, (zero,) * (TAPS - 1), unroll=8)


def owner_back(raw, taps, grad_flat, partner_flat, target):
    lanes = lax.broadcasted_iota(jnp.int32, (GROUP, LANES), 1)
    blocks = raw.shape[0]

    def block(step, carry):
        after, sums = carry
        index = blocks - 1 - step
        grad = grad_flat[pl.ds(pl.multiple_of(step * GROUP, GROUP), GROUP), :].astype(BF16).astype(F32)
        rows = pl.ds(pl.multiple_of(index * GROUP, GROUP), GROUP)
        grad = (grad * partner_flat[rows, :]).astype(BF16).astype(F32)
        value = raw[index].astype(F32)
        total = taps[0] * grad
        new_sums = [sums[0] + value * grad]
        new_after = []
        for lag in range(1, TAPS):
            turned = pltpu.roll(grad, LANES - lag, 1)
            moved = jnp.where(lanes < LANES - lag, turned, after[lag - 1])
            total = total + taps[lag] * moved
            new_sums.append(sums[lag] + value * moved)
            new_after.append(turned)
        target[index] = total.astype(BF16)
        return tuple(new_after), tuple(new_sums)

    zero = jnp.zeros((GROUP, LANES), F32)
    _, sums = lax.fori_loop(
        0, blocks, block, ((zero,) * (TAPS - 1), (zero,) * TAPS), unroll=8
    )
    return sums


def block_kernel(
    features_hbm,
    taps_hbm,
    filter_hbm,
    gain_hbm,
    grad_hbm,
    normed_hbm,
    q_grad_hbm,
    taps_grad_hbm,
    gain_grad_hbm,
    lag_recv,
    k_back_recv,
    v_back_recv,
    normed_ref,
    q_grad_ref,
    taps_grad_ref,
    gain_grad_ref,
    features_ref,
    taps_ref,
    filter_ref,
    gain_ref,
    grad_ref,
    filt_send,
    filt_recv,
    k_send,
    k_recv,
    v_send,
    v_recv,
    conv_send,
    conv_recv,
    back_send,
    back_recv,
    lag_send,
    k_back_send,
    v_back_send,
    before_recv,
    after_send,
    after_recv,
    row_send,
    row_recv,
    part_send,
    part_recv,
    part_sum,
    first_all,
    owner_sum,
    owner_all,
    taps_turned,
    taps_recv,
    pad,
    q_short,
    conv,
    windows,
    k_short,
    v_short,
    flat_a,
    flat_b,
    pad_fwd,
    pad_filt,
    pad_prod,
    toeplitz,
    sems,
    load_sems,
    store_sems,
):
    me = lax.axis_index("ctx")
    rank = lax.axis_index("tp")
    across = (rank + 4) % 8
    width = filter_ref.shape[1]
    chunks = list(enumerate(lane_chunks(width)))
    blocks = filt_recv.shape[0]
    rows = blocks * GROUP
    channels = width * 8
    following = {"ctx": (me + 1) % 64}
    preceding = {"ctx": (me + 63) % 64}

    barrier = pltpu.get_barrier_semaphore()

    def greet(partner):
        pl.semaphore_signal(
            barrier, inc=1, device_id={"ctx": partner, "tp": across}, device_id_type=MESH
        )

    for device in (following, preceding):
        pl.semaphore_signal(barrier, inc=1, device_id=device, device_id_type=MESH)
    for step in range(1, 8):
        pl.semaphore_signal(
            barrier, inc=1, device_id={"tp": (rank + step) % 8}, device_id_type=MESH
        )
    each_partner(me, greet)
    loads = [
        pltpu.make_async_copy(source, target, load_sems.at[i])
        for i, (source, target) in enumerate(
            (
                (filter_hbm, filter_ref),
                (features_hbm, features_ref),
                (taps_hbm, taps_ref),
                (gain_hbm, gain_ref),
                (grad_hbm, grad_ref),
            )
        )
    ]
    for load in loads:
        load.start()
    for load in loads:
        load.wait()

    for index, lanes in chunks:
        spot = pl.ds(16 * index, 16)
        filt_send[spot] = to_pieces(filter_ref[:, lanes].astype(F32))
        k_send[spot] = to_pieces(features_ref[1, :, lanes].astype(F32))
        v_send[spot] = to_pieces(features_ref[2, :, lanes].astype(F32))
    filler = jnp.zeros((LANES - 3 * TAPS, LANES), F32)
    for index, lanes in chunks:
        stack = jnp.concatenate([taps_ref[i, :, lanes] for i in range(3)] + [filler], axis=0)
        taps_turned[pl.ds(LANES * index, LANES), :] = stack.T
    pl.semaphore_wait(barrier, 73)
    start_exchange(me, across, filt_send, filt_recv, sems.at[0])
    own_taps = taps_turned.at[pl.ds(pl.multiple_of(me * GROUP, GROUP), GROUP)]
    taps_copy = remote(own_taps, taps_recv, sems.at[11], {"tp": across})
    taps_copy.start()
    last = features_ref.at[0, pl.ds(LANES - 16, 16)]
    remote(last, before_recv, sems.at[2], following).start()
    start_exchange(me, across, k_send, k_recv, sems.at[1])
    start_exchange(me, across, v_send, v_recv, sems.at[13])

    remote(last, before_recv, sems.at[2], following).wait_recv()
    pad[pl.ds(0, 8), :] = jnp.where(me > 0, before_recv[...].astype(F32)[8:, :], 0.0)
    pad[pl.ds(8, LANES), :] = features_ref[0].astype(F32)
    for _, lanes in chunks:
        for top in (0, 64):
            running = jnp.zeros((64, LANES), F32)
            for lag in range(TAPS):
                running = running + taps_ref[0, lag : lag + 1, lanes] * pad[
                    pl.ds(8 - lag + top, 64), lanes
                ]
            q_short[pl.ds(top, 64), lanes] = running.astype(BF16).astype(F32)

    await_slots(filt_recv, sems.at[0, 1])
    fill_windows(windows, filt_recv)
    build_toeplitz(windows, toeplitz)
    flat_a[...] = filt_recv[...].astype(F32).reshape(rows, LANES)
    fill_padded(pad_filt, flat_a, True)
    taps_copy.wait_recv()
    turned = taps_recv[...]
    k_taps, v_taps = owner_taps(turned, 1), owner_taps(turned, 2)
    await_slots(k_recv, sems.at[1, 1])
    owner_short(k_recv, k_taps, k_short)
    await_slots(v_recv, sems.at[13, 1])
    owner_short(v_recv, v_taps, v_short)
    flat_b[...] = (k_short[...] * v_short[...]).astype(BF16).astype(F32)
    fill_padded(pad_fwd, flat_b, False)
    causal_products(toeplitz, pad_fwd, flat_a)
    conv_send[...] = flat_a[...].reshape(blocks, GROUP, LANES).astype(BF16)
    start_exchange(me, across, conv_send, conv_recv, sems.at[3])
    fill_padded(pad_prod, flat_b, True)
    await_slots(conv_recv, sems.at[3, 1])

    squares = jnp.zeros((LANES, LANES), F32)
    tilts = jnp.zeros((LANES, LANES), F32)
    for index, lanes in chunks:
        value = from_pieces(conv_recv[pl.ds(16 * index, 16)])
        conv[:, lanes] = value
        gated = q_short[:, lanes] * value
        squares = squares + gated * gated
        tilts = tilts + gain_ref[:, lanes] * grad_ref[:, lanes].astype(F32) * gated
    row_send[pl.ds(0, 1), :] = jnp.sum(squares.T, axis=0, keepdims=True)
    row_send[pl.ds(1, 1), :] = jnp.sum(tilts.T, axis=0, keepdims=True)
    for step in range(1, 8):
        remote(row_send, row_recv.at[rank], sems.at[4], {"tp": (rank + step) % 8}).start()
    row_recv[pl.ds(rank, 1)] = row_send[...][None]
    await_slots(row_recv.at[pl.ds(0, 7)], sems.at[4, 1])
    sums = jnp.sum(row_recv[...], axis=0)
    scale = lax.rsqrt(sums[0:1] / channels + norm_eps)
    bend = scale**3 * sums[1:2] / channels
    scale = jnp.broadcast_to(scale, (LANES, LANES)).T
    bend = jnp.broadcast_to(bend, (LANES, LANES)).T

    def gate(lanes):
        value, q_value = conv[:, lanes], q_short[:, lanes]
        gain = gain_ref[:, lanes]
        upstream = grad_ref[:, lanes].astype(F32)
        gated = q_value * value
        grad_gated = scale * (gain * upstream) - gated * bend
        return value, q_value, gain, upstream, gated, grad_gated

    for index, lanes in chunks:
        _, q_value, _, _, _, grad_gated = gate(lanes)
        back_send[pl.ds(16 * index, 16)] = to_pieces(grad_gated * q_value)
    start_exchange(me, across, back_send, back_recv, sems.at[5])

    for index, lanes in chunks:
        value, _, gain, upstream, gated, grad_gated = gate(lanes)
        normed_ref[:, lanes] = (gated * scale * gain).astype(BF16)
        part_send[7 * 4 + index] = jnp.sum(upstream * gated * scale, axis=0, keepdims=True)
        first = (grad_gated * value).astype(BF16)
        after_send[:, lanes] = first[:16]
        first = first.astype(F32)
        conv[:, lanes] = first
        for lag in range(TAPS):
            part_send[lag * 4 + index] = jnp.sum(
                first * pad[pl.ds(8 - lag, LANES), lanes], axis=0, keepdims=True
            )
    remote(after_send, after_recv, sems.at[6], preceding).start()
    store_normed = pltpu.make_async_copy(normed_ref, normed_hbm, store_sems.at[0])
    store_normed.start()

    def send_part(partner):
        place = (partner // 16) * 8 + partner % 8
        remote(
            part_send.at[place], part_recv.at[me], sems.at[7], {"ctx": partner, "tp": across}
        ).start()

    each_partner(me, send_part)

    await_slots(back_recv, sems.at[5, 1])
    fill_windows(windows, back_recv)
    lagged_products(windows, [pad_filt, pad_prod], [flat_a, flat_b])

    def place_filter(index, carry):
        step = pl.multiple_of((blocks - 1 - index) * GROUP, GROUP)
        lag_send[index] = flat_b[pl.ds(step, GROUP), :].astype(BF16)
        return carry

    lax.fori_loop(0, blocks, place_filter, 0, unroll=8)
    start_exchange(me, across, lag_send, lag_recv, sems.at[12])
    k_sums = owner_back(k_recv, k_taps, flat_a, v_short, k_back_send)
    start_exchange(me, across, k_back_send, k_back_recv, sems.at[9])
    v_sums = owner_back(v_recv, v_taps, flat_a, k_short, v_back_send)
    start_exchange(me, across, v_back_send, v_back_recv, sems.at[14])
    lane_ids = lax.broadcasted_iota(jnp.int32, (GROUP, LANES), 1)
    chan_ids = lax.broadcasted_iota(jnp.int32, (GROUP, LANES), 0)
    packed = jnp.zeros((GROUP, LANES), F32)
    for place, value in enumerate(k_sums + v_sums):
        total = jnp.sum(value, axis=1, keepdims=True)
        packed = packed + jnp.where(lane_ids == place * GROUP + chan_ids, total, 0.0)
    owner_sum[...] = jnp.sum(packed, axis=0, keepdims=True)
    start_gather(me, across, owner_sum, owner_all, sems.at[10])

    await_slots(part_recv, sems.at[7, 1])
    part_sum[...] = jnp.sum(part_recv[...], axis=0)
    mine = (me // 16) * 8 + me % 8

    def send_total(partner):
        remote(part_sum, first_all.at[mine], sems.at[8], {"ctx": partner, "tp": across}).start()

    each_of_half(me, send_total)

    remote(after_send, after_recv, sems.at[6], preceding).wait_recv()
    pad[pl.ds(0, LANES), :] = conv[...]
    pad[pl.ds(LANES, 8), :] = jnp.where(me < 63, after_recv[...].astype(F32)[:8, :], 0.0)
    for _, lanes in chunks:
        for top in (0, 64):
            total = jnp.zeros((64, LANES), F32)
            for lag in range(TAPS):
                total = total + taps_ref[0, lag : lag + 1, lanes] * pad[pl.ds(lag + top, 64), lanes]
            q_grad_ref[pl.ds(top, 64), lanes] = total.astype(BF16)

    await_slots(first_all, sems.at[8, 1])
    for index, lanes in chunks:
        for lag in range(TAPS):
            taps_grad_ref[0, lag : lag + 1, lanes] = first_all[lag * len(chunks) + index]
        gain_grad_ref[:, lanes] = first_all[TAPS * len(chunks) + index]
    await_slots(owner_all, sems.at[10, 1])
    lane_ids = lax.broadcasted_iota(jnp.int32, (16, LANES), 1)
    row_ids = lax.broadcasted_iota(jnp.int32, (16, LANES), 0)
    for index, lanes in chunks:
        owned = owner_all[pl.ds(16 * index, 16)].reshape(16, LANES)
        owned = pltpu.roll(owned, 0, 1, stride=GROUP, stride_axis=0)
        for place in range(2 * TAPS):
            turned = pltpu.roll(owned, (LANES - GROUP * place) % LANES, 1) if place else owned
            value = jnp.where(lane_ids // GROUP == row_ids, turned, 0.0)
            taps_grad_ref[1 + place // TAPS, pl.ds(place % TAPS, 1), lanes] = jnp.sum(
                value, axis=0, keepdims=True
            )
    stores = [
        pltpu.make_async_copy(q_grad_ref, q_grad_hbm, store_sems.at[1]),
        pltpu.make_async_copy(taps_grad_ref, taps_grad_hbm, store_sems.at[2]),
        pltpu.make_async_copy(gain_grad_ref, gain_grad_hbm, store_sems.at[3]),
    ]
    for store in stores:
        store.start()

    for ref, number in ((lag_recv, 12), (k_back_recv, 9), (v_back_recv, 14)):
        await_slots(ref, sems.at[number, 1])
    for ref, number in (
        (filt_recv, 0),
        (k_recv, 1),
        (v_recv, 13),
        (conv_recv, 3),
        (row_recv.at[pl.ds(0, 7)], 4),
        (back_recv, 5),
        (part_recv, 7),
        (first_all, 8),
        (k_back_recv, 9),
        (v_back_recv, 14),
        (lag_recv, 12),
        (owner_all, 10),
    ):
        await_slots(ref, sems.at[number, 0])
    taps_copy.wait_send()
    store_normed.wait()
    for store in stores:
        store.wait()
    remote(last, before_recv, sems.at[2], following).wait_send()
    remote(after_send, after_recv, sems.at[6], preceding).wait_send()


def closing_kernel(*refs):
    sources, targets, stages = refs[:7], refs[7:12], refs[12:19]
    filter_stage, stream_stage, load_sems, store_sems = refs[19:]
    normed, feature_grad, filter_grad, taps_grad, gain_grad = targets
    loads = [pltpu.make_async_copy(sources[i], stages[i], load_sems.at[i]) for i in range(7)]
    for load in loads:
        load.start()
    stores = []

    def store(source, target):
        copy = pltpu.make_async_copy(source, target, store_sems.at[len(stores)])
        copy.start()
        stores.append(copy)

    for i, target in enumerate((normed, feature_grad.at[0], taps_grad, gain_grad)):
        loads[i].wait()
        store(stages[i], target)
    turned = (
        (filter_stage, filter_grad),
        (stream_stage.at[0], feature_grad.at[1]),
        (stream_stage.at[1], feature_grad.at[2]),
    )
    for i, (stage, target) in enumerate(turned, 4):
        loads[i].wait()
        for index, lanes in enumerate(lane_chunks(stage.shape[1])):
            stage[:, lanes] = from_pieces(stages[i][pl.ds(16 * index, 16)]).astype(BF16)
        store(stage, target)
    for copy in stores:
        copy.wait()


def per_device(features, short_taps, long_filter, gain, out_grad):
    seq_rows, width = long_filter.shape
    blocks = lax.axis_size("ctx")
    pieces = (blocks, GROUP, LANES)
    flat = (blocks * GROUP, LANES)
    padded = (GROUP, 2 * blocks, LANES)
    row = (1, LANES)
    plane = jax.ShapeDtypeStruct((seq_rows, width), BF16)
    taps = jax.ShapeDtypeStruct((3, TAPS, width), F32)
    gains = jax.ShapeDtypeStruct((1, width), F32)
    arrivals = [jax.ShapeDtypeStruct(pieces, BF16)] * 3
    outs = [plane, plane, taps, gains] + arrivals
    results = pl.pallas_call(
        block_kernel,
        out_shape=outs,
        in_specs=[HBM] * 5,
        out_specs=[HBM] * 7,
        scratch_shapes=[pltpu.VMEM(out.shape, out.dtype) for out in outs[:4]]
        + [
            pltpu.VMEM((3, seq_rows, width), BF16),
            pltpu.VMEM(short_taps.shape, F32),
            pltpu.VMEM((seq_rows, width), BF16),
            pltpu.VMEM((1, width), F32),
            pltpu.VMEM((seq_rows, width), BF16),
        ]
        + [pltpu.VMEM(pieces, BF16)] * 13
        + [pltpu.VMEM((16, width), BF16)] * 3
        + [
            pltpu.VMEM((2, LANES), F32),
            pltpu.VMEM((8, 2, LANES), F32),
            pltpu.VMEM((blocks // 2,) + row, F32),
            pltpu.VMEM((blocks,) + row, F32),
            pltpu.VMEM(row, F32),
            pltpu.VMEM((blocks // 2,) + row, F32),
            pltpu.VMEM(row, F32),
            pltpu.VMEM((blocks,) + row, F32),
            pltpu.VMEM((width, LANES), F32),
            pltpu.VMEM((GROUP, LANES), F32),
            pltpu.VMEM((seq_rows + 8, width), F32),
            pltpu.VMEM((seq_rows, width), F32),
            pltpu.VMEM((seq_rows, width), F32),
            pltpu.VMEM(((blocks + 2) * GROUP, LANES), F32),
        ]
        + [pltpu.VMEM(flat, F32)] * 4
        + [pltpu.VMEM(padded, F32)] * 3
        + [pltpu.VMEM((GROUP, blocks * LANES, LANES), BF16)]
        + [pltpu.SemaphoreType.DMA((15, 2)), pltpu.SemaphoreType.DMA((5,)), pltpu.SemaphoreType.DMA((4,))],
        compiler_params=pltpu.CompilerParams(
            collective_id=0, has_side_effects=True, vmem_limit_bytes=60 << 20
        ),
    )(features, short_taps, long_filter, gain[None, :], out_grad)
    normed, feature_grad, filter_grad, taps_grad, gain_grad = pl.pallas_call(
        closing_kernel,
        out_shape=[plane, jax.ShapeDtypeStruct(features.shape, BF16), plane, taps, gains],
        in_specs=[HBM] * 7,
        out_specs=[HBM] * 5,
        scratch_shapes=[pltpu.VMEM(out.shape, out.dtype) for out in outs]
        + [pltpu.VMEM((seq_rows, width), BF16), pltpu.VMEM((2, seq_rows, width), BF16)]
        + [pltpu.SemaphoreType.DMA((7,))] * 2,
        compiler_params=pltpu.CompilerParams(vmem_limit_bytes=60 << 20),
    )(*results)
    return (normed, feature_grad, filter_grad, taps_grad, gain_grad[0])


def solution(mesh):
    return jax.shard_map(
        per_device,
        mesh=mesh,
        in_specs=(
            P(None, "ctx", "tp"),
            P(None, None, "tp"),
            P("ctx", "tp"),
            P("tp"),
            P("ctx", "tp"),
        ),
        out_specs=(
            P("ctx", "tp"),
            P(None, "ctx", "tp"),
            P("ctx", "tp"),
            P(None, None, "tp"),
            P("tp"),
        ),
        check_vma=False,
    )
```

```python
import functools

import jax
import jax.numpy as jnp
from jax import lax
from jax.experimental import pallas as pl
from jax.experimental.pallas import tpu as pltpu
from jax.sharding import PartitionSpec as P

F32 = jnp.float32
BF16 = jnp.bfloat16
MESH = pl.DeviceIdType.MESH
norm_eps = 1e-06

TAPS = 7
LANES = 128
GROUP = 8
HBM = pl.BlockSpec(memory_space=pltpu.HBM)


def lane_chunks(width):
    return [slice(start, start + LANES) for start in range(0, width, LANES)]


def each_partner(me, visit):
    def one(step, carry):
        visit((me + step) % 64)
        return carry

    lax.fori_loop(0, 64, one, 0)


def each_of_half(me, visit):
    row, half, col = me // 16, (me // 8) % 2, me % 8

    def one(step, carry):
        visit(((row + step // 8) % 4) * 16 + half * 8 + (col + step % 8) % 8)
        return carry

    lax.fori_loop(0, 32, one, 0)


def remote(source, target, sems, device):
    return pltpu.make_async_remote_copy(
        src_ref=source,
        dst_ref=target,
        send_sem=sems.at[0],
        recv_sem=sems.at[1],
        device_id=device,
        device_id_type=MESH,
    )


def start_exchange(me, across, source, target, sems):
    def visit(partner):
        remote(source.at[partner], target.at[me], sems, {"ctx": partner, "tp": across}).start()

    each_partner(me, visit)


def start_gather(me, across, piece, target, sems):
    def visit(partner):
        remote(piece, target.at[me], sems, {"ctx": partner, "tp": across}).start()

    each_partner(me, visit)


def await_slots(ref, sem):
    pltpu.make_async_copy(ref, ref, sem).wait()


def toeplitz_rows(current, other, first, backward):
    rows = lax.broadcasted_iota(jnp.int32, (16, LANES), 0) + first
    lanes = lax.broadcasted_iota(jnp.int32, (16, LANES), 1)
    current = jnp.broadcast_to(current, (16, LANES))
    other = jnp.broadcast_to(other, (16, LANES))
    if backward:
        mixed = jnp.where(lanes >= LANES - 1 - rows, current, other)
        return pltpu.roll(mixed, first + 1, 1, stride=1, stride_axis=0)
    mixed = jnp.where(lanes < LANES - rows, current, other)
    return pltpu.roll(mixed, first, 1, stride=1, stride_axis=0)


def fill_padded(pad, work, mirrored):
    blocks = pad.shape[1] // 2
    if mirrored:
        spots = lax.broadcasted_iota(jnp.int32, (LANES, LANES), 0) + lax.broadcasted_iota(
            jnp.int32, (LANES, LANES), 1
        )
        mirror = jnp.where(spots == LANES - 1, 1.0, 0.0).astype(BF16)
    for chan in range(GROUP):
        rows = work[pl.ds(chan, blocks, stride=GROUP), :]
        if mirrored:
            rows = jnp.dot(rows.astype(BF16), mirror, preferred_element_type=F32)
        pad[chan, pl.ds(0, blocks), :] = jnp.zeros((blocks, LANES), F32)
        pad[chan, pl.ds(blocks, blocks), :] = rows


def fill_windows(windows, pieces):
    blocks = pieces.shape[0]
    rows = blocks * GROUP
    edge = jnp.zeros((GROUP, LANES), F32)
    windows[pl.ds(0, GROUP), :] = edge
    windows[pl.ds(rows + GROUP, GROUP), :] = edge
    windows[pl.ds(GROUP, rows), :] = pieces[...].astype(F32).reshape(rows, LANES)


def toeplitz_block(windows, chan, lag, backward):
    base = pl.multiple_of((lag + 1) * GROUP, GROUP) + chan
    current = windows[pl.ds(base, 1), :]
    other = windows[pl.ds(base + (GROUP if backward else -GROUP), 1), :]
    return [
        toeplitz_rows(current, other, first, backward).astype(BF16) for first in range(0, LANES, 16)
    ]


def build_toeplitz(windows, toeplitz):
    blocks = toeplitz.shape[1] // LANES

    def channel(chan, carry):
        def lags(lag, inner):
            rows = toeplitz_block(windows, chan, lag, False)
            for i, part in enumerate(rows):
                toeplitz[chan, pl.ds(pl.multiple_of(lag * LANES, LANES) + 16 * i, 16), :] = part
            return inner

        return lax.fori_loop(0, blocks, lags, carry, unroll=blocks)

    lax.fori_loop(0, GROUP, channel, 0)


def causal_products(toeplitz, padded, flat):
    blocks = padded.shape[1] // 2

    def channel(chan, carry):
        def two_lags(pair, total):
            left = [padded[chan, pl.ds(blocks - 2 * pair - i, blocks), :] for i in range(2)]
            right = toeplitz[chan, pl.ds(pl.multiple_of(pair * 2 * LANES, 2 * LANES), 2 * LANES), :]
            return total + jnp.dot(
                jnp.concatenate(left, axis=1).astype(BF16), right, preferred_element_type=F32
            )

        total = lax.fori_loop(
            0, blocks // 2, two_lags, jnp.zeros((blocks, LANES), F32), unroll=blocks // 2
        )
        flat[pl.ds(chan, blocks, stride=GROUP), :] = total
        return carry

    lax.fori_loop(0, GROUP, channel, 0, unroll=4)


def lagged_products(windows, padded, flat):
    count = len(padded)
    blocks = padded[0].shape[1] // 2

    def channel(chan, carry):
        def two_lags(pair, total):
            left, right = [], []
            for lag in (2 * pair, 2 * pair + 1):
                right += toeplitz_block(windows, chan, lag, True)
                left.append(
                    jnp.concatenate([pad[chan, pl.ds(lag + 1, blocks), :] for pad in padded], axis=0)
                )
            return total + jnp.dot(
                jnp.concatenate(left, axis=1).astype(BF16),
                jnp.concatenate(right, axis=0),
                preferred_element_type=F32,
            )

        total = lax.fori_loop(
            0, blocks // 2, two_lags, jnp.zeros((count * blocks, LANES), F32), unroll=blocks // 2
        )
        for i, work in enumerate(flat):
            work[pl.ds(chan, blocks, stride=GROUP), :] = total[i * blocks : (i + 1) * blocks]
        return carry

    lax.fori_loop(0, GROUP, channel, 0, unroll=4)


def to_pieces(block):
    return block.T.reshape(16, GROUP, LANES).astype(BF16)


def from_pieces(pieces):
    return pieces.astype(F32).reshape(LANES, LANES).T


def owner_taps(taps, stream):
    return [
        jnp.broadcast_to(taps[:, stream * TAPS + lag : stream * TAPS + lag + 1], (GROUP, LANES))
        for lag in range(TAPS)
    ]


def owner_short(raw, taps, target):
    lanes = lax.broadcasted_iota(jnp.int32, (GROUP, LANES), 1)

    def block(index, before):
        now = raw[index].astype(F32)
        total = taps[0] * now
        after = []
        for lag in range(1, TAPS):
            turned = pltpu.roll(now, lag, 1)
            total = total + taps[lag] * jnp.where(lanes >= lag, turned, before[lag - 1])
            after.append(turned)
        target[pl.ds(pl.multiple_of(index * GROUP, GROUP), GROUP), :] = total.astype(BF16).astype(F32)
        return tuple(after)

    zero = jnp.zeros((GROUP, LANES), F32)
    lax.fori_loop(0, raw.shape[0], block, (zero,) * (TAPS - 1), unroll=32)


def owner_back(raw, taps, grad_flat, partner_flat, target):
    lanes = lax.broadcasted_iota(jnp.int32, (GROUP, LANES), 1)
    blocks = raw.shape[0]

    def block(step, carry):
        after, sums = carry
        index = blocks - 1 - step
        grad = grad_flat[pl.ds(pl.multiple_of(step * GROUP, GROUP), GROUP), :].astype(BF16).astype(F32)
        rows = pl.ds(pl.multiple_of(index * GROUP, GROUP), GROUP)
        grad = (grad * partner_flat[rows, :]).astype(BF16).astype(F32)
        value = raw[index].astype(F32)
        total = taps[0] * grad
        new_sums = [sums[0] + value * grad]
        new_after = []
        for lag in range(1, TAPS):
            turned = pltpu.roll(grad, LANES - lag, 1)
            moved = jnp.where(lanes < LANES - lag, turned, after[lag - 1])
            total = total + taps[lag] * moved
            new_sums.append(sums[lag] + value * moved)
            new_after.append(turned)
        target[index] = total.astype(BF16)
        return tuple(new_after), tuple(new_sums)

    zero = jnp.zeros((GROUP, LANES), F32)
    _, sums = lax.fori_loop(
        0, blocks, block, ((zero,) * (TAPS - 1), (zero,) * TAPS), unroll=16
    )
    return sums


def block_kernel(
    features_hbm,
    taps_hbm,
    filter_hbm,
    gain_hbm,
    grad_hbm,
    normed_hbm,
    q_grad_hbm,
    taps_grad_hbm,
    gain_grad_hbm,
    lag_recv,
    k_back_recv,
    v_back_recv,
    normed_ref,
    q_grad_ref,
    taps_grad_ref,
    gain_grad_ref,
    features_ref,
    taps_ref,
    filter_ref,
    gain_ref,
    grad_ref,
    filt_send,
    filt_recv,
    k_send,
    k_recv,
    v_send,
    v_recv,
    conv_send,
    conv_recv,
    back_send,
    back_recv,
    lag_send,
    k_back_send,
    v_back_send,
    before_recv,
    after_send,
    after_recv,
    row_send,
    row_recv,
    part_send,
    part_recv,
    part_sum,
    first_all,
    owner_sum,
    owner_all,
    taps_turned,
    taps_recv,
    pad,
    q_short,
    conv,
    windows,
    k_short,
    v_short,
    flat_a,
    flat_b,
    pad_fwd,
    pad_filt,
    pad_prod,
    toeplitz,
    sems,
    load_sems,
    store_sems,
):
    me = lax.axis_index("ctx")
    rank = lax.axis_index("tp")
    across = (rank + 4) % 8
    width = filter_ref.shape[1]
    chunks = list(enumerate(lane_chunks(width)))
    blocks = filt_recv.shape[0]
    rows = blocks * GROUP
    channels = width * 8
    following = {"ctx": (me + 1) % 64}
    preceding = {"ctx": (me + 63) % 64}

    barrier = pltpu.get_barrier_semaphore()

    def greet(partner):
        pl.semaphore_signal(
            barrier, inc=1, device_id={"ctx": partner, "tp": across}, device_id_type=MESH
        )

    for device in (following, preceding):
        pl.semaphore_signal(barrier, inc=1, device_id=device, device_id_type=MESH)
    for step in range(1, 8):
        pl.semaphore_signal(
            barrier, inc=1, device_id={"tp": (rank + step) % 8}, device_id_type=MESH
        )
    each_partner(me, greet)
    loads = [
        pltpu.make_async_copy(source, target, load_sems.at[i])
        for i, (source, target) in enumerate(
            (
                (filter_hbm, filter_ref),
                (features_hbm, features_ref),
                (taps_hbm, taps_ref),
                (gain_hbm, gain_ref),
                (grad_hbm, grad_ref),
            )
        )
    ]
    for load in loads:
        load.start()
    for load in loads:
        load.wait()

    for index, lanes in chunks:
        spot = pl.ds(16 * index, 16)
        filt_send[spot] = to_pieces(filter_ref[:, lanes].astype(F32))
        k_send[spot] = to_pieces(features_ref[1, :, lanes].astype(F32))
        v_send[spot] = to_pieces(features_ref[2, :, lanes].astype(F32))
    filler = jnp.zeros((LANES - 3 * TAPS, LANES), F32)
    for index, lanes in chunks:
        stack = jnp.concatenate([taps_ref[i, :, lanes] for i in range(3)] + [filler], axis=0)
        taps_turned[pl.ds(LANES * index, LANES), :] = stack.T
    pl.semaphore_wait(barrier, 73)
    start_exchange(me, across, filt_send, filt_recv, sems.at[0])
    own_taps = taps_turned.at[pl.ds(pl.multiple_of(me * GROUP, GROUP), GROUP)]
    taps_copy = remote(own_taps, taps_recv, sems.at[11], {"tp": across})
    taps_copy.start()
    last = features_ref.at[0, pl.ds(LANES - 16, 16)]
    remote(last, before_recv, sems.at[2], following).start()
    start_exchange(me, across, k_send, k_recv, sems.at[1])
    start_exchange(me, across, v_send, v_recv, sems.at[13])

    remote(last, before_recv, sems.at[2], following).wait_recv()
    pad[pl.ds(0, 8), :] = jnp.where(me > 0, before_recv[...].astype(F32)[8:, :], 0.0)
    pad[pl.ds(8, LANES), :] = features_ref[0].astype(F32)
    for _, lanes in chunks:
        for top in (0, 64):
            running = jnp.zeros((64, LANES), F32)
            for lag in range(TAPS):
                running = running + taps_ref[0, lag : lag + 1, lanes] * pad[
                    pl.ds(8 - lag + top, 64), lanes
                ]
            q_short[pl.ds(top, 64), lanes] = running.astype(BF16).astype(F32)

    await_slots(filt_recv, sems.at[0, 1])
    fill_windows(windows, filt_recv)
    build_toeplitz(windows, toeplitz)
    flat_a[...] = filt_recv[...].astype(F32).reshape(rows, LANES)
    fill_padded(pad_filt, flat_a, True)
    taps_copy.wait_recv()
    turned = taps_recv[...]
    k_taps, v_taps = owner_taps(turned, 1), owner_taps(turned, 2)
    await_slots(k_recv, sems.at[1, 1])
    owner_short(k_recv, k_taps, k_short)
    await_slots(v_recv, sems.at[13, 1])
    owner_short(v_recv, v_taps, v_short)
    flat_b[...] = (k_short[...] * v_short[...]).astype(BF16).astype(F32)
    fill_padded(pad_fwd, flat_b, False)
    causal_products(toeplitz, pad_fwd, flat_a)
    conv_send[...] = flat_a[...].reshape(blocks, GROUP, LANES).astype(BF16)
    start_exchange(me, across, conv_send, conv_recv, sems.at[3])
    fill_padded(pad_prod, flat_b, True)
    await_slots(conv_recv, sems.at[3, 1])

    squares = jnp.zeros((LANES, LANES), F32)
    tilts = jnp.zeros((LANES, LANES), F32)
    for index, lanes in chunks:
        value = from_pieces(conv_recv[pl.ds(16 * index, 16)])
        conv[:, lanes] = value
        gated = q_short[:, lanes] * value
        squares = squares + gated * gated
        tilts = tilts + gain_ref[:, lanes] * grad_ref[:, lanes].astype(F32) * gated
    row_send[pl.ds(0, 1), :] = jnp.sum(squares.T, axis=0, keepdims=True)
    row_send[pl.ds(1, 1), :] = jnp.sum(tilts.T, axis=0, keepdims=True)
    for step in range(1, 8):
        remote(row_send, row_recv.at[rank], sems.at[4], {"tp": (rank + step) % 8}).start()
    row_recv[pl.ds(rank, 1)] = row_send[...][None]
    await_slots(row_recv.at[pl.ds(0, 7)], sems.at[4, 1])
    sums = jnp.sum(row_recv[...], axis=0)
    scale = lax.rsqrt(sums[0:1] / channels + norm_eps)
    bend = scale**3 * sums[1:2] / channels
    scale = jnp.broadcast_to(scale, (LANES, LANES)).T
    bend = jnp.broadcast_to(bend, (LANES, LANES)).T

    def gate(lanes):
        value, q_value = conv[:, lanes], q_short[:, lanes]
        gain = gain_ref[:, lanes]
        upstream = grad_ref[:, lanes].astype(F32)
        gated = q_value * value
        grad_gated = scale * (gain * upstream) - gated * bend
        return value, q_value, gain, upstream, gated, grad_gated

    for index, lanes in chunks:
        _, q_value, _, _, _, grad_gated = gate(lanes)
        back_send[pl.ds(16 * index, 16)] = to_pieces(grad_gated * q_value)
    start_exchange(me, across, back_send, back_recv, sems.at[5])

    for index, lanes in chunks:
        value, _, gain, upstream, gated, grad_gated = gate(lanes)
        normed_ref[:, lanes] = (gated * scale * gain).astype(BF16)
        part_send[7 * 4 + index] = jnp.sum(upstream * gated * scale, axis=0, keepdims=True)
        first = (grad_gated * value).astype(BF16)
        after_send[:, lanes] = first[:16]
        first = first.astype(F32)
        conv[:, lanes] = first
        for lag in range(TAPS):
            part_send[lag * 4 + index] = jnp.sum(
                first * pad[pl.ds(8 - lag, LANES), lanes], axis=0, keepdims=True
            )
    remote(after_send, after_recv, sems.at[6], preceding).start()
    store_normed = pltpu.make_async_copy(normed_ref, normed_hbm, store_sems.at[0])
    store_normed.start()

    def send_part(partner):
        place = (partner // 16) * 8 + partner % 8
        remote(
            part_send.at[place], part_recv.at[me], sems.at[7], {"ctx": partner, "tp": across}
        ).start()

    each_partner(me, send_part)

    await_slots(back_recv, sems.at[5, 1])
    fill_windows(windows, back_recv)
    lagged_products(windows, [pad_filt, pad_prod], [flat_a, flat_b])

    def place_filter(index, carry):
        step = pl.multiple_of((blocks - 1 - index) * GROUP, GROUP)
        lag_send[index] = flat_b[pl.ds(step, GROUP), :].astype(BF16)
        return carry

    lax.fori_loop(0, blocks, place_filter, 0, unroll=8)
    start_exchange(me, across, lag_send, lag_recv, sems.at[12])
    k_sums = owner_back(k_recv, k_taps, flat_a, v_short, k_back_send)
    start_exchange(me, across, k_back_send, k_back_recv, sems.at[9])
    v_sums = owner_back(v_recv, v_taps, flat_a, k_short, v_back_send)
    start_exchange(me, across, v_back_send, v_back_recv, sems.at[14])
    lane_ids = lax.broadcasted_iota(jnp.int32, (GROUP, LANES), 1)
    chan_ids = lax.broadcasted_iota(jnp.int32, (GROUP, LANES), 0)
    packed = jnp.zeros((GROUP, LANES), F32)
    for place, value in enumerate(k_sums + v_sums):
        total = jnp.sum(value, axis=1, keepdims=True)
        packed = packed + jnp.where(lane_ids == place * GROUP + chan_ids, total, 0.0)
    owner_sum[...] = jnp.sum(packed, axis=0, keepdims=True)
    start_gather(me, across, owner_sum, owner_all, sems.at[10])

    await_slots(part_recv, sems.at[7, 1])
    part_sum[...] = jnp.sum(part_recv[...], axis=0)
    mine = (me // 16) * 8 + me % 8

    def send_total(partner):
        remote(part_sum, first_all.at[mine], sems.at[8], {"ctx": partner, "tp": across}).start()

    each_of_half(me, send_total)

    remote(after_send, after_recv, sems.at[6], preceding).wait_recv()
    pad[pl.ds(0, LANES), :] = conv[...]
    pad[pl.ds(LANES, 8), :] = jnp.where(me < 63, after_recv[...].astype(F32)[:8, :], 0.0)
    for _, lanes in chunks:
        for top in (0, 64):
            total = jnp.zeros((64, LANES), F32)
            for lag in range(TAPS):
                total = total + taps_ref[0, lag : lag + 1, lanes] * pad[pl.ds(lag + top, 64), lanes]
            q_grad_ref[pl.ds(top, 64), lanes] = total.astype(BF16)

    await_slots(first_all, sems.at[8, 1])
    for index, lanes in chunks:
        for lag in range(TAPS):
            taps_grad_ref[0, lag : lag + 1, lanes] = first_all[lag * len(chunks) + index]
        gain_grad_ref[:, lanes] = first_all[TAPS * len(chunks) + index]
    await_slots(owner_all, sems.at[10, 1])
    lane_ids = lax.broadcasted_iota(jnp.int32, (16, LANES), 1)
    row_ids = lax.broadcasted_iota(jnp.int32, (16, LANES), 0)
    for index, lanes in chunks:
        owned = owner_all[pl.ds(16 * index, 16)].reshape(16, LANES)
        owned = pltpu.roll(owned, 0, 1, stride=GROUP, stride_axis=0)
        for place in range(2 * TAPS):
            turned = pltpu.roll(owned, (LANES - GROUP * place) % LANES, 1) if place else owned
            value = jnp.where(lane_ids // GROUP == row_ids, turned, 0.0)
            taps_grad_ref[1 + place // TAPS, pl.ds(place % TAPS, 1), lanes] = jnp.sum(
                value, axis=0, keepdims=True
            )
    stores = [
        pltpu.make_async_copy(q_grad_ref, q_grad_hbm, store_sems.at[1]),
        pltpu.make_async_copy(taps_grad_ref, taps_grad_hbm, store_sems.at[2]),
        pltpu.make_async_copy(gain_grad_ref, gain_grad_hbm, store_sems.at[3]),
    ]
    for store in stores:
        store.start()

    for ref, number in ((lag_recv, 12), (k_back_recv, 9), (v_back_recv, 14)):
        await_slots(ref, sems.at[number, 1])
    for ref, number in (
        (filt_recv, 0),
        (k_recv, 1),
        (v_recv, 13),
        (conv_recv, 3),
        (row_recv.at[pl.ds(0, 7)], 4),
        (back_recv, 5),
        (part_recv, 7),
        (first_all, 8),
        (k_back_recv, 9),
        (v_back_recv, 14),
        (lag_recv, 12),
        (owner_all, 10),
    ):
        await_slots(ref, sems.at[number, 0])
    taps_copy.wait_send()
    store_normed.wait()
    for store in stores:
        store.wait()
    remote(last, before_recv, sems.at[2], following).wait_send()
    remote(after_send, after_recv, sems.at[6], preceding).wait_send()


def closing_kernel(*refs):
    sources, targets, stages = refs[:7], refs[7:12], refs[12:19]
    filter_stage, stream_stage, load_sems, store_sems = refs[19:]
    normed, feature_grad, filter_grad, taps_grad, gain_grad = targets
    loads = [pltpu.make_async_copy(sources[i], stages[i], load_sems.at[i]) for i in range(7)]
    for load in loads:
        load.start()
    stores = []

    def store(source, target):
        copy = pltpu.make_async_copy(source, target, store_sems.at[len(stores)])
        copy.start()
        stores.append(copy)

    for i, target in enumerate((normed, feature_grad.at[0], taps_grad, gain_grad)):
        loads[i].wait()
        store(stages[i], target)
    turned = (
        (filter_stage, filter_grad),
        (stream_stage.at[0], feature_grad.at[1]),
        (stream_stage.at[1], feature_grad.at[2]),
    )
    for i, (stage, target) in enumerate(turned, 4):
        loads[i].wait()
        for index, lanes in enumerate(lane_chunks(stage.shape[1])):
            stage[:, lanes] = from_pieces(stages[i][pl.ds(16 * index, 16)]).astype(BF16)
        store(stage, target)
    for copy in stores:
        copy.wait()


def per_device(features, short_taps, long_filter, gain, out_grad):
    seq_rows, width = long_filter.shape
    blocks = lax.axis_size("ctx")
    pieces = (blocks, GROUP, LANES)
    flat = (blocks * GROUP, LANES)
    padded = (GROUP, 2 * blocks, LANES)
    row = (1, LANES)
    plane = jax.ShapeDtypeStruct((seq_rows, width), BF16)
    taps = jax.ShapeDtypeStruct((3, TAPS, width), F32)
    gains = jax.ShapeDtypeStruct((1, width), F32)
    arrivals = [jax.ShapeDtypeStruct(pieces, BF16)] * 3
    outs = [plane, plane, taps, gains] + arrivals
    results = pl.pallas_call(
        block_kernel,
        out_shape=outs,
        in_specs=[HBM] * 5,
        out_specs=[HBM] * 7,
        scratch_shapes=[pltpu.VMEM(out.shape, out.dtype) for out in outs[:4]]
        + [
            pltpu.VMEM((3, seq_rows, width), BF16),
            pltpu.VMEM(short_taps.shape, F32),
            pltpu.VMEM((seq_rows, width), BF16),
            pltpu.VMEM((1, width), F32),
            pltpu.VMEM((seq_rows, width), BF16),
        ]
        + [pltpu.VMEM(pieces, BF16)] * 13
        + [pltpu.VMEM((16, width), BF16)] * 3
        + [
            pltpu.VMEM((2, LANES), F32),
            pltpu.VMEM((8, 2, LANES), F32),
            pltpu.VMEM((blocks // 2,) + row, F32),
            pltpu.VMEM((blocks,) + row, F32),
            pltpu.VMEM(row, F32),
            pltpu.VMEM((blocks // 2,) + row, F32),
            pltpu.VMEM(row, F32),
            pltpu.VMEM((blocks,) + row, F32),
            pltpu.VMEM((width, LANES), F32),
            pltpu.VMEM((GROUP, LANES), F32),
            pltpu.VMEM((seq_rows + 8, width), F32),
            pltpu.VMEM((seq_rows, width), F32),
            pltpu.VMEM((seq_rows, width), F32),
            pltpu.VMEM(((blocks + 2) * GROUP, LANES), F32),
        ]
        + [pltpu.VMEM(flat, F32)] * 4
        + [pltpu.VMEM(padded, F32)] * 3
        + [pltpu.VMEM((GROUP, blocks * LANES, LANES), BF16)]
        + [pltpu.SemaphoreType.DMA((15, 2)), pltpu.SemaphoreType.DMA((5,)), pltpu.SemaphoreType.DMA((4,))],
        compiler_params=pltpu.CompilerParams(
            collective_id=0, has_side_effects=True, vmem_limit_bytes=60 << 20
        ),
    )(features, short_taps, long_filter, gain[None, :], out_grad)
    normed, feature_grad, filter_grad, taps_grad, gain_grad = pl.pallas_call(
        closing_kernel,
        out_shape=[plane, jax.ShapeDtypeStruct(features.shape, BF16), plane, taps, gains],
        in_specs=[HBM] * 7,
        out_specs=[HBM] * 5,
        scratch_shapes=[pltpu.VMEM(out.shape, out.dtype) for out in outs]
        + [pltpu.VMEM((seq_rows, width), BF16), pltpu.VMEM((2, seq_rows, width), BF16)]
        + [pltpu.SemaphoreType.DMA((7,))] * 2,
        compiler_params=pltpu.CompilerParams(vmem_limit_bytes=60 << 20),
    )(*results)
    return (normed, feature_grad, filter_grad, taps_grad, gain_grad[0])


def solution(mesh):
    return jax.shard_map(
        per_device,
        mesh=mesh,
        in_specs=(
            P(None, "ctx", "tp"),
            P(None, None, "tp"),
            P("ctx", "tp"),
            P("tp"),
            P("ctx", "tp"),
        ),
        out_specs=(
            P("ctx", "tp"),
            P(None, "ctx", "tp"),
            P("ctx", "tp"),
            P(None, None, "tp"),
            P("tp"),
        ),
        check_vma=False,
    )
```

```python
import functools

import jax
import jax.numpy as jnp
from jax import lax
from jax.experimental import pallas as pl
from jax.experimental.pallas import tpu as pltpu
from jax.sharding import PartitionSpec as P

F32 = jnp.float32
BF16 = jnp.bfloat16
MESH = pl.DeviceIdType.MESH
norm_eps = 1e-06

TAPS = 7
LANES = 128
GROUP = 8
HBM = pl.BlockSpec(memory_space=pltpu.HBM)


def lane_chunks(width):
    return [slice(start, start + LANES) for start in range(0, width, LANES)]


def each_partner(me, visit):
    def one(step, carry):
        visit((me + step) % 64)
        return carry

    lax.fori_loop(0, 64, one, 0, unroll=4)


def each_of_half(me, visit):
    row, half, col = me // 16, (me // 8) % 2, me % 8

    def one(step, carry):
        visit(((row + step // 8) % 4) * 16 + half * 8 + (col + step % 8) % 8)
        return carry

    lax.fori_loop(0, 32, one, 0)


def remote(source, target, sems, device):
    return pltpu.make_async_remote_copy(
        src_ref=source,
        dst_ref=target,
        send_sem=sems.at[0],
        recv_sem=sems.at[1],
        device_id=device,
        device_id_type=MESH,
    )


def start_exchange(me, across, source, target, sems):
    def visit(partner):
        remote(source.at[partner], target.at[me], sems, {"ctx": partner, "tp": across}).start()

    each_partner(me, visit)


def start_gather(me, across, piece, target, sems):
    def visit(partner):
        remote(piece, target.at[me], sems, {"ctx": partner, "tp": across}).start()

    each_partner(me, visit)


def await_slots(ref, sem):
    pltpu.make_async_copy(ref, ref, sem).wait()


def toeplitz_rows(current, other, first, backward):
    rows = lax.broadcasted_iota(jnp.int32, (16, LANES), 0) + first
    lanes = lax.broadcasted_iota(jnp.int32, (16, LANES), 1)
    current = jnp.broadcast_to(current, (16, LANES))
    other = jnp.broadcast_to(other, (16, LANES))
    if backward:
        mixed = jnp.where(lanes >= LANES - 1 - rows, current, other)
        return pltpu.roll(mixed, first + 1, 1, stride=1, stride_axis=0)
    mixed = jnp.where(lanes < LANES - rows, current, other)
    return pltpu.roll(mixed, first, 1, stride=1, stride_axis=0)


def fill_padded(pad, work, mirrored):
    blocks = pad.shape[1] // 2
    if mirrored:
        spots = lax.broadcasted_iota(jnp.int32, (LANES, LANES), 0) + lax.broadcasted_iota(
            jnp.int32, (LANES, LANES), 1
        )
        mirror = jnp.where(spots == LANES - 1, 1.0, 0.0).astype(BF16)
    for chan in range(GROUP):
        rows = work[pl.ds(chan, blocks, stride=GROUP), :]
        if mirrored:
            rows = jnp.dot(rows.astype(BF16), mirror, preferred_element_type=F32)
        pad[chan, pl.ds(0, blocks), :] = jnp.zeros((blocks, LANES), F32)
        pad[chan, pl.ds(blocks, blocks), :] = rows


def fill_windows(windows, pieces):
    blocks = pieces.shape[0]
    rows = blocks * GROUP
    edge = jnp.zeros((GROUP, LANES), F32)
    windows[pl.ds(0, GROUP), :] = edge
    windows[pl.ds(rows + GROUP, GROUP), :] = edge
    windows[pl.ds(GROUP, rows), :] = pieces[...].astype(F32).reshape(rows, LANES)


def toeplitz_block(windows, chan, lag, backward):
    base = pl.multiple_of((lag + 1) * GROUP, GROUP) + chan
    current = windows[pl.ds(base, 1), :]
    other = windows[pl.ds(base + (GROUP if backward else -GROUP), 1), :]
    return [
        toeplitz_rows(current, other, first, backward).astype(BF16) for first in range(0, LANES, 16)
    ]


def build_toeplitz(windows, toeplitz):
    blocks = toeplitz.shape[1] // LANES

    def channel(chan, carry):
        def lags(lag, inner):
            rows = toeplitz_block(windows, chan, lag, False)
            for i, part in enumerate(rows):
                toeplitz[chan, pl.ds(pl.multiple_of(lag * LANES, LANES) + 16 * i, 16), :] = part
            return inner

        return lax.fori_loop(0, blocks, lags, carry, unroll=blocks)

    lax.fori_loop(0, GROUP, channel, 0)


def causal_products(toeplitz, padded, flat):
    blocks = padded.shape[1] // 2

    def channel(chan, carry):
        def two_lags(pair, total):
            left = [padded[chan, pl.ds(blocks - 2 * pair - i, blocks), :] for i in range(2)]
            right = toeplitz[chan, pl.ds(pl.multiple_of(pair * 2 * LANES, 2 * LANES), 2 * LANES), :]
            return total + jnp.dot(
                jnp.concatenate(left, axis=1).astype(BF16), right, preferred_element_type=F32
            )

        total = lax.fori_loop(
            0, blocks // 2, two_lags, jnp.zeros((blocks, LANES), F32), unroll=blocks // 2
        )
        flat[pl.ds(chan, blocks, stride=GROUP), :] = total
        return carry

    lax.fori_loop(0, GROUP, channel, 0, unroll=4)


def lagged_products(windows, padded, flat):
    count = len(padded)
    blocks = padded[0].shape[1] // 2

    def channel(chan, carry):
        def two_lags(pair, total):
            left, right = [], []
            for lag in (2 * pair, 2 * pair + 1):
                right += toeplitz_block(windows, chan, lag, True)
                left.append(
                    jnp.concatenate([pad[chan, pl.ds(lag + 1, blocks), :] for pad in padded], axis=0)
                )
            return total + jnp.dot(
                jnp.concatenate(left, axis=1).astype(BF16),
                jnp.concatenate(right, axis=0),
                preferred_element_type=F32,
            )

        total = lax.fori_loop(
            0, blocks // 2, two_lags, jnp.zeros((count * blocks, LANES), F32), unroll=blocks // 2
        )
        for i, work in enumerate(flat):
            work[pl.ds(chan, blocks, stride=GROUP), :] = total[i * blocks : (i + 1) * blocks]
        return carry

    lax.fori_loop(0, GROUP, channel, 0, unroll=4)


def to_pieces(block):
    return block.T.reshape(16, GROUP, LANES).astype(BF16)


def from_pieces(pieces):
    return pieces.astype(F32).reshape(LANES, LANES).T


def owner_taps(taps, stream):
    return [
        jnp.broadcast_to(taps[:, stream * TAPS + lag : stream * TAPS + lag + 1], (GROUP, LANES))
        for lag in range(TAPS)
    ]


def owner_short(raw, taps, target):
    lanes = lax.broadcasted_iota(jnp.int32, (GROUP, LANES), 1)

    def block(index, before):
        now = raw[index].astype(F32)
        total = taps[0] * now
        after = []
        for lag in range(1, TAPS):
            turned = pltpu.roll(now, lag, 1)
            total = total + taps[lag] * jnp.where(lanes >= lag, turned, before[lag - 1])
            after.append(turned)
        target[pl.ds(pl.multiple_of(index * GROUP, GROUP), GROUP), :] = total.astype(BF16).astype(F32)
        return tuple(after)

    zero = jnp.zeros((GROUP, LANES), F32)
    lax.fori_loop(0, raw.shape[0], block, (zero,) * (TAPS - 1), unroll=32)


def owner_back(raw, taps, grad_flat, partner_flat, target):
    lanes = lax.broadcasted_iota(jnp.int32, (GROUP, LANES), 1)
    blocks = raw.shape[0]

    def block(step, carry):
        after, sums = carry
        index = blocks - 1 - step
        grad = grad_flat[pl.ds(pl.multiple_of(step * GROUP, GROUP), GROUP), :].astype(BF16).astype(F32)
        rows = pl.ds(pl.multiple_of(index * GROUP, GROUP), GROUP)
        grad = (grad * partner_flat[rows, :]).astype(BF16).astype(F32)
        value = raw[index].astype(F32)
        total = taps[0] * grad
        new_sums = [sums[0] + value * grad]
        new_after = []
        for lag in range(1, TAPS):
            turned = pltpu.roll(grad, LANES - lag, 1)
            moved = jnp.where(lanes < LANES - lag, turned, after[lag - 1])
            total = total + taps[lag] * moved
            new_sums.append(sums[lag] + value * moved)
            new_after.append(turned)
        target[index] = total.astype(BF16)
        return tuple(new_after), tuple(new_sums)

    zero = jnp.zeros((GROUP, LANES), F32)
    _, sums = lax.fori_loop(
        0, blocks, block, ((zero,) * (TAPS - 1), (zero,) * TAPS), unroll=16
    )
    return sums


def block_kernel(
    features_hbm,
    taps_hbm,
    filter_hbm,
    gain_hbm,
    grad_hbm,
    normed_hbm,
    q_grad_hbm,
    taps_grad_hbm,
    gain_grad_hbm,
    lag_recv,
    k_back_recv,
    v_back_recv,
    normed_ref,
    q_grad_ref,
    taps_grad_ref,
    gain_grad_ref,
    features_ref,
    taps_ref,
    filter_ref,
    gain_ref,
    grad_ref,
    filt_send,
    filt_recv,
    k_send,
    k_recv,
    v_send,
    v_recv,
    conv_send,
    conv_recv,
    back_send,
    back_recv,
    lag_send,
    k_back_send,
    v_back_send,
    before_recv,
    after_send,
    after_recv,
    row_send,
    row_recv,
    part_send,
    part_recv,
    part_sum,
    first_all,
    owner_sum,
    owner_all,
    taps_turned,
    taps_recv,
    pad,
    q_short,
    conv,
    windows,
    k_short,
    v_short,
    flat_a,
    flat_b,
    pad_fwd,
    pad_filt,
    pad_prod,
    toeplitz,
    sems,
    load_sems,
    store_sems,
):
    me = lax.axis_index("ctx")
    rank = lax.axis_index("tp")
    across = (rank + 4) % 8
    width = filter_ref.shape[1]
    chunks = list(enumerate(lane_chunks(width)))
    blocks = filt_recv.shape[0]
    rows = blocks * GROUP
    channels = width * 8
    following = {"ctx": (me + 1) % 64}
    preceding = {"ctx": (me + 63) % 64}

    barrier = pltpu.get_barrier_semaphore()

    def greet(partner):
        pl.semaphore_signal(
            barrier, inc=1, device_id={"ctx": partner, "tp": across}, device_id_type=MESH
        )

    for device in (following, preceding):
        pl.semaphore_signal(barrier, inc=1, device_id=device, device_id_type=MESH)
    for step in range(1, 8):
        pl.semaphore_signal(
            barrier, inc=1, device_id={"tp": (rank + step) % 8}, device_id_type=MESH
        )
    each_partner(me, greet)
    loads = [
        pltpu.make_async_copy(source, target, load_sems.at[i])
        for i, (source, target) in enumerate(
            (
                (filter_hbm, filter_ref),
                (features_hbm, features_ref),
                (taps_hbm, taps_ref),
                (gain_hbm, gain_ref),
                (grad_hbm, grad_ref),
            )
        )
    ]
    for load in loads:
        load.start()
    for load in loads:
        load.wait()

    for index, lanes in chunks:
        spot = pl.ds(16 * index, 16)
        filt_send[spot] = to_pieces(filter_ref[:, lanes].astype(F32))
        k_send[spot] = to_pieces(features_ref[1, :, lanes].astype(F32))
        v_send[spot] = to_pieces(features_ref[2, :, lanes].astype(F32))
    filler = jnp.zeros((LANES - 3 * TAPS, LANES), F32)
    for index, lanes in chunks:
        stack = jnp.concatenate([taps_ref[i, :, lanes] for i in range(3)] + [filler], axis=0)
        taps_turned[pl.ds(LANES * index, LANES), :] = stack.T
    pl.semaphore_wait(barrier, 73)
    start_exchange(me, across, filt_send, filt_recv, sems.at[0])
    own_taps = taps_turned.at[pl.ds(pl.multiple_of(me * GROUP, GROUP), GROUP)]
    taps_copy = remote(own_taps, taps_recv, sems.at[11], {"tp": across})
    taps_copy.start()
    last = features_ref.at[0, pl.ds(LANES - 16, 16)]
    remote(last, before_recv, sems.at[2], following).start()
    start_exchange(me, across, k_send, k_recv, sems.at[1])
    start_exchange(me, across, v_send, v_recv, sems.at[13])

    remote(last, before_recv, sems.at[2], following).wait_recv()
    pad[pl.ds(0, 8), :] = jnp.where(me > 0, before_recv[...].astype(F32)[8:, :], 0.0)
    pad[pl.ds(8, LANES), :] = features_ref[0].astype(F32)
    for _, lanes in chunks:
        for top in (0, 64):
            running = jnp.zeros((64, LANES), F32)
            for lag in range(TAPS):
                running = running + taps_ref[0, lag : lag + 1, lanes] * pad[
                    pl.ds(8 - lag + top, 64), lanes
                ]
            q_short[pl.ds(top, 64), lanes] = running.astype(BF16).astype(F32)

    await_slots(filt_recv, sems.at[0, 1])
    fill_windows(windows, filt_recv)
    build_toeplitz(windows, toeplitz)
    flat_a[...] = filt_recv[...].astype(F32).reshape(rows, LANES)
    fill_padded(pad_filt, flat_a, True)
    taps_copy.wait_recv()
    turned = taps_recv[...]
    k_taps, v_taps = owner_taps(turned, 1), owner_taps(turned, 2)
    await_slots(k_recv, sems.at[1, 1])
    owner_short(k_recv, k_taps, k_short)
    await_slots(v_recv, sems.at[13, 1])
    owner_short(v_recv, v_taps, v_short)
    flat_b[...] = (k_short[...] * v_short[...]).astype(BF16).astype(F32)
    fill_padded(pad_fwd, flat_b, False)
    causal_products(toeplitz, pad_fwd, flat_a)
    conv_send[...] = flat_a[...].reshape(blocks, GROUP, LANES).astype(BF16)
    start_exchange(me, across, conv_send, conv_recv, sems.at[3])
    fill_padded(pad_prod, flat_b, True)
    await_slots(conv_recv, sems.at[3, 1])

    squares = jnp.zeros((LANES, LANES), F32)
    tilts = jnp.zeros((LANES, LANES), F32)
    for index, lanes in chunks:
        value = from_pieces(conv_recv[pl.ds(16 * index, 16)])
        conv[:, lanes] = value
        gated = q_short[:, lanes] * value
        squares = squares + gated * gated
        tilts = tilts + gain_ref[:, lanes] * grad_ref[:, lanes].astype(F32) * gated
    row_send[pl.ds(0, 1), :] = jnp.sum(squares.T, axis=0, keepdims=True)
    row_send[pl.ds(1, 1), :] = jnp.sum(tilts.T, axis=0, keepdims=True)
    for step in range(1, 8):
        remote(row_send, row_recv.at[rank], sems.at[4], {"tp": (rank + step) % 8}).start()
    row_recv[pl.ds(rank, 1)] = row_send[...][None]
    await_slots(row_recv.at[pl.ds(0, 7)], sems.at[4, 1])
    sums = jnp.sum(row_recv[...], axis=0)
    scale = lax.rsqrt(sums[0:1] / channels + norm_eps)
    bend = scale**3 * sums[1:2] / channels
    scale = jnp.broadcast_to(scale, (LANES, LANES)).T
    bend = jnp.broadcast_to(bend, (LANES, LANES)).T

    def gate(lanes):
        value, q_value = conv[:, lanes], q_short[:, lanes]
        gain = gain_ref[:, lanes]
        upstream = grad_ref[:, lanes].astype(F32)
        gated = q_value * value
        grad_gated = scale * (gain * upstream) - gated * bend
        return value, q_value, gain, upstream, gated, grad_gated

    for index, lanes in chunks:
        _, q_value, _, _, _, grad_gated = gate(lanes)
        back_send[pl.ds(16 * index, 16)] = to_pieces(grad_gated * q_value)
    start_exchange(me, across, back_send, back_recv, sems.at[5])

    for index, lanes in chunks:
        value, _, gain, upstream, gated, grad_gated = gate(lanes)
        normed_ref[:, lanes] = (gated * scale * gain).astype(BF16)
        part_send[7 * 4 + index] = jnp.sum(upstream * gated * scale, axis=0, keepdims=True)
        first = (grad_gated * value).astype(BF16)
        after_send[:, lanes] = first[:16]
        first = first.astype(F32)
        conv[:, lanes] = first
        for lag in range(TAPS):
            part_send[lag * 4 + index] = jnp.sum(
                first * pad[pl.ds(8 - lag, LANES), lanes], axis=0, keepdims=True
            )
    remote(after_send, after_recv, sems.at[6], preceding).start()
    store_normed = pltpu.make_async_copy(normed_ref, normed_hbm, store_sems.at[0])
    store_normed.start()

    def send_part(partner):
        place = (partner // 16) * 8 + partner % 8
        remote(
            part_send.at[place], part_recv.at[me], sems.at[7], {"ctx": partner, "tp": across}
        ).start()

    each_partner(me, send_part)

    await_slots(back_recv, sems.at[5, 1])
    fill_windows(windows, back_recv)
    lagged_products(windows, [pad_filt, pad_prod], [flat_a, flat_b])

    def place_filter(index, carry):
        step = pl.multiple_of((blocks - 1 - index) * GROUP, GROUP)
        lag_send[index] = flat_b[pl.ds(step, GROUP), :].astype(BF16)
        return carry

    lax.fori_loop(0, blocks, place_filter, 0, unroll=8)
    start_exchange(me, across, lag_send, lag_recv, sems.at[12])
    k_sums = owner_back(k_recv, k_taps, flat_a, v_short, k_back_send)
    start_exchange(me, across, k_back_send, k_back_recv, sems.at[9])
    v_sums = owner_back(v_recv, v_taps, flat_a, k_short, v_back_send)
    start_exchange(me, across, v_back_send, v_back_recv, sems.at[14])
    lane_ids = lax.broadcasted_iota(jnp.int32, (GROUP, LANES), 1)
    chan_ids = lax.broadcasted_iota(jnp.int32, (GROUP, LANES), 0)
    packed = jnp.zeros((GROUP, LANES), F32)
    for place, value in enumerate(k_sums + v_sums):
        total = jnp.sum(value, axis=1, keepdims=True)
        packed = packed + jnp.where(lane_ids == place * GROUP + chan_ids, total, 0.0)
    owner_sum[...] = jnp.sum(packed, axis=0, keepdims=True)
    start_gather(me, across, owner_sum, owner_all, sems.at[10])

    await_slots(part_recv, sems.at[7, 1])
    part_sum[...] = jnp.sum(part_recv[...], axis=0)
    mine = (me // 16) * 8 + me % 8

    def send_total(partner):
        remote(part_sum, first_all.at[mine], sems.at[8], {"ctx": partner, "tp": across}).start()

    each_of_half(me, send_total)

    remote(after_send, after_recv, sems.at[6], preceding).wait_recv()
    pad[pl.ds(0, LANES), :] = conv[...]
    pad[pl.ds(LANES, 8), :] = jnp.where(me < 63, after_recv[...].astype(F32)[:8, :], 0.0)
    for _, lanes in chunks:
        for top in (0, 64):
            total = jnp.zeros((64, LANES), F32)
            for lag in range(TAPS):
                total = total + taps_ref[0, lag : lag + 1, lanes] * pad[pl.ds(lag + top, 64), lanes]
            q_grad_ref[pl.ds(top, 64), lanes] = total.astype(BF16)

    await_slots(first_all, sems.at[8, 1])
    for index, lanes in chunks:
        for lag in range(TAPS):
            taps_grad_ref[0, lag : lag + 1, lanes] = first_all[lag * len(chunks) + index]
        gain_grad_ref[:, lanes] = first_all[TAPS * len(chunks) + index]
    await_slots(owner_all, sems.at[10, 1])
    lane_ids = lax.broadcasted_iota(jnp.int32, (16, LANES), 1)
    row_ids = lax.broadcasted_iota(jnp.int32, (16, LANES), 0)
    for index, lanes in chunks:
        owned = owner_all[pl.ds(16 * index, 16)].reshape(16, LANES)
        owned = pltpu.roll(owned, 0, 1, stride=GROUP, stride_axis=0)
        for place in range(2 * TAPS):
            turned = pltpu.roll(owned, (LANES - GROUP * place) % LANES, 1) if place else owned
            value = jnp.where(lane_ids // GROUP == row_ids, turned, 0.0)
            taps_grad_ref[1 + place // TAPS, pl.ds(place % TAPS, 1), lanes] = jnp.sum(
                value, axis=0, keepdims=True
            )
    stores = [
        pltpu.make_async_copy(q_grad_ref, q_grad_hbm, store_sems.at[1]),
        pltpu.make_async_copy(taps_grad_ref, taps_grad_hbm, store_sems.at[2]),
        pltpu.make_async_copy(gain_grad_ref, gain_grad_hbm, store_sems.at[3]),
    ]
    for store in stores:
        store.start()

    for ref, number in ((lag_recv, 12), (k_back_recv, 9), (v_back_recv, 14)):
        await_slots(ref, sems.at[number, 1])
    for ref, number in (
        (filt_recv, 0),
        (k_recv, 1),
        (v_recv, 13),
        (conv_recv, 3),
        (row_recv.at[pl.ds(0, 7)], 4),
        (back_recv, 5),
        (part_recv, 7),
        (first_all, 8),
        (k_back_recv, 9),
        (v_back_recv, 14),
        (lag_recv, 12),
        (owner_all, 10),
    ):
        await_slots(ref, sems.at[number, 0])
    taps_copy.wait_send()
    store_normed.wait()
    for store in stores:
        store.wait()
    remote(last, before_recv, sems.at[2], following).wait_send()
    remote(after_send, after_recv, sems.at[6], preceding).wait_send()


def closing_kernel(*refs):
    sources, targets, stages = refs[:7], refs[7:12], refs[12:19]
    filter_stage, stream_stage, load_sems, store_sems = refs[19:]
    normed, feature_grad, filter_grad, taps_grad, gain_grad = targets
    loads = [pltpu.make_async_copy(sources[i], stages[i], load_sems.at[i]) for i in range(7)]
    for load in loads:
        load.start()
    stores = []

    def store(source, target):
        copy = pltpu.make_async_copy(source, target, store_sems.at[len(stores)])
        copy.start()
        stores.append(copy)

    for i, target in enumerate((normed, feature_grad.at[0], taps_grad, gain_grad)):
        loads[i].wait()
        store(stages[i], target)
    turned = (
        (filter_stage, filter_grad),
        (stream_stage.at[0], feature_grad.at[1]),
        (stream_stage.at[1], feature_grad.at[2]),
    )
    for i, (stage, target) in enumerate(turned, 4):
        loads[i].wait()
        for index, lanes in enumerate(lane_chunks(stage.shape[1])):
            stage[:, lanes] = from_pieces(stages[i][pl.ds(16 * index, 16)]).astype(BF16)
        store(stage, target)
    for copy in stores:
        copy.wait()


def per_device(features, short_taps, long_filter, gain, out_grad):
    seq_rows, width = long_filter.shape
    blocks = lax.axis_size("ctx")
    pieces = (blocks, GROUP, LANES)
    flat = (blocks * GROUP, LANES)
    padded = (GROUP, 2 * blocks, LANES)
    row = (1, LANES)
    plane = jax.ShapeDtypeStruct((seq_rows, width), BF16)
    taps = jax.ShapeDtypeStruct((3, TAPS, width), F32)
    gains = jax.ShapeDtypeStruct((1, width), F32)
    arrivals = [jax.ShapeDtypeStruct(pieces, BF16)] * 3
    outs = [plane, plane, taps, gains] + arrivals
    results = pl.pallas_call(
        block_kernel,
        out_shape=outs,
        in_specs=[HBM] * 5,
        out_specs=[HBM] * 7,
        scratch_shapes=[pltpu.VMEM(out.shape, out.dtype) for out in outs[:4]]
        + [
            pltpu.VMEM((3, seq_rows, width), BF16),
            pltpu.VMEM(short_taps.shape, F32),
            pltpu.VMEM((seq_rows, width), BF16),
            pltpu.VMEM((1, width), F32),
            pltpu.VMEM((seq_rows, width), BF16),
        ]
        + [pltpu.VMEM(pieces, BF16)] * 13
        + [pltpu.VMEM((16, width), BF16)] * 3
        + [
            pltpu.VMEM((2, LANES), F32),
            pltpu.VMEM((8, 2, LANES), F32),
            pltpu.VMEM((blocks // 2,) + row, F32),
            pltpu.VMEM((blocks,) + row, F32),
            pltpu.VMEM(row, F32),
            pltpu.VMEM((blocks // 2,) + row, F32),
            pltpu.VMEM(row, F32),
            pltpu.VMEM((blocks,) + row, F32),
            pltpu.VMEM((width, LANES), F32),
            pltpu.VMEM((GROUP, LANES), F32),
            pltpu.VMEM((seq_rows + 8, width), F32),
            pltpu.VMEM((seq_rows, width), F32),
            pltpu.VMEM((seq_rows, width), F32),
            pltpu.VMEM(((blocks + 2) * GROUP, LANES), F32),
        ]
        + [pltpu.VMEM(flat, F32)] * 4
        + [pltpu.VMEM(padded, F32)] * 3
        + [pltpu.VMEM((GROUP, blocks * LANES, LANES), BF16)]
        + [pltpu.SemaphoreType.DMA((15, 2)), pltpu.SemaphoreType.DMA((5,)), pltpu.SemaphoreType.DMA((4,))],
        compiler_params=pltpu.CompilerParams(
            collective_id=0, has_side_effects=True, vmem_limit_bytes=60 << 20
        ),
    )(features, short_taps, long_filter, gain[None, :], out_grad)
    normed, feature_grad, filter_grad, taps_grad, gain_grad = pl.pallas_call(
        closing_kernel,
        out_shape=[plane, jax.ShapeDtypeStruct(features.shape, BF16), plane, taps, gains],
        in_specs=[HBM] * 7,
        out_specs=[HBM] * 5,
        scratch_shapes=[pltpu.VMEM(out.shape, out.dtype) for out in outs]
        + [pltpu.VMEM((seq_rows, width), BF16), pltpu.VMEM((2, seq_rows, width), BF16)]
        + [pltpu.SemaphoreType.DMA((7,))] * 2,
        compiler_params=pltpu.CompilerParams(vmem_limit_bytes=60 << 20),
    )(*results)
    return (normed, feature_grad, filter_grad, taps_grad, gain_grad[0])


def solution(mesh):
    return jax.shard_map(
        per_device,
        mesh=mesh,
        in_specs=(
            P(None, "ctx", "tp"),
            P(None, None, "tp"),
            P("ctx", "tp"),
            P("tp"),
            P("ctx", "tp"),
        ),
        out_specs=(
            P("ctx", "tp"),
            P(None, "ctx", "tp"),
            P("ctx", "tp"),
            P(None, None, "tp"),
            P("tp"),
        ),
        check_vma=False,
    )
```
